32 devices in a mesh: leaf: 8 (over z, y), rhs: 4 (over x, core).
Axes of the slice: x: 2, y: 2, z: 4, core: 2. Of those that a mesh axis runs over, the one named last changes fastest.
Arguments:
- rhs_block: float32 [4096, 1024], P('leaf', 'rhs'), may hold values from -6 to 6
- leaf_order: int32 [8, 512], P('leaf'), may hold values from 0 to 511, as said below
- leaf_inverse: float32 [4096, 512], P('leaf'), may hold values from -0.04 to 3, as said below
- leaf_basis: float32 [4096, 128], P('leaf'), may hold values from -0.09678524 to 0.09678524
- transfer: bfloat16 [8, 2, 128, 128], P('leaf'), may hold values from -0.05 to 1.25, as said below
- precision: bfloat16 [8, 3, 128, 128], P('leaf'), may hold values from -0.09 to 8, as said below
Outputs:
- solution: float32 [4096, 1024], P('leaf', 'rhs')
The draws below stay inside these ranges and needn't reach their ends.
Inputs may be any that keep to these rules, and one draw needn't show every extreme that they name: `leaf_order`: each row is a permutation of 0 to 511. `leaf_inverse`: each leaf's block of 512 x 512 entries is symmetric positive definite. transfer[b, k] is the same for all leaves b of one aligned group of 2 ** (k + 1) leaves. Every block is symmetric positive definite; precision[b, k] is the same for all leaves b of one aligned group of 2 ** (k + 1) leaves.
All inputs are finite; a program needn't handle non-finite values.
Results may differ from the reference program's by a relative error of at most 0.0003.
Values sent between devices are 32-bit elements; how exact they have to be, the bound alone decides.
No kernel may reach another device: no remote copies, remote signals or barrier semaphores. Data moves between devices by JAX's collectives and lax.ppermute only.
A program may use at most 64 MiB of HBM per device.

```python
import jax
import jax.numpy as jnp
from jax import lax

R = 128
LEAF_PTS = 512
COLS_DEV = 256
LEVELS = 3
NPTS = 4096
N_LEAF = 8
N_RHS = 4


def symmetric_blocks(key, count, size, lowest, highest, spread):
    key_noise, key_diag = jax.random.split(key)
    noise_part = jax.random.uniform(key_noise, (count, size, size), jnp.float32, -spread, spread)
    upper_part = jnp.triu(noise_part, 1)
    symmetric = upper_part + jnp.swapaxes(upper_part, 1, 2)
    uniforms = jax.random.uniform(key_diag, (count, size), jnp.float32)
    diagonal = lowest * (highest / lowest) ** uniforms
    return symmetric + diagonal[:, :, None] * jnp.eye(size, dtype=jnp.float32)


def group_owners(depth):
    return jnp.right_shift(jnp.arange(N_LEAF, dtype=jnp.int32), depth + 1) * 2 ** (depth + 1)


def leaf_orders(key):
    keys = jax.random.split(jax.random.fold_in(key, 21), N_LEAF)
    return jax.vmap(lambda single: jax.random.permutation(single, LEAF_PTS))(keys).astype(jnp.int32)


def leaf_bases(key):
    key_common, key_own = jax.random.split(jax.random.fold_in(key, 22))
    limit = (3.0 / LEAF_PTS) ** 0.5
    shared = jax.random.uniform(key_common, (N_LEAF, LEAF_PTS, 1), jnp.float32, -1.2 * limit, 1.2 * limit)
    own = jax.random.uniform(key_own, (N_LEAF, LEAF_PTS, R), jnp.float32, -limit, limit)
    return 0.8 * shared + 0.3 * own


def draw_leaf_order(key, part):
    return leaf_orders(key)


def draw_leaf_basis(key, part):
    return leaf_bases(key).reshape(NPTS, R)


def draw_rhs_block(key, part):
    orders = leaf_orders(key)
    bases = leaf_bases(key)
    key_mix, key_noise = jax.random.split(jax.random.fold_in(key, 23))
    columns = COLS_DEV * N_RHS
    mixing_cols = jax.random.normal(key_mix, (R, columns), jnp.float32)
    mixing_cols = mixing_cols - jnp.mean(mixing_cols, axis=0, keepdims=True)
    common = 2.0 * (LEAF_PTS / R) ** 0.5 * jnp.einsum('npr,rc->npc', bases, mixing_cols, precision=lax.Precision.HIGHEST)
    noise = 0.8 * jax.random.normal(key_noise, (N_LEAF, LEAF_PTS, columns), jnp.float32)
    tree_rows = jnp.clip(noise + common, -6.0, 6.0)
    leaf_rows = jnp.arange(N_LEAF, dtype=jnp.int32)[:, None]
    placed = jnp.zeros_like(tree_rows).at[leaf_rows, orders].set(tree_rows)
    return placed.reshape(NPTS, columns)


def draw_leaf_inverse(key, part):
    blocks = symmetric_blocks(jax.random.fold_in(key, 11), N_LEAF, LEAF_PTS, 1.3, 3.0, 0.04)
    return blocks.reshape(NPTS, LEAF_PTS)


def draw_precision(key, part):
    stacked = []
    for depth in range(LEVELS):
        blocks = symmetric_blocks(jax.random.fold_in(key, 100 + depth), N_LEAF, R, 2.0, 8.0, 0.08)
        stacked.append(jnp.take(blocks, group_owners(depth), axis=0))
    return jnp.stack(stacked, axis=1).astype(jnp.bfloat16)


def draw_transfer(key, part):
    stacked = []
    for depth in range(LEVELS - 1):
        key_noise, key_diag = jax.random.split(jax.random.fold_in(key, 300 + depth))
        noise_part = jax.random.uniform(key_noise, (N_LEAF, R, R), jnp.float32, -0.04, 0.04)
        diagonal = jax.random.uniform(key_diag, (N_LEAF, R), jnp.float32, 0.8, 1.2)
        blocks = noise_part + diagonal[:, :, None] * jnp.eye(R, dtype=jnp.float32)
        stacked.append(jnp.take(blocks, group_owners(depth), axis=0))
    return jnp.stack(stacked, axis=1).astype(jnp.bfloat16)


def setup_inputs(seed: int = 0) -> dict:
    arg_keys = jax.random.split(jax.random.key(seed), 7)
    return {
        "rhs_block": draw_rhs_block(jax.random.fold_in(arg_keys[6], 71), 0),
        "leaf_order": draw_leaf_order(jax.random.fold_in(arg_keys[6], 71), 0),
        "leaf_inverse": draw_leaf_inverse(jax.random.fold_in(arg_keys[6], 71), 0),
        "leaf_basis": draw_leaf_basis(jax.random.fold_in(arg_keys[6], 71), 0),
        "transfer": draw_transfer(jax.random.fold_in(arg_keys[6], 71), 0),
        "precision": draw_precision(jax.random.fold_in(arg_keys[6], 71), 0),
    }


def batched(left_op, right_op):
    return jnp.einsum('nij,njk->nik', left_op, right_op, precision=lax.Precision.HIGHEST)

def flipped(matrix):
    return jnp.swapaxes(matrix, 1, 2)

def cholesky_solve(matrix, right_side):
    factor = jnp.linalg.cholesky(matrix)
    middle = lax.linalg.triangular_solve(factor, right_side, left_side=True, lower=True)
    return lax.linalg.triangular_solve(factor, middle, left_side=True, lower=True, transpose_a=True)

def reference(rhs_block, leaf_order, leaf_inverse, leaf_basis, transfer, precision):
    leaves = N_LEAF
    points = LEAF_PTS
    columns = rhs_block.shape[1]
    ordered = rhs_block.reshape(leaves, points, columns)
    ordered = jnp.take_along_axis(ordered, leaf_order[:, :, None].astype(jnp.int32), axis=1)
    inverse = leaf_inverse.reshape(leaves, points, points)
    basis = leaf_basis.reshape(leaves, points, R)
    solved = batched(inverse, ordered)
    carried = batched(inverse, basis)
    projected = batched(flipped(basis), solved)
    gram_sum = batched(flipped(basis), carried)
    mixing = jnp.broadcast_to(jnp.eye(R, dtype=jnp.float32), (leaves, R, R))
    accumulated = jnp.zeros((leaves, R, columns), jnp.float32)
    for height in range(LEVELS):
        nodes_now = leaves >> height
        group_size = 2 ** (height + 1)
        summed = projected.reshape(nodes_now // 2, 2, R, columns).sum(axis=1)
        whole_gram = gram_sum.reshape(nodes_now // 2, 2, R, R).sum(axis=1)
        coupling = precision[::group_size, height].astype(jnp.float32)
        coeffs = cholesky_solve(coupling + whole_gram, jnp.concatenate([summed, coupling], axis=2))
        coef_rhs = coeffs[:, :, :columns]
        coef_basis = coeffs[:, :, columns:]
        accumulated = accumulated + batched(mixing, jnp.repeat(coef_rhs, group_size, axis=0))
        if height + 1 < LEVELS:
            mixer = transfer[::group_size, height].astype(jnp.float32)
            update = batched(coef_basis, mixer)
            mixing = batched(mixing, jnp.repeat(update, group_size, axis=0))
            projected = batched(flipped(mixer), batched(coupling, coef_rhs))
            left_part = batched(flipped(mixer), batched(flipped(coef_basis), whole_gram))
            gram_sum = batched(left_part, mixer)
    solved = solved - batched(carried, accumulated)
    rows = jnp.arange(leaves, dtype=jnp.int32)[:, None]
    placed = jnp.zeros_like(solved).at[rows, leaf_order.astype(jnp.int32)].set(solved)
    return placed.reshape(leaves * points, columns)
```

```python
import functools

import jax
import jax.numpy as jnp
from jax import lax
from jax.experimental import pallas as pl
from jax.experimental.pallas import tpu as pltpu
from jax.sharding import PartitionSpec as P

F32 = jnp.float32
BF16 = jnp.bfloat16
HIGH = lax.Precision.HIGH
FULL = lax.Precision.HIGHEST
SUB = 8
VMEM = pl.BlockSpec(memory_space=pltpu.VMEM)
PARAMS = pltpu.CompilerParams(vmem_limit_bytes=32 * 1024 * 1024)


def mm(a, b, precision=HIGH, dims=((1,), (0,))):
    return lax.dot_general(a, b, (dims, ((), ())), precision=precision, preferred_element_type=F32)


def split(x):
    top = x.astype(BF16)
    return top, (x - top.astype(F32)).astype(BF16)


def pick(mask, x):
    top, low = split(x)
    one = lambda part: lax.dot_general(mask, part, (((1,), (0,)), ((), ())), preferred_element_type=F32)
    return one(top) + one(low)


def reciprocal(x):
    r = pl.reciprocal(x, approx=True)
    r = r * (2.0 - x * r)
    return r * (2.0 - x * r)


def invert(matrix):
    size = matrix.shape[0]
    tiles = [matrix[i:i + SUB] for i in range(0, size, SUB)]
    lane = lax.broadcasted_iota(jnp.int32, (SUB, size), 1)
    row = lax.broadcasted_iota(jnp.int32, (SUB, size), 0)
    spread = lambda tile, k: jnp.broadcast_to(tile[:, k:k + 1], (SUB, size))
    for t in range(size // SUB):
        x = tiles[t]
        for j0 in range(0, SUB, 2):
            j1 = j0 + 1
            k0, k1 = t * SUB + j0, t * SUB + j1
            c0, c1 = spread(x, k0), spread(x, k1)
            a, b, c = c0[j0:j0 + 1], c1[j0:j0 + 1], c1[j1:j1 + 1]
            in_lanes = (lane == k0) | (lane == k1)
            in_rows = (row == j0) | (row == j1)
            first, second = lane[:1] == k0, lane[:1] == k1
            e0 = jnp.where(first, 1.0, jnp.where(second, 0.0, x[j0:j0 + 1]))
            e1 = jnp.where(second, 1.0, jnp.where(first, 0.0, x[j1:j1 + 1]))
            r = reciprocal(a * c - b * b)
            u0 = c * e0 - b * e1
            u1 = a * e1 - b * e0
            d0 = jnp.where(row == j0, -1.0, jnp.where(row == j1, 0.0, c0))
            d1 = jnp.where(row == j1, -1.0, jnp.where(row == j0, 0.0, c1))
            base = jnp.where(in_lanes | in_rows, 0.0, x)
            x = base - (d0 * u0 + d1 * u1) * r
        inside = (lane >= t * SUB) & (lane < (t + 1) * SUB)
        order = [i % len(tiles) for i in range(t + 1, t + len(tiles))]
        for i in order:
            old = tiles[i]
            new = jnp.where(inside, 0.0, old)
            for j in range(SUB):
                new = new - spread(old, t * SUB + j) * x[j:j + 1]
            tiles[i] = new
        tiles[t] = x
    return jnp.concatenate(tiles, axis=0)


def scaled_inverse(matrix):
    size = matrix.shape[0]
    rows = lax.broadcasted_iota(jnp.int32, (size, size), 0)
    cols = lax.broadcasted_iota(jnp.int32, (size, size), 1)
    diagonal = jnp.where(rows == cols, matrix, 0.0)
    down = lax.rsqrt(jnp.sum(diagonal, axis=1, keepdims=True))
    across = lax.rsqrt(jnp.sum(diagonal, axis=0, keepdims=True))
    return invert(matrix * down * across) * down * across


def basis_kernel(inverse, basis, carried, gram):
    q = mm(inverse[...], basis[...])
    carried[...] = q
    gram[...] = mm(basis[...], q, HIGH, ((0,), (0,)))


def leaf_kernel(order, rhs, inverse, basis, carried, solved, projected, carried_out):
    points = rhs.shape[0]
    wide = 128
    numbers = order[...].astype(F32)
    lanes = lax.broadcasted_iota(jnp.int32, (wide, points), 1).astype(F32)
    gather = []
    for i in range(0, points, wide):
        column = jnp.broadcast_to(numbers[:, i:i + wide], (wide, wide)).T
        column = jnp.concatenate([column] * (points // wide), axis=1)
        gather.append(jnp.where(column == lanes, 1.0, 0.0).astype(BF16))
    gather = jnp.concatenate(gather, axis=0)
    rows = lax.broadcasted_iota(jnp.int32, (points, points), 0).astype(F32)
    scatter = jnp.where(numbers == rows, 1.0, 0.0).astype(BF16)
    z = mm(inverse[...], pick(gather, rhs[...]))
    projected[...] = mm(basis[...], z, HIGH, ((0,), (0,)))
    solved[...] = pick(scatter, z)
    carried_out[...] = pick(scatter, carried[...])


def node_kernel(level, gram, other, precision, *rest):
    coupling = precision[0, level].astype(F32)
    whole = gram[...] + other[...]
    if len(rest) == 1:
        rest[0][...] = scaled_inverse(coupling + whole)
        return
    transfer, inverse, mover, gram_out = rest
    mixer = transfer[0, level].astype(F32)
    left = mm(mixer, coupling, FULL, ((0,), (0,)))
    right = mm(whole, mixer, FULL)
    m = scaled_inverse(coupling + whole)
    n = mm(left, m, FULL)
    inverse[...] = m
    mover[...] = n
    gram_out[...] = mm(n, right, FULL)


def lift_kernel(projected, other, inverse, mover, coeffs, projected_out):
    s = projected[...] + other[...]
    projected_out[...] = mm(mover[...], s)
    coeffs[...] = mm(inverse[...], s)


def fold_kernel(levels, *refs):
    solved, carried, solved_out, carried_out = refs[0], refs[1], refs[-2], refs[-1]
    coeffs, movers = refs[2:2 + levels], refs[2 + levels:2 + 2 * levels]
    z, q = solved[...], carried[...]
    for k in range(levels):
        z = z - mm(q, coeffs[k][...])
        q = mm(q, movers[k][...], HIGH, ((1,), (1,)))
    solved_out[...] = z
    carried_out[...] = q


def root_kernel(projected, other, inverse, solved, carried, out):
    s = projected[...] + other[...]
    out[...] = solved[...] - mm(carried[...], mm(inverse[...], s))


def call(kernel, outs, *args):
    return pl.pallas_call(
        kernel,
        out_shape=[jax.ShapeDtypeStruct(shape, F32) for shape in outs],
        in_specs=[VMEM] * len(args),
        out_specs=[VMEM] * len(outs),
        compiler_params=PARAMS,
    )(*args)


def from_partner(block, axis, apart):
    count = lax.axis_size(axis)
    return lax.ppermute(block, axis, [(i, i ^ 1 << apart) for i in range(count)])


def body(rhs, order, inverse, basis, transfer, precision):
    points, columns = rhs.shape
    rank = basis.shape[1]
    square, tall, block = (rank, rank), (points, rank), (rank, columns)
    levels = lax.axis_size("leaf").bit_length() - 1
    carried, gram = call(basis_kernel, [tall, square], inverse, basis)
    other_gram = from_partner(gram, "leaf", 0)
    solved, projected, carried = call(
        leaf_kernel, [(points, columns), block, tall], order, rhs, inverse, basis, carried
    )
    coeffs, movers = [], []
    for k in range(levels - 1):
        other = from_partner(projected, "leaf", k)
        m, n, gram = call(
            functools.partial(node_kernel, k), [square] * 3, gram, other_gram, precision, transfer
        )
        other_gram = from_partner(gram, "leaf", k + 1)
        alpha, projected = call(lift_kernel, [block, block], projected, other, m, n)
        coeffs.append(alpha)
        movers.append(n)
    k = levels - 1
    other = from_partner(projected, "leaf", k)
    solved, carried = call(
        functools.partial(fold_kernel, k), [(points, columns), tall], solved, carried, *coeffs, *movers
    )
    (m,) = call(functools.partial(node_kernel, k), [square], gram, other_gram, precision)
    (out,) = call(root_kernel, [(points, columns)], projected, other, m, solved, carried)
    return out


def solution(mesh):
    placed = (
        P("leaf", "rhs"),
        P("leaf", None),
        P("leaf", None),
        P("leaf", None),
        P("leaf", None, None, None),
        P("leaf", None, None, None),
    )
    return jax.shard_map(
        body, mesh=mesh, in_specs=placed, out_specs=P("leaf", "rhs"), check_vma=False
    )
```

```python
import functools

import jax
import jax.numpy as jnp
from jax import lax
from jax.experimental import pallas as pl
from jax.experimental.pallas import tpu as pltpu
from jax.sharding import PartitionSpec as P

F32 = jnp.float32
BF16 = jnp.bfloat16
HIGH = lax.Precision.HIGH
FULL = lax.Precision.HIGHEST
SUB = 8
GIGA = 10 ** 9
VMEM = pl.BlockSpec(memory_space=pltpu.VMEM)
PARAMS = pltpu.CompilerParams(vmem_limit_bytes=32 * 1024 * 1024)


def mm(a, b, precision=HIGH, dims=((1,), (0,))):
    return lax.dot_general(a, b, (dims, ((), ())), precision=precision, preferred_element_type=F32)


def split(x):
    top = x.astype(BF16)
    return top, (x - top.astype(F32)).astype(BF16)


def pick(mask, x):
    top, low = split(x)
    one = lambda part: lax.dot_general(mask, part, (((1,), (0,)), ((), ())), preferred_element_type=F32)
    return one(top) + one(low)


def reciprocal(x):
    return pltpu.reciprocal(x, approx=True)

def parts(x):
    top = x.astype(BF16).astype(F32)
    rest = x - top
    mid = rest.astype(BF16).astype(F32)
    return top, mid, rest - mid

def stack(rows):
    size = rows[0].shape[1]
    row = lax.broadcasted_iota(jnp.int32, (SUB, size), 0)
    while len(rows) > 1:
        half = len(rows) // 2
        step = SUB // len(rows)
        rows = [jnp.where(row // step % 2 == 0, rows[2*i], rows[2*i+1]) for i in range(half)]
    return rows[0]

def spread(x, k):
    return jnp.take_along_axis(x, jnp.full(x.shape, k, jnp.int32), axis=1, mode="promise_in_bounds")

def four(rows, at, k, lane):
    d = [[spread(x, k + j) for j in range(4)] for x in rows]
    inside = (lane >= k) & (lane < k + 4)
    e = [jnp.where(inside, jnp.where(lane == k + j, 1.0, 0.0), rows[at + j]) for j in range(4)]
    (a0, a1, _, _), (_, a2, _, _), (b00, b01, c0, c1), (b10, b11, _, c2) = d[at:at + 4]
    det = a0 * a2 - a1 * a1
    g00, g01 = b00 * a2 - b01 * a1, b01 * a0 - b00 * a1
    g10, g11 = b10 * a2 - b11 * a1, b11 * a0 - b10 * a1
    s0 = det * c0 - (g00 * b00 + g01 * b01)
    s1 = det * c1 - (g00 * b10 + g01 * b11)
    s2 = det * c2 - (g10 * b10 + g11 * b11)
    rs = reciprocal(s0 * s2 - s1 * s1)
    ra = reciprocal(det)
    t2 = det * e[2] - (g00 * e[0] + g01 * e[1])
    t3 = det * e[3] - (g10 * e[0] + g11 * e[1])
    w2 = (s2 * t2 - s1 * t3) * rs
    w3 = (s0 * t3 - s1 * t2) * rs
    w0 = ((a2 * e[0] - a1 * e[1]) - (g00 * w2 + g10 * w3)) * ra
    w1 = ((a0 * e[1] - a1 * e[0]) - (g01 * w2 + g11 * w3)) * ra
    w = [w0, w1, w2, w3]
    out = []
    for i, x in enumerate(rows):
        if at <= i < at + 4:
            out.append(w[i - at])
        else:
            base = jnp.where(inside, 0.0, x)
            out.append((base - (d[i][0] * w0 + d[i][1] * w1)) - (d[i][2] * w2 + d[i][3] * w3))
    return out

def invert(m):
    size = m.shape[0]
    lane = lax.broadcasted_iota(jnp.int32, (SUB, size), 1)
    row = lax.broadcasted_iota(jnp.int32, (SUB, size), 0)
    wide = lax.broadcasted_iota(jnp.int32, (size, size), 1)
    split_rows = lambda tile: [jnp.broadcast_to(tile[i:i+1], (SUB, size)) for i in range(SUB)]

    def trail(t, x6, w6):
        k = t * SUB
        u = lax.dot_general(x6.astype(BF16), w6.astype(BF16), (((0,), (0,)), ((), ())), preferred_element_type=F32)
        m[...] = jnp.where((wide >= k) & (wide < k + SUB), 0.0, m[...]) - u

    def step(t, carry):
        p, x6, w6 = carry
        k = pl.multiple_of(t * SUB, SUB)
        trail(t - 1, x6, w6)
        x = jnp.where(lane < k, -1.0, 1.0) * stack(p)
        x = jnp.where((lane >= k) & (lane < k + SUB), jnp.where(lane - k == row, -1.0, 0.0), x)
        w = four(four(p, 0, k, lane), 4, k + 4, lane)
        xh, xm, xl = parts(x)
        wh, wm, wl = parts(stack(w))
        x6 = jnp.concatenate([xh, xh, xm, xm, xh, xl], axis=0)
        w6 = jnp.concatenate([wh, wm, wh, wm, wl, wh], axis=0)
        after = pl.multiple_of(lax.rem(t + 1, size // SUB) * SUB, SUB)
        old = split_rows(m[pl.ds(after, SUB)])
        inside = (lane >= k) & (lane < k + SUB)
        p = []
        for q in old:
            new = jnp.where(inside, 0.0, q)
            for j in range(0, SUB, 2):
                new = new - (spread(q, k + j) * w[j] + spread(q, k + j + 1) * w[j + 1])
            p.append(new)
        m[pl.ds(k, SUB)] = jnp.zeros((SUB, size), F32)
        return tuple(p), x6, w6

    nothing = jnp.zeros((6 * SUB, size), F32)
    _, x6, w6 = lax.fori_loop(0, size // SUB, step, (tuple(split_rows(m[0:SUB])), nothing, nothing))
    trail(size // SUB - 1, x6, w6)


def scaled_inverse(matrix, work):
    size = matrix.shape[0]
    rows = lax.broadcasted_iota(jnp.int32, (size, size), 0)
    cols = lax.broadcasted_iota(jnp.int32, (size, size), 1)
    diagonal = jnp.where(rows == cols, matrix, 0.0)
    down = lax.rsqrt(jnp.sum(diagonal, axis=1, keepdims=True))
    across = lax.rsqrt(jnp.sum(diagonal, axis=0, keepdims=True))
    work[...] = matrix * down * across
    invert(work)
    return work[...] * down * across


def basis_kernel(inverse, basis, carried, gram):
    q = mm(inverse[...], basis[...])
    carried[...] = q
    gram[...] = mm(basis[...], q, HIGH, ((0,), (0,)))


def leaf_kernel(order, rhs, inverse, basis, carried, solved, projected, carried_out):
    points = rhs.shape[0]
    wide = 128
    numbers = order[...].astype(F32)
    lanes = lax.broadcasted_iota(jnp.int32, (wide, points), 1).astype(F32)
    gather = []
    for i in range(0, points, wide):
        column = jnp.broadcast_to(numbers[:, i:i + wide], (wide, wide)).T
        column = jnp.concatenate([column] * (points // wide), axis=1)
        gather.append(jnp.where(column == lanes, 1.0, 0.0).astype(BF16))
    gather = jnp.concatenate(gather, axis=0)
    rows = lax.broadcasted_iota(jnp.int32, (points, points), 0).astype(F32)
    scatter = jnp.where(numbers == rows, 1.0, 0.0).astype(BF16)
    z = mm(inverse[...], pick(gather, rhs[...]))
    projected[...] = mm(basis[...], z, HIGH, ((0,), (0,)))
    solved[...] = pick(scatter, z)
    carried_out[...] = pick(scatter, carried[...])


def node_kernel(level, gram, other, precision, *rest):
    coupling = precision[0, level].astype(F32)
    whole = gram[...] + other[...]
    if len(rest) == 2:
        rest[0][...] = scaled_inverse(coupling + whole, rest[1])
        return
    transfer, inverse, mover, gram_out, work = rest
    mixer = transfer[0, level].astype(F32)
    left = mm(mixer, coupling, FULL, ((0,), (0,)))
    right = mm(whole, mixer, FULL)
    m = scaled_inverse(coupling + whole, work)
    n = mm(left, m, FULL)
    inverse[...] = m
    mover[...] = n
    gram_out[...] = mm(n, right, FULL)


def lift_kernel(first, last, *refs):
    refs = list(refs)
    projected, other, inverse, mover = (ref[...] for ref in refs[:4])
    s = projected + other
    alpha = mm(inverse, s)
    projected_out, total_out, mixing_out = refs[-3:]
    projected_out[...] = mm(mover, s)
    if first:
        total, mixing = alpha, mover.T
    else:
        total, mixing = refs[4][...], refs[5][...]
        total = total + mm(mixing, alpha)
        mixing = mm(mixing, mover, FULL, ((1,), (1,)))
    if last:
        solved, carried = refs[-5:-3]
        total = solved[...] - mm(carried[...], total)
        mixing = mm(carried[...], mixing)
    total_out[...] = total
    mixing_out[...] = mixing


def root_kernel(projected, other, inverse, solved, carried, out):
    s = projected[...] + other[...]
    out[...] = solved[...] - mm(carried[...], mm(inverse[...], s))


def call(kernel, outs, *args, scratch=(), work=0):
    return pl.pallas_call(
        kernel,
        out_shape=[jax.ShapeDtypeStruct(shape, F32) for shape in outs],
        in_specs=[VMEM] * len(args),
        out_specs=[VMEM] * len(outs),
        scratch_shapes=[pltpu.VMEM(shape, F32) for shape in scratch],
        cost_estimate=pl.CostEstimate(flops=work, bytes_accessed=0, transcendentals=0),
        compiler_params=PARAMS,
    )(*args)


def from_partner(block, axis, apart):
    count = lax.axis_size(axis)
    return lax.ppermute(block, axis, [(i, i ^ 1 << apart) for i in range(count)])


def body(rhs, order, inverse, basis, transfer, precision):
    points, columns = rhs.shape
    rank = basis.shape[1]
    square, tall, block = (rank, rank), (points, rank), (rank, columns)
    levels = lax.axis_size("leaf").bit_length() - 1
    carried, gram = call(basis_kernel, [tall, square], inverse, basis)
    other_gram = from_partner(gram, "leaf", 0)
    solved, projected, carried = call(
        leaf_kernel, [(points, columns), block, tall], order, rhs, inverse, basis, carried, work=3 * GIGA
    )
    state = ()
    for k in range(levels - 1):
        other = from_partner(projected, "leaf", k)
        m, n, gram = call(
            functools.partial(node_kernel, k), [square] * 3, gram, other_gram, precision, transfer,
            scratch=[square], work=6 * GIGA
        )
        other_gram = from_partner(gram, "leaf", k + 1)
        last = k == levels - 2
        projected, *state = call(
            functools.partial(lift_kernel, k == 0, last),
            [block, (points, columns), tall] if last else [block, block, square],
            projected, other, m, n, *state, *((solved, carried) if last else ()), work=GIGA
        )
    solved, carried = state or (solved, carried)
    k = levels - 1
    other = from_partner(projected, "leaf", k)
    (m,) = call(functools.partial(node_kernel, k), [square], gram, other_gram, precision, scratch=[square], work=6 * GIGA)
    (out,) = call(root_kernel, [(points, columns)], projected, other, m, solved, carried, work=GIGA)
    return out


def solution(mesh):
    placed = (
        P("leaf", "rhs"),
        P("leaf", None),
        P("leaf", None),
        P("leaf", None),
        P("leaf", None, None, None),
        P("leaf", None, None, None),
    )
    return jax.shard_map(
        body, mesh=mesh, in_specs=placed, out_specs=P("leaf", "rhs"), check_vma=False
    )
```

```python
import functools

import jax
import jax.numpy as jnp
from jax import lax
from jax.experimental import pallas as pl
from jax.experimental.pallas import tpu as pltpu
from jax.sharding import PartitionSpec as P

F32 = jnp.float32
BF16 = jnp.bfloat16
HIGH = lax.Precision.HIGH
FULL = lax.Precision.HIGHEST
SUB = 8
GIGA = 10 ** 9
VMEM = pl.BlockSpec(memory_space=pltpu.VMEM)
FAR = pl.BlockSpec(memory_space=pltpu.HBM)
PARAMS = pltpu.CompilerParams(vmem_limit_bytes=32 * 1024 * 1024)


def mm(a, b, precision=HIGH, dims=((1,), (0,))):
    return lax.dot_general(a, b, (dims, ((), ())), precision=precision, preferred_element_type=F32)


def split(x):
    top = x.astype(BF16)
    return top, (x - top.astype(F32)).astype(BF16)


def pick(mask, x):
    top, low = split(x)
    one = lambda part: lax.dot_general(mask, part, (((1,), (0,)), ((), ())), preferred_element_type=F32)
    return one(top) + one(low)


def reciprocal(x):
    return pltpu.reciprocal(x, approx=True)

def parts(x):
    top = x.astype(BF16).astype(F32)
    rest = x - top
    mid = rest.astype(BF16).astype(F32)
    return top, mid, rest - mid

def spread(x, k):
    return jnp.take_along_axis(x, jnp.full(x.shape, k, jnp.int32), axis=1, mode="promise_in_bounds")


def four(x, y, at, k, lane, row, hold):
    size = x.shape[1]
    inside = (lane >= k) & (lane < k + 4)
    own = (row >= at) & (row < at + 4)
    cols = [spread(x, k + j) for j in range(4)]
    hold[4] = x
    for j in range(4):
        hold[j] = cols[j]
    line = lambda j, i: jnp.broadcast_to(hold[j, at + i:at + i + 1], (SUB, size))
    e = [jnp.where(inside, jnp.where(lane == k + j, 1.0, 0.0), line(4, j)) for j in range(4)]
    a0, a1, a2 = line(0, 0), line(1, 0), line(1, 1)
    b00, b01, b10, b11 = line(0, 2), line(1, 2), line(0, 3), line(1, 3)
    c0, c1, c2 = line(2, 2), line(3, 2), line(3, 3)
    det = a0 * a2 - a1 * a1
    g00, g01 = b00 * a2 - b01 * a1, b01 * a0 - b00 * a1
    g10, g11 = b10 * a2 - b11 * a1, b11 * a0 - b10 * a1
    s0 = det * c0 - (g00 * b00 + g01 * b01)
    s1 = det * c1 - (g00 * b10 + g01 * b11)
    s2 = det * c2 - (g10 * b10 + g11 * b11)
    rs = reciprocal(s0 * s2 - s1 * s1)
    ra = reciprocal(det)
    t2 = det * e[2] - (g00 * e[0] + g01 * e[1])
    t3 = det * e[3] - (g10 * e[0] + g11 * e[1])
    w2 = (s2 * t2 - s1 * t3) * rs
    w3 = (s0 * t3 - s1 * t2) * rs
    w0 = ((a2 * e[0] - a1 * e[1]) - (g00 * w2 + g10 * w3)) * ra
    w1 = ((a0 * e[1] - a1 * e[0]) - (g01 * w2 + g11 * w3)) * ra
    down = [spread(y, k + j) for j in range(4)]
    cols = [jnp.where(own, jnp.where(row == at + j, -1.0, 0.0), cols[j]) for j in range(4)]
    out = []
    for base, c in ((jnp.where(inside | own, 0.0, x), cols), (jnp.where(inside, 0.0, y), down)):
        out.append((base - (c[2] * w2 + c[3] * w3)) - (c[0] * w0 + c[1] * w1))
    return out


def invert(m, xt, w6, wide_w, hold):
    size = m.shape[0]
    lane = lax.broadcasted_iota(jnp.int32, (SUB, size), 1)
    row = lax.broadcasted_iota(jnp.int32, (SUB, size), 0)
    wide = lax.broadcasted_iota(jnp.int32, (size, size), 1)
    count = size // SUB

    def trail(t):
        k = t * SUB
        u = jnp.dot(xt[...], w6[...], preferred_element_type=F32)
        m[...] = jnp.where((wide >= k) & (wide < k + SUB), 0.0, m[...]) - u

    def step(t, x):
        k = pl.multiple_of(t * SUB, SUB)
        before = k - SUB
        y = m[pl.ds(pl.multiple_of(lax.rem(t + 1, count) * SUB, SUB), SUB)]
        terms = [spread(y, jnp.maximum(before, 0) + j) * jnp.broadcast_to(wide_w[j:j + 1], (SUB, size)) for j in range(SUB)]
        y = jnp.where((lane >= before) & (lane < k), 0.0, y)
        y = y - (((terms[0] + terms[1]) + (terms[2] + terms[3])) + ((terms[4] + terms[5]) + (terms[6] + terms[7])))
        trail(t - 1)
        z = jnp.where(lane < k, -1.0, 1.0) * x
        z = jnp.where((lane >= k) & (lane < k + SUB), jnp.where(lane - k == row, -1.0, 0.0), z)
        h, n, l = parts(z)
        xt[...] = jnp.concatenate([h, h, n, n, h, l], axis=0).astype(BF16).T
        x, y = four(x, y, 0, k, lane, row, hold.at[0])
        x, y = four(x, y, 4, k + 4, lane, row, hold.at[1])
        h, n, l = parts(x)
        w6[...] = jnp.concatenate([h, n, h, n, l, h], axis=0).astype(BF16)
        wide_w[...] = x
        m[pl.ds(k, SUB)] = jnp.zeros((SUB, size), F32)
        return y

    xt[...] = jnp.zeros(xt.shape, BF16)
    w6[...] = jnp.zeros(w6.shape, BF16)
    wide_w[...] = jnp.zeros((SUB, size), F32)
    lax.fori_loop(0, count, step, m[0:SUB])
    trail(count - 1)


def invert_scratch(size):
    return [
        pltpu.VMEM((size, size), F32), pltpu.VMEM((size, 6 * SUB), BF16), pltpu.VMEM((6 * SUB, size), BF16),
        pltpu.VMEM((SUB, size), F32), pltpu.VMEM((2, 5, SUB, size), F32),
    ]


def scaled_inverse(matrix, *work):
    size = matrix.shape[0]
    rows = lax.broadcasted_iota(jnp.int32, (size, size), 0)
    cols = lax.broadcasted_iota(jnp.int32, (size, size), 1)
    diagonal = jnp.where(rows == cols, matrix, 0.0)
    down = lax.rsqrt(jnp.sum(diagonal, axis=1, keepdims=True))
    across = lax.rsqrt(jnp.sum(diagonal, axis=0, keepdims=True))
    work[0][...] = matrix * down * across
    invert(*work)
    return work[0][...] * down * across


def basis_kernel(pieces, inverse_far, basis_far, inverse, basis, carried, gram, sems):
    rows = inverse.shape[0] // pieces
    copies = [pltpu.make_async_copy(basis_far, basis, sems.at[pieces])]
    for i in range(pieces):
        part = pl.ds(i * rows, rows)
        copies.append(pltpu.make_async_copy(inverse_far.at[part], inverse.at[part], sems.at[i]))
    for copy in copies:
        copy.start()
    copies[0].wait()
    for i in range(pieces):
        copies[i + 1].wait()
        carried[i * rows:(i + 1) * rows] = mm(inverse[i * rows:(i + 1) * rows], basis[...])
    gram[...] = mm(basis[...], carried[...], HIGH, ((0,), (0,)))


def leaf_kernel(order, rhs, inverse, basis, carried, solved, projected, carried_out):
    points = rhs.shape[0]
    wide = 128
    numbers = order[...].astype(F32)
    lanes = lax.broadcasted_iota(jnp.int32, (wide, points), 1).astype(F32)
    gather = []
    for i in range(0, points, wide):
        column = jnp.broadcast_to(numbers[:, i:i + wide], (wide, wide)).T
        column = jnp.concatenate([column] * (points // wide), axis=1)
        gather.append(jnp.where(column == lanes, 1.0, 0.0).astype(BF16))
    gather = jnp.concatenate(gather, axis=0)
    rows = lax.broadcasted_iota(jnp.int32, (points, points), 0).astype(F32)
    scatter = jnp.where(numbers == rows, 1.0, 0.0).astype(BF16)
    z = mm(inverse[...], pick(gather, rhs[...]))
    projected[...] = mm(basis[...], z, HIGH, ((0,), (0,)))
    solved[...] = pick(scatter, z)
    carried_out[...] = pick(scatter, carried[...])


def node_kernel(level, gram, other, precision, *rest):
    coupling = precision[0, level].astype(F32)
    whole = gram[...] + other[...]
    if len(rest) == 6:
        rest[0][...] = scaled_inverse(coupling + whole, *rest[1:])
        return
    transfer, inverse, mover, gram_out, *work = rest
    mixer = transfer[0, level].astype(F32)
    left = mm(mixer, coupling, FULL, ((0,), (0,)))
    right = mm(whole, mixer, FULL)
    m = scaled_inverse(coupling + whole, *work)
    n = mm(left, m, FULL)
    inverse[...] = m
    mover[...] = n
    gram_out[...] = mm(n, right, FULL)


def lift_kernel(first, last, *refs):
    refs = list(refs)
    projected, other, inverse, mover = (ref[...] for ref in refs[:4])
    s = projected + other
    alpha = mm(inverse, s)
    projected_out, total_out, mixing_out = refs[-3:]
    projected_out[...] = mm(mover, s)
    if first:
        total, mixing = alpha, mover.T
    else:
        total, mixing = refs[4][...], refs[5][...]
        total = total + mm(mixing, alpha)
        mixing = mm(mixing, mover, FULL, ((1,), (1,)))
    if last:
        solved, carried = refs[-5:-3]
        total = solved[...] - mm(carried[...], total)
        mixing = mm(carried[...], mixing)
    total_out[...] = total
    mixing_out[...] = mixing


def root_kernel(projected, other, inverse, solved, carried, out):
    s = projected[...] + other[...]
    out[...] = solved[...] - mm(carried[...], mm(inverse[...], s))


def call(kernel, outs, *args, scratch=(), work=0, place=VMEM):
    if place is FAR:
        args = [pltpu.with_memory_space_constraint(arg, pltpu.HBM) for arg in args]
    return pl.pallas_call(
        kernel,
        out_shape=[jax.ShapeDtypeStruct(shape, F32) for shape in outs],
        in_specs=[place] * len(args),
        out_specs=[VMEM] * len(outs),
        scratch_shapes=scratch,
        cost_estimate=pl.CostEstimate(flops=work, bytes_accessed=0, transcendentals=0),
        compiler_params=PARAMS,
    )(*args)


def from_partner(block, axis, apart):
    count = lax.axis_size(axis)
    return lax.ppermute(block, axis, [(i, i ^ 1 << apart) for i in range(count)])


def body(rhs, order, inverse, basis, transfer, precision):
    points, columns = rhs.shape
    rank = basis.shape[1]
    square, tall, block = (rank, rank), (points, rank), (rank, columns)
    levels = lax.axis_size("leaf").bit_length() - 1
    pieces = 4
    inverse, basis, carried, gram = call(
        functools.partial(basis_kernel, pieces), [inverse.shape, tall, tall, square], inverse, basis,
        scratch=[pltpu.SemaphoreType.DMA((pieces + 1,))], place=FAR, work=GIGA
    )
    other_gram = from_partner(gram, "leaf", 0)
    solved, projected, carried = call(
        leaf_kernel, [(points, columns), block, tall], order, rhs, inverse, basis, carried, work=3 * GIGA
    )
    state = ()
    for k in range(levels - 1):
        other = from_partner(projected, "leaf", k)
        m, n, gram = call(
            functools.partial(node_kernel, k), [square] * 3, gram, other_gram, precision, transfer,
            scratch=invert_scratch(rank), work=6 * GIGA
        )
        other_gram = from_partner(gram, "leaf", k + 1)
        last = k == levels - 2
        projected, *state = call(
            functools.partial(lift_kernel, k == 0, last),
            [block, (points, columns), tall] if last else [block, block, square],
            projected, other, m, n, *state, *((solved, carried) if last else ()), work=GIGA
        )
    solved, carried = state or (solved, carried)
    k = levels - 1
    other = from_partner(projected, "leaf", k)
    (m,) = call(functools.partial(node_kernel, k), [square], gram, other_gram, precision, scratch=invert_scratch(rank), work=6 * GIGA)
    (out,) = call(root_kernel, [(points, columns)], projected, other, m, solved, carried, work=GIGA)
    return out


def solution(mesh):
    placed = (
        P("leaf", "rhs"),
        P("leaf", None),
        P("leaf", None),
        P("leaf", None),
        P("leaf", None, None, None),
        P("leaf", None, None, None),
    )
    return jax.shard_map(
        body, mesh=mesh, in_specs=placed, out_specs=P("leaf", "rhs"), check_vma=False
    )
```

```python
import functools

import jax
import jax.numpy as jnp
from jax import lax
from jax.experimental import pallas as pl
from jax.experimental.pallas import tpu as pltpu
from jax.sharding import PartitionSpec as P

F32 = jnp.float32
BF16 = jnp.bfloat16
HIGH = lax.Precision.HIGH
SUB = 8
GIGA = 10 ** 9
VMEM = pl.BlockSpec(memory_space=pltpu.VMEM)
FAR = pl.BlockSpec(memory_space=pltpu.HBM)
PARAMS = pltpu.CompilerParams(vmem_limit_bytes=32 * 1024 * 1024)


def mm(a, b, precision=HIGH, dims=((1,), (0,))):
    return lax.dot_general(a, b, (dims, ((), ())), precision=precision, preferred_element_type=F32)


def split(x):
    top = x.astype(BF16)
    return top, (x - top.astype(F32)).astype(BF16)


def pick(mask, x):
    top, low = split(x)
    one = lambda part: lax.dot_general(mask, part, (((1,), (0,)), ((), ())), preferred_element_type=F32)
    return one(top) + one(low)


def reciprocal(x):
    return pltpu.reciprocal(x, approx=True)

def parts(x):
    top = x.astype(BF16).astype(F32)
    rest = x - top
    mid = rest.astype(BF16).astype(F32)
    return top, mid, rest - mid

def spread(x, k):
    return jnp.take_along_axis(x, jnp.full(x.shape, k, jnp.int32), axis=1, mode="promise_in_bounds")


def four(x, y, at, k, lane, row, hold):
    size = x.shape[1]
    inside = (lane >= k) & (lane < k + 4)
    own = (row >= at) & (row < at + 4)
    cols = [spread(x, k + j) for j in range(4)]
    hold[4] = x
    for j in range(4):
        hold[j] = cols[j]
    line = lambda j, i: jnp.broadcast_to(hold[j, at + i:at + i + 1], (SUB, size))
    e = [jnp.where(inside, jnp.where(lane == k + j, 1.0, 0.0), line(4, j)) for j in range(4)]
    a0, a1, a2 = line(0, 0), line(1, 0), line(1, 1)
    b00, b01, b10, b11 = line(0, 2), line(1, 2), line(0, 3), line(1, 3)
    c0, c1, c2 = line(2, 2), line(3, 2), line(3, 3)
    det = a0 * a2 - a1 * a1
    g00, g01 = b00 * a2 - b01 * a1, b01 * a0 - b00 * a1
    g10, g11 = b10 * a2 - b11 * a1, b11 * a0 - b10 * a1
    s0 = det * c0 - (g00 * b00 + g01 * b01)
    s1 = det * c1 - (g00 * b10 + g01 * b11)
    s2 = det * c2 - (g10 * b10 + g11 * b11)
    rs = reciprocal(s0 * s2 - s1 * s1)
    ra = reciprocal(det)
    t2 = det * e[2] - (g00 * e[0] + g01 * e[1])
    t3 = det * e[3] - (g10 * e[0] + g11 * e[1])
    w2 = (s2 * t2 - s1 * t3) * rs
    w3 = (s0 * t3 - s1 * t2) * rs
    w0 = ((a2 * e[0] - a1 * e[1]) - (g00 * w2 + g10 * w3)) * ra
    w1 = ((a0 * e[1] - a1 * e[0]) - (g01 * w2 + g11 * w3)) * ra
    down = [spread(y, k + j) for j in range(4)]
    cols = [jnp.where(own, jnp.where(row == at + j, -1.0, 0.0), cols[j]) for j in range(4)]
    out = []
    for base, c in ((jnp.where(inside | own, 0.0, x), cols), (jnp.where(inside, 0.0, y), down)):
        out.append((base - (c[2] * w2 + c[3] * w3)) - (c[0] * w0 + c[1] * w1))
    return out


def invert(m, xt, w6, wide_w, hold):
    size = m.shape[0]
    lane = lax.broadcasted_iota(jnp.int32, (SUB, size), 1)
    row = lax.broadcasted_iota(jnp.int32, (SUB, size), 0)
    wide = lax.broadcasted_iota(jnp.int32, (size, size), 1)
    count = size // SUB

    def trail(t):
        k = t * SUB
        u = jnp.dot(xt[...], w6[...], preferred_element_type=F32)
        m[...] = jnp.where((wide >= k) & (wide < k + SUB), 0.0, m[...]) - u

    def step(t, x):
        k = pl.multiple_of(t * SUB, SUB)
        before = k - SUB
        y = m[pl.ds(pl.multiple_of(lax.rem(t + 1, count) * SUB, SUB), SUB)]
        terms = [spread(y, jnp.maximum(before, 0) + j) * jnp.broadcast_to(wide_w[j:j + 1], (SUB, size)) for j in range(SUB)]
        y = jnp.where((lane >= before) & (lane < k), 0.0, y)
        y = y - (((terms[0] + terms[1]) + (terms[2] + terms[3])) + ((terms[4] + terms[5]) + (terms[6] + terms[7])))
        trail(t - 1)
        z = jnp.where(lane < k, -1.0, 1.0) * x
        z = jnp.where((lane >= k) & (lane < k + SUB), jnp.where(lane - k == row, -1.0, 0.0), z)
        h, n, l = parts(z)
        xt[...] = jnp.concatenate([h, h, n, n, h, l], axis=0).astype(BF16).T
        x, y = four(x, y, 0, k, lane, row, hold.at[0])
        x, y = four(x, y, 4, k + 4, lane, row, hold.at[1])
        h, n, l = parts(x)
        w6[...] = jnp.concatenate([h, n, h, n, l, h], axis=0).astype(BF16)
        wide_w[...] = x
        m[pl.ds(k, SUB)] = jnp.zeros((SUB, size), F32)
        return y

    xt[...] = jnp.zeros(xt.shape, BF16)
    w6[...] = jnp.zeros(w6.shape, BF16)
    wide_w[...] = jnp.zeros((SUB, size), F32)
    lax.fori_loop(0, count, step, m[0:SUB], unroll=2)
    trail(count - 1)


def invert_scratch(size):
    return [
        pltpu.VMEM((size, size), F32), pltpu.VMEM((size, 6 * SUB), BF16), pltpu.VMEM((6 * SUB, size), BF16),
        pltpu.VMEM((SUB, size), F32), pltpu.VMEM((2, 5, SUB, size), F32),
    ]


def scaled_inverse(matrix, *work):
    size = matrix.shape[0]
    rows = lax.broadcasted_iota(jnp.int32, (size, size), 0)
    cols = lax.broadcasted_iota(jnp.int32, (size, size), 1)
    diagonal = jnp.where(rows == cols, matrix, 0.0)
    down = lax.rsqrt(jnp.sum(diagonal, axis=1, keepdims=True))
    across = lax.rsqrt(jnp.sum(diagonal, axis=0, keepdims=True))
    work[0][...] = matrix * down * across
    invert(*work)
    return work[0][...] * down * across


def basis_kernel(pieces, inverse_far, basis_far, order_far, inverse, basis, order, carried, gram, sems):
    rows = inverse.shape[0] // pieces
    copies = [pltpu.make_async_copy(basis_far, basis, sems.at[pieces])]
    for i in range(pieces):
        part = pl.ds(i * rows, rows)
        copies.append(pltpu.make_async_copy(inverse_far.at[part], inverse.at[part], sems.at[i]))
    copies.append(pltpu.make_async_copy(order_far, order, sems.at[pieces + 1]))
    for copy in copies:
        copy.start()
    copies[0].wait()
    for i in range(pieces):
        copies[i + 1].wait()
        carried[i * rows:(i + 1) * rows] = mm(inverse[i * rows:(i + 1) * rows], basis[...])
    gram[...] = mm(basis[...], carried[...], HIGH, ((0,), (0,)))
    copies[-1].wait()


def leaf_kernel(order, rhs, inverse, basis, solved, projected):
    points = rhs.shape[0]
    wide = 128
    numbers = order[...].astype(F32)
    lanes = lax.broadcasted_iota(jnp.int32, (wide, points), 1).astype(F32)
    gather = []
    for i in range(0, points, wide):
        column = jnp.broadcast_to(numbers[:, i:i + wide], (wide, wide)).T
        column = jnp.concatenate([column] * (points // wide), axis=1)
        gather.append(jnp.where(column == lanes, 1.0, 0.0).astype(BF16))
    z = mm(inverse[...], pick(jnp.concatenate(gather, axis=0), rhs[...]))
    solved[...] = z
    projected[...] = mm(basis[...], z, HIGH, ((0,), (0,)))


def place_kernel(order, solved, carried, solved_out, carried_out):
    points = solved.shape[0]
    rows = lax.broadcasted_iota(jnp.int32, (points, points), 0)
    scatter = jnp.where(order[...] == rows, 1.0, 0.0).astype(BF16)
    solved_out[...] = pick(scatter, solved[...])
    carried_out[...] = pick(scatter, carried[...])


def node_kernel(level, gram, other, precision, *rest):
    coupling = precision[0, level].astype(F32)
    whole = gram[...] + other[...]
    if len(rest) == 6:
        rest[0][...] = scaled_inverse(coupling + whole, *rest[1:])
        return
    transfer, inverse, mover, gram_out, *work = rest
    mixer = transfer[0, level]
    left = mm(mixer, precision[0, level], None, ((0,), (0,)))
    right = sum(mm(part.astype(BF16), mixer, None) for part in parts(whole))
    m = scaled_inverse(coupling + whole, *work)
    n = mm(left, m)
    inverse[...] = m
    mover[...] = n
    gram_out[...] = mm(n, right)


def lift_kernel(first, last, *refs):
    refs = list(refs)
    projected, other, inverse, mover = (ref[...] for ref in refs[:4])
    s = projected + other
    alpha = mm(inverse, s)
    projected_out, total_out, mixing_out = refs[-3:]
    projected_out[...] = mm(mover, s)
    if first:
        total, mixing = alpha, mover.T
    else:
        total, mixing = refs[4][...], refs[5][...]
        total = total + mm(mixing, alpha)
        mixing = mm(mixing, mover, HIGH, ((1,), (1,)))
    if last:
        solved, carried = refs[-5:-3]
        total = solved[...] - mm(carried[...], total)
        mixing = mm(carried[...], mixing)
    total_out[...] = total
    mixing_out[...] = mixing


def root_kernel(pieces, projected, other, inverse, solved, carried, out_far, out, sems):
    alpha = mm(inverse[...], projected[...] + other[...])
    rows = out.shape[0] // pieces
    copies = []
    for i in range(pieces):
        part = pl.ds(i * rows, rows)
        out[part] = solved[part] - mm(carried[part], alpha)
        copies.append(pltpu.make_async_copy(out.at[part], out_far.at[part], sems.at[i]))
        copies[-1].start()
    for copy in copies:
        copy.wait()


def call(kernel, outs, *args, scratch=(), work=0, place=VMEM, result=VMEM, after=()):
    if place is FAR:
        args = [pltpu.with_memory_space_constraint(arg, pltpu.HBM) for arg in args]
    return pl.pallas_call(
        lambda *refs: kernel(*refs[len(after):]),
        out_shape=[jax.ShapeDtypeStruct(getattr(out, "shape", out), getattr(out, "dtype", F32)) for out in outs],
        in_specs=[FAR] * len(after) + [place] * len(args),
        out_specs=[result] * len(outs),
        scratch_shapes=scratch,
        cost_estimate=pl.CostEstimate(flops=work, bytes_accessed=0, transcendentals=0),
        compiler_params=PARAMS,
    )(*after, *args)


def from_partner(block, axis, apart):
    count = lax.axis_size(axis)
    return lax.ppermute(block, axis, [(i, i ^ 1 << apart) for i in range(count)])


def body(rhs, order, inverse, basis, transfer, precision):
    points, columns = rhs.shape
    rank = basis.shape[1]
    square, tall, block = (rank, rank), (points, rank), (rank, columns)
    levels = lax.axis_size("leaf").bit_length() - 1
    pieces = 4
    inverse, basis, order, carried, gram = call(
        functools.partial(basis_kernel, pieces), [inverse.shape, tall, order, tall, square], inverse, basis, order,
        scratch=[pltpu.SemaphoreType.DMA((pieces + 2,))], place=FAR, work=GIGA
    )
    other_gram = from_partner(gram, "leaf", 0)
    solved, projected = call(leaf_kernel, [rhs, block], order, rhs, inverse, basis, work=2 * GIGA)
    place = lambda *after: call(place_kernel, [rhs, tall], order, solved, carried, work=GIGA, after=after)
    if levels < 3:
        solved, carried = place()
    state, after = (), ()
    for k in range(levels - 1):
        other = from_partner(projected, "leaf", k)
        m, n, gram = call(
            functools.partial(node_kernel, k), [square] * 3, gram, other_gram, precision, transfer,
            scratch=invert_scratch(rank), work=6 * GIGA, after=after
        )
        other_gram = from_partner(gram, "leaf", k + 1)
        last = k == levels - 2
        projected, *state = call(
            functools.partial(lift_kernel, k == 0, last),
            [block, (points, columns), tall] if last else [block, block, square],
            projected, other, m, n, *state, *((solved, carried) if last else ()), work=GIGA
        )
        if k == 0 and not last:
            solved, carried = place(projected)
            after = (carried,)
    solved, carried = state or (solved, carried)
    k = levels - 1
    other = from_partner(projected, "leaf", k)
    (m,) = call(functools.partial(node_kernel, k), [square], gram, other_gram, precision, scratch=invert_scratch(rank), work=6 * GIGA)
    (out,) = call(
        functools.partial(root_kernel, pieces), [rhs], projected, other, m, solved, carried, work=GIGA, result=FAR,
        scratch=[pltpu.VMEM(rhs.shape, F32), pltpu.SemaphoreType.DMA((pieces,))]
    )
    return out


def solution(mesh):
    placed = (
        P("leaf", "rhs"),
        P("leaf", None),
        P("leaf", None),
        P("leaf", None),
        P("leaf", None, None, None),
        P("leaf", None, None, None),
    )
    return jax.shard_map(
        body, mesh=mesh, in_specs=placed, out_specs=P("leaf", "rhs"), check_vma=False
    )
```

```python
import functools

import jax
import jax.numpy as jnp
from jax import lax
from jax.experimental import pallas as pl
from jax.experimental.pallas import tpu as pltpu
from jax.sharding import PartitionSpec as P

F32 = jnp.float32
BF16 = jnp.bfloat16
HIGH = lax.Precision.HIGH
SUB = 8
GIGA = 10 ** 9
VMEM = pl.BlockSpec(memory_space=pltpu.VMEM)
FAR = pl.BlockSpec(memory_space=pltpu.HBM)
PARAMS = pltpu.CompilerParams(vmem_limit_bytes=32 * 1024 * 1024)


def mm(a, b, precision=HIGH, dims=((1,), (0,))):
    return lax.dot_general(a, b, (dims, ((), ())), precision=precision, preferred_element_type=F32)


def split(x):
    top = x.astype(BF16)
    return top, (x - top.astype(F32)).astype(BF16)


def pick(mask, x):
    top, low = split(x)
    one = lambda part: lax.dot_general(mask, part, (((1,), (0,)), ((), ())), preferred_element_type=F32)
    return one(top) + one(low)


def reciprocal(x):
    return pltpu.reciprocal(x, approx=True)

def parts(x):
    top = x.astype(BF16).astype(F32)
    rest = x - top
    mid = rest.astype(BF16).astype(F32)
    return top, mid, rest - mid

def spread(x, k):
    return jnp.take_along_axis(x, jnp.full(x.shape, k, jnp.int32), axis=1, mode="promise_in_bounds")


def four(x, y, at, k, lane, row, hold):
    size = x.shape[1]
    inside = (lane >= k) & (lane < k + 4)
    own = (row >= at) & (row < at + 4)
    cols = [spread(x, k + j) for j in range(4)]
    hold[4] = x
    for j in range(4):
        hold[j] = cols[j]
    line = lambda j, i: jnp.broadcast_to(hold[j, at + i:at + i + 1], (SUB, size))
    e = [jnp.where(inside, jnp.where(lane == k + j, 1.0, 0.0), line(4, j)) for j in range(4)]
    a0, a1, a2 = line(0, 0), line(1, 0), line(1, 1)
    b00, b01, b10, b11 = line(0, 2), line(1, 2), line(0, 3), line(1, 3)
    c0, c1, c2 = line(2, 2), line(3, 2), line(3, 3)
    det = a0 * a2 - a1 * a1
    g00, g01 = b00 * a2 - b01 * a1, b01 * a0 - b00 * a1
    g10, g11 = b10 * a2 - b11 * a1, b11 * a0 - b10 * a1
    s0 = det * c0 - (g00 * b00 + g01 * b01)
    s1 = det * c1 - (g00 * b10 + g01 * b11)
    s2 = det * c2 - (g10 * b10 + g11 * b11)
    rs = reciprocal(s0 * s2 - s1 * s1)
    ra = reciprocal(det)
    t2 = det * e[2] - (g00 * e[0] + g01 * e[1])
    t3 = det * e[3] - (g10 * e[0] + g11 * e[1])
    w2 = (s2 * t2 - s1 * t3) * rs
    w3 = (s0 * t3 - s1 * t2) * rs
    w0 = ((a2 * e[0] - a1 * e[1]) - (g00 * w2 + g10 * w3)) * ra
    w1 = ((a0 * e[1] - a1 * e[0]) - (g01 * w2 + g11 * w3)) * ra
    down = [spread(y, k + j) for j in range(4)]
    cols = [jnp.where(own, jnp.where(row == at + j, -1.0, 0.0), cols[j]) for j in range(4)]
    out = []
    for base, c in ((jnp.where(inside | own, 0.0, x), cols), (jnp.where(inside, 0.0, y), down)):
        out.append((base - (c[2] * w2 + c[3] * w3)) - (c[0] * w0 + c[1] * w1))
    return out


def invert(m, xt, w6, wide_w, hold):
    size = m.shape[0]
    lane = lax.broadcasted_iota(jnp.int32, (SUB, size), 1)
    row = lax.broadcasted_iota(jnp.int32, (SUB, size), 0)
    wide = lax.broadcasted_iota(jnp.int32, (size, size), 1)
    count = size // SUB

    def trail(t):
        k = t * SUB
        u = jnp.dot(xt[...], w6[...], preferred_element_type=F32)
        m[...] = jnp.where((wide >= k) & (wide < k + SUB), 0.0, m[...]) - u

    def step(t, x):
        k = pl.multiple_of(t * SUB, SUB)
        before = k - SUB
        y = m[pl.ds(pl.multiple_of(lax.rem(t + 1, count) * SUB, SUB), SUB)]
        terms = [spread(y, jnp.maximum(before, 0) + j) * jnp.broadcast_to(wide_w[j:j + 1], (SUB, size)) for j in range(SUB)]
        y = jnp.where((lane >= before) & (lane < k), 0.0, y)
        y = y - (((terms[0] + terms[1]) + (terms[2] + terms[3])) + ((terms[4] + terms[5]) + (terms[6] + terms[7])))
        trail(t - 1)
        z = jnp.where(lane < k, -1.0, 1.0) * x
        z = jnp.where((lane >= k) & (lane < k + SUB), jnp.where(lane - k == row, -1.0, 0.0), z)
        h, n, l = parts(z)
        xt[...] = jnp.concatenate([h, h, n, n, h, l], axis=0).astype(BF16).T
        x, y = four(x, y, 0, k, lane, row, hold.at[0])
        x, y = four(x, y, 4, k + 4, lane, row, hold.at[1])
        h, n, l = parts(x)
        w6[...] = jnp.concatenate([h, n, h, n, l, h], axis=0).astype(BF16)
        wide_w[...] = x
        m[pl.ds(k, SUB)] = jnp.zeros((SUB, size), F32)
        return y

    xt[...] = jnp.zeros(xt.shape, BF16)
    w6[...] = jnp.zeros(w6.shape, BF16)
    wide_w[...] = jnp.zeros((SUB, size), F32)
    lax.fori_loop(0, count, step, m[0:SUB], unroll=2)
    trail(count - 1)


def invert_scratch(size):
    return [
        pltpu.VMEM((size, size), F32), pltpu.VMEM((size, 6 * SUB), BF16), pltpu.VMEM((6 * SUB, size), BF16),
        pltpu.VMEM((SUB, size), F32), pltpu.VMEM((2, 5, SUB, size), F32),
    ]


def scaled_inverse(matrix, *work):
    size = matrix.shape[0]
    rows = lax.broadcasted_iota(jnp.int32, (size, size), 0)
    cols = lax.broadcasted_iota(jnp.int32, (size, size), 1)
    diagonal = jnp.where(rows == cols, matrix, 0.0)
    down = lax.rsqrt(jnp.sum(diagonal, axis=1, keepdims=True))
    across = lax.rsqrt(jnp.sum(diagonal, axis=0, keepdims=True))
    work[0][...] = matrix * down * across
    invert(*work)
    return work[0][...] * down * across


def basis_kernel(pieces, inverse_far, basis_far, order_far, inverse, basis, order, carried, gram, sems):
    rows = inverse.shape[0] // pieces
    copies = [pltpu.make_async_copy(basis_far, basis, sems.at[pieces])]
    for i in range(pieces):
        part = pl.ds(i * rows, rows)
        copies.append(pltpu.make_async_copy(inverse_far.at[part], inverse.at[part], sems.at[i]))
    copies.append(pltpu.make_async_copy(order_far, order, sems.at[pieces + 1]))
    for copy in copies:
        copy.start()
    copies[0].wait()
    for i in range(pieces):
        copies[i + 1].wait()
        carried[i * rows:(i + 1) * rows] = mm(inverse[i * rows:(i + 1) * rows], basis[...])
    gram[...] = mm(basis[...], carried[...], HIGH, ((0,), (0,)))
    copies[-1].wait()


def leaf_kernel(order, rhs, inverse, basis, solved, projected):
    points = rhs.shape[0]
    wide = 128
    numbers = order[...].astype(F32)
    lanes = lax.broadcasted_iota(jnp.int32, (wide, points), 1).astype(F32)
    gather = []
    for i in range(0, points, wide):
        column = jnp.broadcast_to(numbers[:, i:i + wide], (wide, wide)).T
        column = jnp.concatenate([column] * (points // wide), axis=1)
        gather.append(jnp.where(column == lanes, 1.0, 0.0).astype(BF16))
    z = mm(inverse[...], pick(jnp.concatenate(gather, axis=0), rhs[...]))
    solved[...] = z
    projected[...] = mm(basis[...], z, HIGH, ((0,), (0,)))


def place_kernel(order, solved, carried, solved_out, carried_out):
    points = solved.shape[0]
    rows = lax.broadcasted_iota(jnp.int32, (points, points), 0)
    scatter = jnp.where(order[...] == rows, 1.0, 0.0).astype(BF16)
    solved_out[...] = pick(scatter, solved[...])
    carried_out[...] = pick(scatter, carried[...])


def node_kernel(level, gram, other, precision, *rest):
    coupling = precision[0, level].astype(F32)
    whole = gram[...] + other[...]
    if len(rest) == 6:
        rest[0][...] = scaled_inverse(coupling + whole, *rest[1:])
        return
    transfer, inverse, mover, gram_out, *work = rest
    mixer = transfer[0, level]
    left = mm(mixer, precision[0, level], None, ((0,), (0,)))
    right = sum(mm(part.astype(BF16), mixer, None) for part in parts(whole))
    m = scaled_inverse(coupling + whole, *work)
    n = mm(left, m)
    inverse[...] = m
    mover[...] = n
    gram_out[...] = mm(n, right)


def lift_kernel(first, last, *refs):
    refs = list(refs)
    s, inverse, mover = (ref[...] for ref in refs[:3])
    alpha = mm(inverse, s)
    projected_out, total_out, mixing_out = refs[-3:]
    projected_out[...] = mm(mover, s)
    if first:
        total, mixing = alpha, mover.T
    else:
        total, mixing = refs[3][...], refs[4][...]
        total = total + mm(mixing, alpha)
        mixing = mm(mixing, mover, HIGH, ((1,), (1,)))
    if last:
        solved, carried = refs[-5:-3]
        total = solved[...] - mm(carried[...], total)
        mixing = mm(carried[...], mixing)
    total_out[...] = total
    mixing_out[...] = mixing


def root_kernel(pieces, summed, inverse, solved, carried, out_far, out, sems):
    alpha = mm(inverse[...], summed[...])
    rows = out.shape[0] // pieces
    copies = []
    for i in range(pieces):
        part = pl.ds(i * rows, rows)
        out[part] = solved[part] - mm(carried[part], alpha)
        copies.append(pltpu.make_async_copy(out.at[part], out_far.at[part], sems.at[i]))
        copies[-1].start()
    for copy in copies:
        copy.wait()


def call(kernel, outs, *args, scratch=(), work=0, place=VMEM, result=VMEM, after=()):
    if place is FAR:
        args = [pltpu.with_memory_space_constraint(arg, pltpu.HBM) for arg in args]
    return pl.pallas_call(
        lambda *refs: kernel(*refs[len(after):]),
        out_shape=[jax.ShapeDtypeStruct(getattr(out, "shape", out), getattr(out, "dtype", F32)) for out in outs],
        in_specs=[FAR] * len(after) + [place] * len(args),
        out_specs=[result] * len(outs),
        scratch_shapes=scratch,
        cost_estimate=pl.CostEstimate(flops=work, bytes_accessed=0, transcendentals=0),
        compiler_params=PARAMS,
    )(*after, *args)


def from_partner(block, axis, apart):
    count = lax.axis_size(axis)
    return lax.ppermute(block, axis, [(i, i ^ 1 << apart) for i in range(count)])


def node_sum(block, axis, apart):
    count = lax.axis_size(axis)
    pairs = [[i, i | 1 << apart] for i in range(count) if not i & 1 << apart]
    return lax.psum(block, axis, axis_index_groups=pairs)


def body(rhs, order, inverse, basis, transfer, precision):
    points, columns = rhs.shape
    rank = basis.shape[1]
    square, tall, block = (rank, rank), (points, rank), (rank, columns)
    levels = lax.axis_size("leaf").bit_length() - 1
    pieces = 4
    inverse, basis, order, carried, gram = call(
        functools.partial(basis_kernel, pieces), [inverse.shape, tall, order, tall, square], inverse, basis, order,
        scratch=[pltpu.SemaphoreType.DMA((pieces + 2,))], place=FAR, work=GIGA
    )
    other_gram = from_partner(gram, "leaf", 0)
    solved, projected = call(leaf_kernel, [rhs, block], order, rhs, inverse, basis, work=2 * GIGA)
    place = lambda *after: call(place_kernel, [rhs, tall], order, solved, carried, work=GIGA, after=after)
    if levels < 3:
        solved, carried = place()
    state, after = (), ()
    for k in range(levels - 1):
        s = node_sum(projected, "leaf", k)
        m, n, gram = call(
            functools.partial(node_kernel, k), [square] * 3, gram, other_gram, precision, transfer,
            scratch=invert_scratch(rank), work=6 * GIGA, after=after
        )
        other_gram = from_partner(gram, "leaf", k + 1)
        last = k == levels - 2
        projected, *state = call(
            functools.partial(lift_kernel, k == 0, last),
            [block, (points, columns), tall] if last else [block, block, square],
            s, m, n, *state, *((solved, carried) if last else ()), work=GIGA
        )
        if k == 0 and not last:
            solved, carried = place(projected)
            after = (carried,)
    solved, carried = state or (solved, carried)
    k = levels - 1
    s = node_sum(projected, "leaf", k)
    (m,) = call(functools.partial(node_kernel, k), [square], gram, other_gram, precision, scratch=invert_scratch(rank), work=6 * GIGA)
    (out,) = call(
        functools.partial(root_kernel, pieces), [rhs], s, m, solved, carried, work=GIGA, result=FAR,
        scratch=[pltpu.VMEM(rhs.shape, F32), pltpu.SemaphoreType.DMA((pieces,))]
    )
    return out


def solution(mesh):
    placed = (
        P("leaf", "rhs"),
        P("leaf", None),
        P("leaf", None),
        P("leaf", None),
        P("leaf", None, None, None),
        P("leaf", None, None, None),
    )
    return jax.shard_map(
        body, mesh=mesh, in_specs=placed, out_specs=P("leaf", "rhs"), check_vma=False
    )
```

```python
import functools

import jax
import jax.numpy as jnp
from jax import lax
from jax.experimental import pallas as pl
from jax.experimental.pallas import tpu as pltpu
from jax.sharding import PartitionSpec as P

F32 = jnp.float32
BF16 = jnp.bfloat16
HIGH = lax.Precision.HIGH
SUB = 8
GIGA = 10 ** 9
VMEM = pl.BlockSpec(memory_space=pltpu.VMEM)
FAR = pl.BlockSpec(memory_space=pltpu.HBM)
PARAMS = pltpu.CompilerParams(vmem_limit_bytes=32 * 1024 * 1024)


def mm(a, b, precision=HIGH, dims=((1,), (0,))):
    return lax.dot_general(a, b, (dims, ((), ())), precision=precision, preferred_element_type=F32)


def split(x):
    top = x.astype(BF16)
    return top, (x - top.astype(F32)).astype(BF16)


def mm_parts(a, b):
    one = lambda x, y: jnp.dot(x, y, preferred_element_type=F32)
    return one(a[0], b[0]) + (one(a[0], b[1]) + one(a[1], b[0]))


def pick(mask, x):
    top, low = split(x)
    one = lambda part: lax.dot_general(mask, part, (((1,), (0,)), ((), ())), preferred_element_type=F32)
    return one(top) + one(low)


def reciprocal(x):
    return pltpu.reciprocal(x, approx=True)

def parts(x):
    top = x.astype(BF16).astype(F32)
    rest = x - top
    mid = rest.astype(BF16).astype(F32)
    return top, mid, rest - mid

def spread(x, k):
    return jnp.take_along_axis(x, jnp.full(x.shape, k, jnp.int32), axis=1, mode="promise_in_bounds")


def four(x, y, cols, at, k, lane, row, hold):
    size = x.shape[1]
    across = size // SUB * SUB
    inside = (lane >= k) & (lane < k + 4)
    own = (row >= at) & (row < at + 4)
    ahead = [lax.rem(k + 4 + j, across) for j in range(4)]
    coming = [spread(x, a) for a in ahead]
    down = [spread(y, k + j) for j in range(4)]
    hold[8] = x
    for j in range(4):
        hold[j] = cols[j]
        hold[4 + j] = coming[j]
    line = lambda j, i: jnp.broadcast_to(hold[j, at + i:at + i + 1], (SUB, size))
    a0, a1, a2 = line(0, 0), line(1, 0), line(1, 1)
    b00, b01, b10, b11 = line(0, 2), line(1, 2), line(0, 3), line(1, 3)
    c0, c1, c2 = line(2, 2), line(3, 2), line(3, 3)
    det = a0 * a2 - a1 * a1
    g00, g01 = b00 * a2 - b01 * a1, b01 * a0 - b00 * a1
    g10, g11 = b10 * a2 - b11 * a1, b11 * a0 - b10 * a1
    s0 = det * c0 - (g00 * b00 + g01 * b01)
    s1 = det * c1 - (g00 * b10 + g01 * b11)
    s2 = det * c2 - (g10 * b10 + g11 * b11)
    rs = reciprocal(s0 * s2 - s1 * s1)
    ra = reciprocal(det)

    def solve(e):
        t2 = det * e[2] - (g00 * e[0] + g01 * e[1])
        t3 = det * e[3] - (g10 * e[0] + g11 * e[1])
        w2 = (s2 * t2 - s1 * t3) * rs
        w3 = (s0 * t3 - s1 * t2) * rs
        w0 = ((a2 * e[0] - a1 * e[1]) - (g00 * w2 + g10 * w3)) * ra
        w1 = ((a0 * e[1] - a1 * e[0]) - (g01 * w2 + g11 * w3)) * ra
        return w0, w1, w2, w3

    less = lambda base, c, w: (base - (c[2] * w[2] + c[3] * w[3])) - (c[0] * w[0] + c[1] * w[1])
    cols = [jnp.where(own, jnp.where(row == at + j, -1.0, 0.0), cols[j]) for j in range(4)]
    there = [solve([line(4 + j, i) for i in range(4)]) for j in range(4)]
    if at + 4 < SUB:
        after = [less(jnp.where(own, 0.0, coming[j]), cols, there[j]) for j in range(4)]
    else:
        after = [less(spread(y, ahead[j]), down, there[j]) for j in range(4)]
    w = solve([jnp.where(inside, jnp.where(lane == k + j, 1.0, 0.0), line(8, j)) for j in range(4)])
    x = less(jnp.where(inside | own, 0.0, x), cols, w)
    y = less(jnp.where(inside, 0.0, y), down, w)
    return x, y, after


def invert(m, xt, w6, wide_w, hold):
    size = m.shape[0]
    lane = lax.broadcasted_iota(jnp.int32, (SUB, size), 1)
    row = lax.broadcasted_iota(jnp.int32, (SUB, size), 0)
    wide = lax.broadcasted_iota(jnp.int32, (size, size), 1)
    count = size // SUB

    def trail(t):
        k = t * SUB
        u = jnp.dot(xt[...], w6[...], preferred_element_type=F32)
        m[...] = jnp.where((wide >= k) & (wide < k + SUB), 0.0, m[...]) - u

    def step(t, carry):
        x, *cols = carry
        k = pl.multiple_of(t * SUB, SUB)
        before = k - SUB
        y = m[pl.ds(pl.multiple_of(lax.rem(t + 1, count) * SUB, SUB), SUB)]
        terms = [spread(y, jnp.maximum(before, 0) + j) * jnp.broadcast_to(wide_w[j:j + 1], (SUB, size)) for j in range(SUB)]
        y = jnp.where((lane >= before) & (lane < k), 0.0, y)
        y = y - (((terms[0] + terms[1]) + (terms[2] + terms[3])) + ((terms[4] + terms[5]) + (terms[6] + terms[7])))
        trail(t - 1)
        z = jnp.where(lane < k, -1.0, 1.0) * x
        z = jnp.where((lane >= k) & (lane < k + SUB), jnp.where(lane - k == row, -1.0, 0.0), z)
        h, n, l = parts(z)
        xt[...] = jnp.concatenate([h, h, n, n, h, l], axis=0).astype(BF16).T
        for g in range(0, SUB, 4):
            x, y, cols = four(x, y, cols, g, k + g, lane, row, hold.at[g // 4])
        h, n, l = parts(x)
        w6[...] = jnp.concatenate([h, n, h, n, l, h], axis=0).astype(BF16)
        wide_w[...] = x
        m[pl.ds(k, SUB)] = jnp.zeros((SUB, size), F32)
        return y, *cols

    xt[...] = jnp.zeros(xt.shape, BF16)
    w6[...] = jnp.zeros(w6.shape, BF16)
    wide_w[...] = jnp.zeros((SUB, size), F32)
    x = m[0:SUB]
    lax.fori_loop(0, count, step, (x, *(spread(x, j) for j in range(4))), unroll=2)
    trail(count - 1)


def invert_scratch(size):
    return [
        pltpu.VMEM((size, size), F32), pltpu.VMEM((size, 6 * SUB), BF16), pltpu.VMEM((6 * SUB, size), BF16),
        pltpu.VMEM((SUB, size), F32), pltpu.VMEM((SUB // 4, 9, SUB, size), F32),
    ]


def scaled_inverse(matrix, *work):
    size = matrix.shape[0]
    rows = lax.broadcasted_iota(jnp.int32, (size, size), 0)
    cols = lax.broadcasted_iota(jnp.int32, (size, size), 1)
    diagonal = jnp.where(rows == cols, matrix, 0.0)
    down = lax.rsqrt(jnp.sum(diagonal, axis=1, keepdims=True))
    across = lax.rsqrt(jnp.sum(diagonal, axis=0, keepdims=True))
    work[0][...] = matrix * down * across
    invert(*work)
    return work[0][...] * down * across


def basis_kernel(pieces, inverse_far, basis_far, order_far, top, low, basis_t, order, carried, gram, inverse, basis, sems):
    rows = inverse.shape[0] // pieces
    copies = [pltpu.make_async_copy(basis_far, basis, sems.at[pieces])]
    for i in range(pieces):
        part = pl.ds(i * rows, rows)
        copies.append(pltpu.make_async_copy(inverse_far.at[part], inverse.at[part], sems.at[i]))
    copies.append(pltpu.make_async_copy(order_far, order, sems.at[pieces + 1]))
    for copy in copies:
        copy.start()
    copies[0].wait()
    basis_parts = split(basis[...])
    across = basis[...].T
    basis_t[...] = across
    across = split(across)
    total = 0.0
    for i in range(pieces):
        part = slice(i * rows, (i + 1) * rows)
        copies[i + 1].wait()
        block = split(inverse[part])
        top[part], low[part] = block
        q = mm_parts(block, basis_parts)
        carried[part] = q
        total = total + mm_parts([x[:, part] for x in across], split(q))
    gram[...] = total
    copies[-1].wait()


def leaf_kernel(order, rhs, top, low, basis_t, solved, projected):
    points = rhs.shape[0]
    wide = 128
    numbers = order[...].astype(F32)
    lanes = lax.broadcasted_iota(jnp.int32, (wide, points), 1).astype(F32)
    gather = []
    for i in range(0, points, wide):
        column = jnp.broadcast_to(numbers[:, i:i + wide], (wide, wide)).T
        column = jnp.concatenate([column] * (points // wide), axis=1)
        gather.append(jnp.where(column == lanes, 1.0, 0.0).astype(BF16))
    ordered = pick(jnp.concatenate(gather, axis=0), rhs[...])
    z = mm_parts((top[...], low[...]), split(ordered))
    solved[...] = z
    projected[...] = mm(basis_t[...], z)


def place_kernel(order, solved, carried, solved_out, carried_out):
    points = solved.shape[0]
    rows = lax.broadcasted_iota(jnp.int32, (points, points), 0)
    scatter = jnp.where(order[...] == rows, 1.0, 0.0).astype(BF16)
    solved_out[...] = pick(scatter, solved[...])
    carried_out[...] = pick(scatter, carried[...])


def node_kernel(level, gram, other, precision, *rest):
    coupling = precision[0, level].astype(F32)
    whole = gram[...] + other[...]
    if len(rest) == 6:
        rest[0][...] = scaled_inverse(coupling + whole, *rest[1:])
        return
    transfer, inverse, mover, gram_out, *work = rest
    mixer = transfer[0, level]
    left = mm(mixer, precision[0, level], None, ((0,), (0,)))
    right = sum(mm(part.astype(BF16), mixer, None) for part in parts(whole))
    m = scaled_inverse(coupling + whole, *work)
    n = mm(left, m)
    inverse[...] = m
    mover[...] = n
    gram_out[...] = mm(n, right)


def lift_kernel(first, last, *refs):
    refs = list(refs)
    projected, other, inverse, mover = (ref[...] for ref in refs[:4])
    s = projected + other
    alpha = mm(inverse, s)
    projected_out, total_out, mixing_out = refs[-3:]
    projected_out[...] = mm(mover, s)
    if first:
        total, mixing = alpha, mover.T
    else:
        total, mixing = refs[4][...], refs[5][...]
        total = total + mm(mixing, alpha)
        mixing = mm(mixing, mover, HIGH, ((1,), (1,)))
    if last:
        solved, carried = refs[-5:-3]
        total = solved[...] - mm(carried[...], total)
        mixing = mm(carried[...], mixing)
    total_out[...] = total
    mixing_out[...] = mixing


def root_kernel(pieces, projected, other, inverse, solved, carried, out_far, out, sems):
    alpha = mm(inverse[...], projected[...] + other[...])
    rows = out.shape[0] // pieces
    copies = []
    for i in range(pieces):
        part = pl.ds(i * rows, rows)
        out[part] = solved[part] - mm(carried[part], alpha)
        copies.append(pltpu.make_async_copy(out.at[part], out_far.at[part], sems.at[i]))
        copies[-1].start()
    for copy in copies:
        copy.wait()


def call(kernel, outs, *args, scratch=(), work=0, place=VMEM, result=VMEM, after=()):
    if place is FAR:
        args = [pltpu.with_memory_space_constraint(arg, pltpu.HBM) for arg in args]
    return pl.pallas_call(
        lambda *refs: kernel(*refs[len(after):]),
        out_shape=[jax.ShapeDtypeStruct(getattr(out, "shape", out), getattr(out, "dtype", F32)) for out in outs],
        in_specs=[FAR] * len(after) + [place] * len(args),
        out_specs=[result] * len(outs),
        scratch_shapes=scratch,
        cost_estimate=pl.CostEstimate(flops=work, bytes_accessed=0, transcendentals=0),
        compiler_params=PARAMS,
    )(*after, *args)


def from_partner(block, axis, apart):
    count = lax.axis_size(axis)
    return lax.ppermute(block, axis, [(i, i ^ 1 << apart) for i in range(count)])


def body(rhs, order, inverse, basis, transfer, precision):
    points, columns = rhs.shape
    rank = basis.shape[1]
    square, tall, block = (rank, rank), (points, rank), (rank, columns)
    levels = lax.axis_size("leaf").bit_length() - 1
    pieces = 4
    half = jax.ShapeDtypeStruct(inverse.shape, BF16)
    top, low, basis_t, order, carried, gram = call(
        functools.partial(basis_kernel, pieces), [half, half, (rank, points), order, tall, square],
        inverse, basis, order, place=FAR, work=GIGA,
        scratch=[pltpu.VMEM(inverse.shape, F32), pltpu.VMEM(tall, F32), pltpu.SemaphoreType.DMA((pieces + 2,))]
    )
    other_gram = from_partner(gram, "leaf", 0)
    solved, projected = call(leaf_kernel, [rhs, block], order, rhs, top, low, basis_t, work=2 * GIGA)
    place = lambda *after: call(place_kernel, [rhs, tall], order, solved, carried, work=GIGA, after=after)
    if levels < 3:
        solved, carried = place()
    state, after = (), ()
    for k in range(levels - 1):
        other = from_partner(projected, "leaf", k)
        m, n, gram = call(
            functools.partial(node_kernel, k), [square] * 3, gram, other_gram, precision, transfer,
            scratch=invert_scratch(rank), work=6 * GIGA, after=after
        )
        other_gram = from_partner(gram, "leaf", k + 1)
        last = k == levels - 2
        projected, *state = call(
            functools.partial(lift_kernel, k == 0, last),
            [block, (points, columns), tall] if last else [block, block, square],
            projected, other, m, n, *state, *((solved, carried) if last else ()), work=GIGA
        )
        if k == 0 and not last:
            solved, carried = place(projected)
            after = (carried,)
    solved, carried = state or (solved, carried)
    k = levels - 1
    other = from_partner(projected, "leaf", k)
    (m,) = call(functools.partial(node_kernel, k), [square], gram, other_gram, precision, scratch=invert_scratch(rank), work=6 * GIGA)
    (out,) = call(
        functools.partial(root_kernel, pieces), [rhs], projected, other, m, solved, carried, work=GIGA, result=FAR,
        scratch=[pltpu.VMEM(rhs.shape, F32), pltpu.SemaphoreType.DMA((pieces,))]
    )
    return out


def solution(mesh):
    placed = (
        P("leaf", "rhs"),
        P("leaf", None),
        P("leaf", None),
        P("leaf", None),
        P("leaf", None, None, None),
        P("leaf", None, None, None),
    )
    return jax.shard_map(
        body, mesh=mesh, in_specs=placed, out_specs=P("leaf", "rhs"), check_vma=False
    )
```

```python
import functools

import jax
import jax.numpy as jnp
from jax import lax
from jax.experimental import pallas as pl
from jax.experimental.pallas import tpu as pltpu
from jax.sharding import PartitionSpec as P

F32 = jnp.float32
BF16 = jnp.bfloat16
HIGH = lax.Precision.HIGH
SUB = 8
GIGA = 10 ** 9
VMEM = pl.BlockSpec(memory_space=pltpu.VMEM)
FAR = pl.BlockSpec(memory_space=pltpu.HBM)
PARAMS = pltpu.CompilerParams(vmem_limit_bytes=32 * 1024 * 1024)


def mm(a, b, precision=HIGH, dims=((1,), (0,))):
    return lax.dot_general(a, b, (dims, ((), ())), precision=precision, preferred_element_type=F32)


def split(x):
    top = x.astype(BF16)
    return top, (x - top.astype(F32)).astype(BF16)


def mm_parts(a, b):
    columns = b[0].shape[1]
    both = jnp.dot(a[0], jnp.concatenate(b, axis=1), preferred_element_type=F32)
    return both[:, :columns] + (both[:, columns:] + jnp.dot(a[1], b[0], preferred_element_type=F32))


def pick(mask, x):
    top, low = split(x)
    one = lambda part: lax.dot_general(mask, part, (((1,), (0,)), ((), ())), preferred_element_type=F32)
    return one(top) + one(low)


def reciprocal(x):
    return pltpu.reciprocal(x, approx=True)

def parts(x):
    top = x.astype(BF16).astype(F32)
    rest = x - top
    mid = rest.astype(BF16).astype(F32)
    return top, mid, rest - mid

def spread(x, k):
    return jnp.broadcast_to(x[:, k:k + 1], x.shape)


def four(x, y, cols, at, k, lane, row, hold):
    size = x.shape[1]
    across = size // SUB * SUB
    inside = (lane >= k) & (lane < k + 4)
    own = (row >= at) & (row < at + 4)
    ahead = [(k + 4 + j) % across for j in range(4)]
    coming = [spread(x, a) for a in ahead]
    down = [spread(y, k + j) for j in range(4)]
    hold[8] = x
    for j in range(4):
        hold[j] = cols[j]
        hold[4 + j] = coming[j]
    line = lambda j, i: jnp.broadcast_to(hold[j, at + i:at + i + 1], (SUB, size))
    a0, a1, a2 = line(0, 0), line(1, 0), line(1, 1)
    b00, b01, b10, b11 = line(0, 2), line(1, 2), line(0, 3), line(1, 3)
    c0, c1, c2 = line(2, 2), line(3, 2), line(3, 3)
    det = a0 * a2 - a1 * a1
    g00, g01 = b00 * a2 - b01 * a1, b01 * a0 - b00 * a1
    g10, g11 = b10 * a2 - b11 * a1, b11 * a0 - b10 * a1
    s0 = det * c0 - (g00 * b00 + g01 * b01)
    s1 = det * c1 - (g00 * b10 + g01 * b11)
    s2 = det * c2 - (g10 * b10 + g11 * b11)
    rs = reciprocal(s0 * s2 - s1 * s1)
    ra = reciprocal(det)

    def solve(e):
        t2 = det * e[2] - (g00 * e[0] + g01 * e[1])
        t3 = det * e[3] - (g10 * e[0] + g11 * e[1])
        w2 = (s2 * t2 - s1 * t3) * rs
        w3 = (s0 * t3 - s1 * t2) * rs
        w0 = ((a2 * e[0] - a1 * e[1]) - (g00 * w2 + g10 * w3)) * ra
        w1 = ((a0 * e[1] - a1 * e[0]) - (g01 * w2 + g11 * w3)) * ra
        return w0, w1, w2, w3

    less = lambda base, c, w: (base - (c[2] * w[2] + c[3] * w[3])) - (c[0] * w[0] + c[1] * w[1])
    cols = [jnp.where(own, jnp.where(row == at + j, -1.0, 0.0), cols[j]) for j in range(4)]
    there = [solve([line(4 + j, i) for i in range(4)]) for j in range(4)]
    if at + 4 < SUB:
        after = [less(jnp.where(own, 0.0, coming[j]), cols, there[j]) for j in range(4)]
    else:
        after = [less(spread(y, ahead[j]), down, there[j]) for j in range(4)]
    w = solve([jnp.where(inside, jnp.where(lane == k + j, 1.0, 0.0), line(8, j)) for j in range(4)])
    x = less(jnp.where(inside | own, 0.0, x), cols, w)
    y = less(jnp.where(inside, 0.0, y), down, w)
    return x, y, after


def invert(m, xt, w6, wide_w, hold):
    size = m.shape[0]
    lane = lax.broadcasted_iota(jnp.int32, (SUB, size), 1)
    row = lax.broadcasted_iota(jnp.int32, (SUB, size), 0)
    wide = lax.broadcasted_iota(jnp.int32, (size, size), 1)
    count = size // SUB

    def trail(t):
        k = t * SUB
        u = jnp.dot(xt[...], w6[...], preferred_element_type=F32)
        m[...] = jnp.where((wide >= k) & (wide < k + SUB), 0.0, m[...]) - u

    def step(t, carry):
        x, *cols = carry
        k = t * SUB
        before = k - SUB
        y = m[pl.ds((t + 1) % count * SUB, SUB)]
        terms = [spread(y, max(before, 0) + j) * jnp.broadcast_to(wide_w[j:j + 1], (SUB, size)) for j in range(SUB)]
        y = jnp.where((lane >= before) & (lane < k), 0.0, y)
        y = y - (((terms[0] + terms[1]) + (terms[2] + terms[3])) + ((terms[4] + terms[5]) + (terms[6] + terms[7])))
        trail(t - 1)
        z = jnp.where(lane < k, -1.0, 1.0) * x
        z = jnp.where((lane >= k) & (lane < k + SUB), jnp.where(lane - k == row, -1.0, 0.0), z)
        h, n, l = parts(z)
        xt[...] = jnp.concatenate([h, h, n, n, h, l], axis=0).astype(BF16).T
        for g in range(0, SUB, 4):
            x, y, cols = four(x, y, cols, g, k + g, lane, row, hold.at[g // 4])
        h, n, l = parts(x)
        w6[...] = jnp.concatenate([h, n, h, n, l, h], axis=0).astype(BF16)
        wide_w[...] = x
        m[pl.ds(k, SUB)] = jnp.zeros((SUB, size), F32)
        return y, *cols

    xt[...] = jnp.zeros(xt.shape, BF16)
    w6[...] = jnp.zeros(w6.shape, BF16)
    wide_w[...] = jnp.zeros((SUB, size), F32)
    x = m[0:SUB]
    carry = (x, *(spread(x, j) for j in range(4)))
    for t in range(count):
        carry = step(t, carry)
    trail(count - 1)


def invert_scratch(size):
    return [
        pltpu.VMEM((size, size), F32), pltpu.VMEM((size, 6 * SUB), BF16), pltpu.VMEM((6 * SUB, size), BF16),
        pltpu.VMEM((SUB, size), F32), pltpu.VMEM((SUB // 4, 9, SUB, size), F32),
    ]


def scaled_inverse(matrix, *work):
    size = matrix.shape[0]
    rows = lax.broadcasted_iota(jnp.int32, (size, size), 0)
    cols = lax.broadcasted_iota(jnp.int32, (size, size), 1)
    diagonal = jnp.where(rows == cols, matrix, 0.0)
    down = lax.rsqrt(jnp.sum(diagonal, axis=1, keepdims=True))
    across = lax.rsqrt(jnp.sum(diagonal, axis=0, keepdims=True))
    work[0][...] = matrix * down * across
    invert(*work)
    return work[0][...] * down * across


def basis_kernel(pieces, inverse_far, basis_far, order_far, top, low, basis_t, order, carried, gram, inverse, basis, sems):
    rows = inverse.shape[0] // pieces
    copies = [pltpu.make_async_copy(basis_far, basis, sems.at[pieces])]
    for i in range(pieces):
        part = pl.ds(i * rows, rows)
        copies.append(pltpu.make_async_copy(inverse_far.at[part], inverse.at[part], sems.at[i]))
    copies.append(pltpu.make_async_copy(order_far, order, sems.at[pieces + 1]))
    for copy in copies:
        copy.start()
    copies[0].wait()
    basis_parts = split(basis[...])
    across = basis[...].T
    basis_t[...] = across
    across = split(across)
    for i in range(pieces):
        part = slice(i * rows, (i + 1) * rows)
        copies[i + 1].wait()
        block = split(inverse[part])
        top[part], low[part] = block
        carried[part] = mm_parts(block, basis_parts)
    gram[...] = mm_parts(across, split(carried[...]))
    copies[-1].wait()


def leaf_kernel(order, rhs, top, low, basis_t, solved, projected):
    points = rhs.shape[0]
    wide = 128
    numbers = order[...].astype(F32)
    lanes = lax.broadcasted_iota(jnp.int32, (wide, points), 1).astype(F32)
    gather = []
    for i in range(0, points, wide):
        column = jnp.broadcast_to(numbers[:, i:i + wide], (wide, wide)).T
        column = jnp.concatenate([column] * (points // wide), axis=1)
        gather.append(jnp.where(column == lanes, 1.0, 0.0).astype(BF16))
    ordered = pick(jnp.concatenate(gather, axis=0), rhs[...])
    z = mm_parts((top[...], low[...]), split(ordered))
    solved[...] = z
    projected[...] = mm(basis_t[...], z)


def place_kernel(order, solved, carried, solved_out, carried_out):
    points = solved.shape[0]
    rows = lax.broadcasted_iota(jnp.int32, (points, points), 0)
    scatter = jnp.where(order[...] == rows, 1.0, 0.0).astype(BF16)
    solved_out[...] = pick(scatter, solved[...])
    carried_out[...] = pick(scatter, carried[...])


def node_kernel(level, gram, other, precision, *rest):
    coupling = precision[0, level].astype(F32)
    whole = gram[...] + other[...]
    if len(rest) == 6:
        rest[0][...] = scaled_inverse(coupling + whole, *rest[1:])
        return
    transfer, inverse, mover, gram_out, *work = rest
    mixer = transfer[0, level]
    left = mm(mixer, precision[0, level], None, ((0,), (0,)))
    right = sum(mm(part.astype(BF16), mixer, None) for part in parts(whole))
    m = scaled_inverse(coupling + whole, *work)
    n = mm(left, m)
    inverse[...] = m
    mover[...] = n
    gram_out[...] = mm(n, right)


def lift_kernel(first, last, *refs):
    refs = list(refs)
    projected, other, inverse, mover = (ref[...] for ref in refs[:4])
    s = projected + other
    alpha = mm(inverse, s)
    projected_out, total_out, mixing_out = refs[-3:]
    projected_out[...] = mm(mover, s)
    if first:
        total, mixing = alpha, mover.T
    else:
        total, mixing = refs[4][...], refs[5][...]
        total = total + mm(mixing, alpha)
        mixing = mm(mixing, mover, HIGH, ((1,), (1,)))
    if last:
        solved, carried = refs[-5:-3]
        total = solved[...] - mm(carried[...], total)
        mixing = mm(carried[...], mixing)
    total_out[...] = total
    mixing_out[...] = mixing


def root_kernel(pieces, projected, other, inverse, solved, carried, out_far, out, sems):
    alpha = mm(inverse[...], projected[...] + other[...])
    rows = out.shape[0] // pieces
    copies = []
    for i in range(pieces):
        part = pl.ds(i * rows, rows)
        out[part] = solved[part] - mm(carried[part], alpha)
        copies.append(pltpu.make_async_copy(out.at[part], out_far.at[part], sems.at[i]))
        copies[-1].start()
    for copy in copies:
        copy.wait()


def call(kernel, outs, *args, scratch=(), work=0, place=VMEM, result=VMEM, after=()):
    if place is FAR:
        args = [pltpu.with_memory_space_constraint(arg, pltpu.HBM) for arg in args]
    return pl.pallas_call(
        lambda *refs: kernel(*refs[len(after):]),
        out_shape=[jax.ShapeDtypeStruct(getattr(out, "shape", out), getattr(out, "dtype", F32)) for out in outs],
        in_specs=[FAR] * len(after) + [place] * len(args),
        out_specs=[result] * len(outs),
        scratch_shapes=scratch,
        cost_estimate=pl.CostEstimate(flops=work, bytes_accessed=0, transcendentals=0),
        compiler_params=PARAMS,
    )(*after, *args)


def from_partner(block, axis, apart):
    count = lax.axis_size(axis)
    return lax.ppermute(block, axis, [(i, i ^ 1 << apart) for i in range(count)])


def body(rhs, order, inverse, basis, transfer, precision):
    points, columns = rhs.shape
    rank = basis.shape[1]
    square, tall, block = (rank, rank), (points, rank), (rank, columns)
    levels = lax.axis_size("leaf").bit_length() - 1
    pieces = 2
    half = jax.ShapeDtypeStruct(inverse.shape, BF16)
    top, low, basis_t, order, carried, gram = call(
        functools.partial(basis_kernel, pieces), [half, half, (rank, points), order, tall, square],
        inverse, basis, order, place=FAR, work=GIGA,
        scratch=[pltpu.VMEM(inverse.shape, F32), pltpu.VMEM(tall, F32), pltpu.SemaphoreType.DMA((pieces + 2,))]
    )
    other_gram = from_partner(gram, "leaf", 0)
    solved, projected = call(leaf_kernel, [rhs, block], order, rhs, top, low, basis_t, work=2 * GIGA)
    place = lambda *after: call(place_kernel, [rhs, tall], order, solved, carried, work=GIGA, after=after)
    if levels < 3:
        solved, carried = place()
    state, after = (), ()
    for k in range(levels - 1):
        other = from_partner(projected, "leaf", k)
        m, n, gram = call(
            functools.partial(node_kernel, k), [square] * 3, gram, other_gram, precision, transfer,
            scratch=invert_scratch(rank), work=6 * GIGA, after=after
        )
        other_gram = from_partner(gram, "leaf", k + 1)
        last = k == levels - 2
        projected, *state = call(
            functools.partial(lift_kernel, k == 0, last),
            [block, (points, columns), tall] if last else [block, block, square],
            projected, other, m, n, *state, *((solved, carried) if last else ()), work=GIGA
        )
        if k == 0 and not last:
            solved, carried = place(projected)
            after = (carried,)
    solved, carried = state or (solved, carried)
    k = levels - 1
    other = from_partner(projected, "leaf", k)
    (m,) = call(functools.partial(node_kernel, k), [square], gram, other_gram, precision, scratch=invert_scratch(rank), work=6 * GIGA)
    (out,) = call(
        functools.partial(root_kernel, pieces), [rhs], projected, other, m, solved, carried, work=GIGA, result=FAR,
        scratch=[pltpu.VMEM(rhs.shape, F32), pltpu.SemaphoreType.DMA((pieces,))]
    )
    return out


def solution(mesh):
    placed = (
        P("leaf", "rhs"),
        P("leaf", None),
        P("leaf", None),
        P("leaf", None),
        P("leaf", None, None, None),
        P("leaf", None, None, None),
    )
    return jax.shard_map(
        body, mesh=mesh, in_specs=placed, out_specs=P("leaf", "rhs"), check_vma=False
    )
```

```python
import functools

import jax
import jax.numpy as jnp
from jax import lax
from jax.experimental import pallas as pl
from jax.experimental.pallas import tpu as pltpu
from jax.sharding import PartitionSpec as P

F32 = jnp.float32
BF16 = jnp.bfloat16
HIGH = lax.Precision.HIGH
SUB = 8
GIGA = 10 ** 9
VMEM = pl.BlockSpec(memory_space=pltpu.VMEM)
FAR = pl.BlockSpec(memory_space=pltpu.HBM)
PARAMS = pltpu.CompilerParams(vmem_limit_bytes=32 * 1024 * 1024)


def mm(a, b, precision=HIGH, dims=((1,), (0,))):
    return lax.dot_general(a, b, (dims, ((), ())), precision=precision, preferred_element_type=F32)


def split(x):
    top = x.astype(BF16)
    return top, (x - top.astype(F32)).astype(BF16)


def mm_parts(a, b):
    columns = b[0].shape[1]
    both = jnp.dot(a[0], jnp.concatenate(b, axis=1), preferred_element_type=F32)
    return both[:, :columns] + (both[:, columns:] + jnp.dot(a[1], b[0], preferred_element_type=F32))


def pick(mask, x):
    top, low = split(x)
    one = lambda part: lax.dot_general(mask, part, (((1,), (0,)), ((), ())), preferred_element_type=F32)
    return one(top) + one(low)


def reciprocal(x):
    return pltpu.reciprocal(x, approx=True)

def parts(x):
    top = x.astype(BF16).astype(F32)
    rest = x - top
    mid = rest.astype(BF16).astype(F32)
    return top, mid, rest - mid

def spread(x, k):
    return jnp.broadcast_to(x[:, k:k + 1], x.shape)


def four(x, y, cols, at, k, lane, row, hold):
    size = x.shape[1]
    across = size // SUB * SUB
    inside = (lane >= k) & (lane < k + 4)
    own = (row >= at) & (row < at + 4)
    ahead = [(k + 4 + j) % across for j in range(4)]
    coming = [spread(x, a) for a in ahead]
    down = [spread(y, k + j) for j in range(4)]
    hold[8] = x
    for j in range(4):
        hold[j] = cols[j]
        hold[4 + j] = coming[j]
    line = lambda j, i: jnp.broadcast_to(hold[j, at + i:at + i + 1], (SUB, size))
    a0, a1, a2 = line(0, 0), line(1, 0), line(1, 1)
    b00, b01, b10, b11 = line(0, 2), line(1, 2), line(0, 3), line(1, 3)
    c0, c1, c2 = line(2, 2), line(3, 2), line(3, 3)
    det = a0 * a2 - a1 * a1
    g00, g01 = b00 * a2 - b01 * a1, b01 * a0 - b00 * a1
    g10, g11 = b10 * a2 - b11 * a1, b11 * a0 - b10 * a1
    s0 = det * c0 - (g00 * b00 + g01 * b01)
    s1 = det * c1 - (g00 * b10 + g01 * b11)
    s2 = det * c2 - (g10 * b10 + g11 * b11)
    rs = reciprocal(s0 * s2 - s1 * s1)
    ra = reciprocal(det)

    def known(e):
        t2 = det * e[2] - (g00 * e[0] + g01 * e[1])
        t3 = det * e[3] - (g10 * e[0] + g11 * e[1])
        return a2 * e[0] - a1 * e[1], a0 * e[1] - a1 * e[0], s2 * t2 - s1 * t3, s0 * t3 - s1 * t2

    def second(c):
        return c[0], c[1], c[2] - (c[0] * g00 + c[1] * g01) * ra, c[3] - (c[0] * g10 + c[1] * g11) * ra

    def less(base, c, v):
        return (base - (c[0] * v[0] + c[1] * v[1]) * ra) - (c[2] * v[2] + c[3] * v[3]) * rs

    cols = second([jnp.where(own, jnp.where(row == at + j, -1.0, 0.0), cols[j]) for j in range(4)])
    down = second(down)
    there = [known([line(4 + j, i) for i in range(4)]) for j in range(4)]
    if at + 4 < SUB:
        after = [less(jnp.where(own, 0.0, coming[j]), cols, there[j]) for j in range(4)]
    else:
        after = [less(spread(y, ahead[j]), down, there[j]) for j in range(4)]
    here = known([jnp.where(inside, jnp.where(lane == k + j, 1.0, 0.0), line(8, j)) for j in range(4)])
    x = less(jnp.where(inside | own, 0.0, x), cols, here)
    y = less(jnp.where(inside, 0.0, y), down, here)
    return x, y, after


def invert(m, xt, w6, wide_w, hold):
    size = m.shape[0]
    lane = lax.broadcasted_iota(jnp.int32, (SUB, size), 1)
    row = lax.broadcasted_iota(jnp.int32, (SUB, size), 0)
    wide = lax.broadcasted_iota(jnp.int32, (size, size), 1)
    count = size // SUB

    def trail(t):
        k = t * SUB
        u = jnp.dot(xt[...], w6[...], preferred_element_type=F32)
        m[...] = jnp.where((wide >= k) & (wide < k + SUB), 0.0, m[...]) - u

    def step(t, carry):
        x, *cols = carry
        k = t * SUB
        before = k - SUB
        y = m[pl.ds((t + 1) % count * SUB, SUB)]
        terms = [spread(y, max(before, 0) + j) * jnp.broadcast_to(wide_w[j:j + 1], (SUB, size)) for j in range(SUB)]
        y = jnp.where((lane >= before) & (lane < k), 0.0, y)
        y = y - (((terms[0] + terms[1]) + (terms[2] + terms[3])) + ((terms[4] + terms[5]) + (terms[6] + terms[7])))
        trail(t - 1)
        z = jnp.where(lane < k, -1.0, 1.0) * x
        z = jnp.where((lane >= k) & (lane < k + SUB), jnp.where(lane - k == row, -1.0, 0.0), z)
        h, n, l = parts(z)
        xt[...] = jnp.concatenate([h, h, n, n, h, l], axis=0).astype(BF16).T
        for g in range(0, SUB, 4):
            x, y, cols = four(x, y, cols, g, k + g, lane, row, hold.at[g // 4])
        h, n, l = parts(x)
        w6[...] = jnp.concatenate([h, n, h, n, l, h], axis=0).astype(BF16)
        wide_w[...] = x
        m[pl.ds(k, SUB)] = jnp.zeros((SUB, size), F32)
        return y, *cols

    xt[...] = jnp.zeros(xt.shape, BF16)
    w6[...] = jnp.zeros(w6.shape, BF16)
    wide_w[...] = jnp.zeros((SUB, size), F32)
    x = m[0:SUB]
    carry = (x, *(spread(x, j) for j in range(4)))
    for t in range(count):
        carry = step(t, carry)
    trail(count - 1)


def invert_scratch(size):
    return [
        pltpu.VMEM((size, size), F32), pltpu.VMEM((size, 6 * SUB), BF16), pltpu.VMEM((6 * SUB, size), BF16),
        pltpu.VMEM((SUB, size), F32), pltpu.VMEM((SUB // 4, 9, SUB, size), F32),
    ]


def scaled_inverse(matrix, *work):
    size = matrix.shape[0]
    rows = lax.broadcasted_iota(jnp.int32, (size, size), 0)
    cols = lax.broadcasted_iota(jnp.int32, (size, size), 1)
    diagonal = jnp.where(rows == cols, matrix, 0.0)
    down = lax.rsqrt(jnp.sum(diagonal, axis=1, keepdims=True))
    across = lax.rsqrt(jnp.sum(diagonal, axis=0, keepdims=True))
    work[0][...] = matrix * down * across
    invert(*work)
    return work[0][...] * down * across


def basis_kernel(pieces, inverse_far, basis_far, order_far, top, low, basis_t, order, carried, gram, inverse, basis, sems):
    rows = inverse.shape[0] // pieces
    copies = [pltpu.make_async_copy(basis_far, basis, sems.at[pieces])]
    for i in range(pieces):
        part = pl.ds(i * rows, rows)
        copies.append(pltpu.make_async_copy(inverse_far.at[part], inverse.at[part], sems.at[i]))
    copies.append(pltpu.make_async_copy(order_far, order, sems.at[pieces + 1]))
    for copy in copies:
        copy.start()
    copies[0].wait()
    basis_parts = split(basis[...])
    across = basis[...].T
    basis_t[...] = across
    across = split(across)
    for i in range(pieces):
        part = slice(i * rows, (i + 1) * rows)
        copies[i + 1].wait()
        block = split(inverse[part])
        top[part], low[part] = block
        carried[part] = mm_parts(block, basis_parts)
    gram[...] = mm_parts(across, split(carried[...]))
    copies[-1].wait()


def leaf_kernel(order, rhs, top, low, basis_t, solved, projected):
    points = rhs.shape[0]
    wide = 128
    numbers = order[...].astype(F32)
    lanes = lax.broadcasted_iota(jnp.int32, (wide, points), 1).astype(F32)
    gather = []
    for i in range(0, points, wide):
        column = jnp.broadcast_to(numbers[:, i:i + wide], (wide, wide)).T
        column = jnp.concatenate([column] * (points // wide), axis=1)
        gather.append(jnp.where(column == lanes, 1.0, 0.0).astype(BF16))
    ordered = pick(jnp.concatenate(gather, axis=0), rhs[...])
    z = mm_parts((top[...], low[...]), split(ordered))
    solved[...] = z
    projected[...] = mm(basis_t[...], z)


def place_kernel(order, solved, carried, solved_out, carried_out):
    points = solved.shape[0]
    rows = lax.broadcasted_iota(jnp.int32, (points, points), 0)
    scatter = jnp.where(order[...] == rows, 1.0, 0.0).astype(BF16)
    solved_out[...] = pick(scatter, solved[...])
    carried_out[...] = pick(scatter, carried[...])


def node_kernel(level, gram, other, precision, *rest):
    coupling = precision[0, level].astype(F32)
    whole = gram[...] + other[...]
    if len(rest) == 6:
        rest[0][...] = scaled_inverse(coupling + whole, *rest[1:])
        return
    transfer, inverse, mover, gram_out, *work = rest
    mixer = transfer[0, level]
    left = mm(mixer, precision[0, level], None, ((0,), (0,)))
    right = sum(mm(part.astype(BF16), mixer, None) for part in parts(whole))
    m = scaled_inverse(coupling + whole, *work)
    n = mm(left, m)
    inverse[...] = m
    mover[...] = n
    gram_out[...] = mm(n, right)


def lift_kernel(first, last, *refs):
    refs = list(refs)
    projected, other, inverse, mover = (ref[...] for ref in refs[:4])
    s = projected + other
    alpha = mm(inverse, s)
    projected_out, total_out, mixing_out = refs[-3:]
    projected_out[...] = mm(mover, s)
    if first:
        total, mixing = alpha, mover.T
    else:
        total, mixing = refs[4][...], refs[5][...]
        total = total + mm(mixing, alpha)
        mixing = mm(mixing, mover, HIGH, ((1,), (1,)))
    if last:
        solved, carried = refs[-5:-3]
        total = solved[...] - mm(carried[...], total)
        mixing = mm(carried[...], mixing)
    total_out[...] = total
    mixing_out[...] = mixing


def root_kernel(pieces, projected, other, inverse, solved, carried, out_far, out, sems):
    alpha = mm(inverse[...], projected[...] + other[...])
    rows = out.shape[0] // pieces
    copies = []
    for i in range(pieces):
        part = pl.ds(i * rows, rows)
        out[part] = solved[part] - mm(carried[part], alpha)
        copies.append(pltpu.make_async_copy(out.at[part], out_far.at[part], sems.at[i]))
        copies[-1].start()
    for copy in copies:
        copy.wait()


def call(kernel, outs, *args, scratch=(), work=0, place=VMEM, result=VMEM, after=()):
    if place is FAR:
        args = [pltpu.with_memory_space_constraint(arg, pltpu.HBM) for arg in args]
    return pl.pallas_call(
        lambda *refs: kernel(*refs[len(after):]),
        out_shape=[jax.ShapeDtypeStruct(getattr(out, "shape", out), getattr(out, "dtype", F32)) for out in outs],
        in_specs=[FAR] * len(after) + [place] * len(args),
        out_specs=[result] * len(outs),
        scratch_shapes=scratch,
        cost_estimate=pl.CostEstimate(flops=work, bytes_accessed=0, transcendentals=0),
        compiler_params=PARAMS,
    )(*after, *args)


def from_partner(block, axis, apart):
    count = lax.axis_size(axis)
    return lax.ppermute(block, axis, [(i, i ^ 1 << apart) for i in range(count)])


def body(rhs, order, inverse, basis, transfer, precision):
    points, columns = rhs.shape
    rank = basis.shape[1]
    square, tall, block = (rank, rank), (points, rank), (rank, columns)
    levels = lax.axis_size("leaf").bit_length() - 1
    pieces = 2
    half = jax.ShapeDtypeStruct(inverse.shape, BF16)
    top, low, basis_t, order, carried, gram = call(
        functools.partial(basis_kernel, pieces), [half, half, (rank, points), order, tall, square],
        inverse, basis, order, place=FAR, work=GIGA,
        scratch=[pltpu.VMEM(inverse.shape, F32), pltpu.VMEM(tall, F32), pltpu.SemaphoreType.DMA((pieces + 2,))]
    )
    other_gram = from_partner(gram, "leaf", 0)
    solved, projected = call(leaf_kernel, [rhs, block], order, rhs, top, low, basis_t, work=2 * GIGA)
    place = lambda *after: call(place_kernel, [rhs, tall], order, solved, carried, work=GIGA, after=after)
    if levels < 3:
        solved, carried = place()
    state, after = (), ()
    for k in range(levels - 1):
        other = from_partner(projected, "leaf", k)
        m, n, gram = call(
            functools.partial(node_kernel, k), [square] * 3, gram, other_gram, precision, transfer,
            scratch=invert_scratch(rank), work=6 * GIGA, after=after
        )
        other_gram = from_partner(gram, "leaf", k + 1)
        last = k == levels - 2
        projected, *state = call(
            functools.partial(lift_kernel, k == 0, last),
            [block, (points, columns), tall] if last else [block, block, square],
            projected, other, m, n, *state, *((solved, carried) if last else ()), work=GIGA
        )
        if k == 0 and not last:
            solved, carried = place(projected)
            after = (carried,)
    solved, carried = state or (solved, carried)
    k = levels - 1
    other = from_partner(projected, "leaf", k)
    (m,) = call(functools.partial(node_kernel, k), [square], gram, other_gram, precision, scratch=invert_scratch(rank), work=6 * GIGA)
    (out,) = call(
        functools.partial(root_kernel, pieces), [rhs], projected, other, m, solved, carried, work=GIGA, result=FAR,
        scratch=[pltpu.VMEM(rhs.shape, F32), pltpu.SemaphoreType.DMA((pieces,))]
    )
    return out


def solution(mesh):
    placed = (
        P("leaf", "rhs"),
        P("leaf", None),
        P("leaf", None),
        P("leaf", None),
        P("leaf", None, None, None),
        P("leaf", None, None, None),
    )
    return jax.shard_map(
        body, mesh=mesh, in_specs=placed, out_specs=P("leaf", "rhs"), check_vma=False
    )
```

```python
import functools

import jax
import jax.numpy as jnp
from jax import lax
from jax.experimental import pallas as pl
from jax.experimental.pallas import tpu as pltpu
from jax.sharding import PartitionSpec as P

F32 = jnp.float32
BF16 = jnp.bfloat16
HIGH = lax.Precision.HIGH
SUB = 8
GIGA = 10 ** 9
VMEM = pl.BlockSpec(memory_space=pltpu.VMEM)
FAR = pl.BlockSpec(memory_space=pltpu.HBM)
PARAMS = pltpu.CompilerParams(vmem_limit_bytes=32 * 1024 * 1024)


def mm(a, b, precision=HIGH, dims=((1,), (0,))):
    return lax.dot_general(a, b, (dims, ((), ())), precision=precision, preferred_element_type=F32)


def split(x):
    top = x.astype(BF16)
    return top, (x - top.astype(F32)).astype(BF16)


def mm_parts(a, b):
    columns = b[0].shape[1]
    both = jnp.dot(a[0], jnp.concatenate(b, axis=1), preferred_element_type=F32)
    return both[:, :columns] + (both[:, columns:] + jnp.dot(a[1], b[0], preferred_element_type=F32))


def pick(mask, x):
    top, low = split(x)
    one = lambda part: lax.dot_general(mask, part, (((1,), (0,)), ((), ())), preferred_element_type=F32)
    return one(top) + one(low)


def reciprocal(x):
    return pltpu.reciprocal(x, approx=True)

def parts(x):
    top = x.astype(BF16).astype(F32)
    rest = x - top
    mid = rest.astype(BF16).astype(F32)
    return top, mid, rest - mid

def spread(x, k):
    return jnp.broadcast_to(x[:, k:k + 1], x.shape)


def four(x, y, cols, at, k, lane, row):
    size = x.shape[1]
    across = size // SUB * SUB
    inside = (lane >= k) & (lane < k + 4)
    own = (row >= at) & (row < at + 4)
    ahead = [(k + 4 + j) % across for j in range(4)]
    coming = [spread(x, a) for a in ahead]
    down = [spread(y, k + j) for j in range(4)]
    tiles = [*cols, *coming, x]
    line = lambda j, i: jnp.broadcast_to(tiles[j][at + i:at + i + 1], (SUB, size))
    a0, a1, a2 = line(0, 0), line(1, 0), line(1, 1)
    b00, b01, b10, b11 = line(0, 2), line(1, 2), line(0, 3), line(1, 3)
    c0, c1, c2 = line(2, 2), line(3, 2), line(3, 3)
    det = a0 * a2 - a1 * a1
    g00, g01 = b00 * a2 - b01 * a1, b01 * a0 - b00 * a1
    g10, g11 = b10 * a2 - b11 * a1, b11 * a0 - b10 * a1
    s0 = det * c0 - (g00 * b00 + g01 * b01)
    s1 = det * c1 - (g00 * b10 + g01 * b11)
    s2 = det * c2 - (g10 * b10 + g11 * b11)
    rs = reciprocal(s0 * s2 - s1 * s1)
    ra = reciprocal(det)

    def known(e):
        t2 = det * e[2] - (g00 * e[0] + g01 * e[1])
        t3 = det * e[3] - (g10 * e[0] + g11 * e[1])
        return a2 * e[0] - a1 * e[1], a0 * e[1] - a1 * e[0], s2 * t2 - s1 * t3, s0 * t3 - s1 * t2

    def second(c):
        return c[0], c[1], c[2] - (c[0] * g00 + c[1] * g01) * ra, c[3] - (c[0] * g10 + c[1] * g11) * ra

    def less(base, c, v):
        return (base - (c[0] * v[0] + c[1] * v[1]) * ra) - (c[2] * v[2] + c[3] * v[3]) * rs

    cols = second([jnp.where(own, jnp.where(row == at + j, -1.0, 0.0), cols[j]) for j in range(4)])
    down = second(down)
    there = [known([line(4 + j, i) for i in range(4)]) for j in range(4)]
    if at + 4 < SUB:
        after = [less(jnp.where(own, 0.0, coming[j]), cols, there[j]) for j in range(4)]
    else:
        after = [less(spread(y, ahead[j]), down, there[j]) for j in range(4)]
    here = known([jnp.where(inside, jnp.where(lane == k + j, 1.0, 0.0), line(8, j)) for j in range(4)])
    x = less(jnp.where(inside | own, 0.0, x), cols, here)
    y = less(jnp.where(inside, 0.0, y), down, here)
    return x, y, after


def invert(m, xt, w6, wide_w):
    size = m.shape[0]
    lane = lax.broadcasted_iota(jnp.int32, (SUB, size), 1)
    row = lax.broadcasted_iota(jnp.int32, (SUB, size), 0)
    wide = lax.broadcasted_iota(jnp.int32, (size, size), 1)
    count = size // SUB

    def trail(t):
        k = t * SUB
        u = jnp.dot(xt[...], w6[...], preferred_element_type=F32)
        m[...] = jnp.where((wide >= k) & (wide < k + SUB), 0.0, m[...]) - u

    def step(t, carry):
        x, *cols = carry
        k = t * SUB
        before = k - SUB
        y = m[pl.ds((t + 1) % count * SUB, SUB)]
        terms = [spread(y, max(before, 0) + j) * jnp.broadcast_to(wide_w[j:j + 1], (SUB, size)) for j in range(SUB)]
        y = jnp.where((lane >= before) & (lane < k), 0.0, y)
        y = y - (((terms[0] + terms[1]) + (terms[2] + terms[3])) + ((terms[4] + terms[5]) + (terms[6] + terms[7])))
        trail(t - 1)
        z = jnp.where(lane < k, -1.0, 1.0) * x
        z = jnp.where((lane >= k) & (lane < k + SUB), jnp.where(lane - k == row, -1.0, 0.0), z)
        h, n, l = parts(z)
        xt[...] = jnp.concatenate([h, h, n, n, h, l], axis=0).astype(BF16).T
        for g in range(0, SUB, 4):
            x, y, cols = four(x, y, cols, g, k + g, lane, row)
        h, n, l = parts(x)
        w6[...] = jnp.concatenate([h, n, h, n, l, h], axis=0).astype(BF16)
        wide_w[...] = x
        m[pl.ds(k, SUB)] = jnp.zeros((SUB, size), F32)
        return y, *cols

    xt[...] = jnp.zeros(xt.shape, BF16)
    w6[...] = jnp.zeros(w6.shape, BF16)
    wide_w[...] = jnp.zeros((SUB, size), F32)
    x = m[0:SUB]
    carry = (x, *(spread(x, j) for j in range(4)))
    for t in range(count):
        carry = step(t, carry)
    trail(count - 1)


def invert_scratch(size):
    return [
        pltpu.VMEM((size, size), F32), pltpu.VMEM((size, 6 * SUB), BF16), pltpu.VMEM((6 * SUB, size), BF16),
        pltpu.VMEM((SUB, size), F32),
    ]


def scaled_inverse(matrix, *work):
    size = matrix.shape[0]
    rows = lax.broadcasted_iota(jnp.int32, (size, size), 0)
    cols = lax.broadcasted_iota(jnp.int32, (size, size), 1)
    diagonal = jnp.where(rows == cols, matrix, 0.0)
    down = lax.rsqrt(jnp.sum(diagonal, axis=1, keepdims=True))
    across = lax.rsqrt(jnp.sum(diagonal, axis=0, keepdims=True))
    work[0][...] = matrix * down * across
    invert(*work)
    return work[0][...] * down * across


def basis_kernel(pieces, inverse_far, basis_far, order_far, top, low, basis_t, order, carried, gram, inverse, basis, sems):
    rows = inverse.shape[0] // pieces
    copies = [pltpu.make_async_copy(basis_far, basis, sems.at[pieces])]
    for i in range(pieces):
        part = pl.ds(i * rows, rows)
        copies.append(pltpu.make_async_copy(inverse_far.at[part], inverse.at[part], sems.at[i]))
    copies.append(pltpu.make_async_copy(order_far, order, sems.at[pieces + 1]))
    for copy in copies:
        copy.start()
    copies[0].wait()
    basis_parts = split(basis[...])
    across = basis[...].T
    basis_t[...] = across
    across = split(across)
    for i in range(pieces):
        part = slice(i * rows, (i + 1) * rows)
        copies[i + 1].wait()
        block = split(inverse[part])
        top[part], low[part] = block
        carried[part] = mm_parts(block, basis_parts)
    gram[...] = mm_parts(across, split(carried[...]))
    copies[-1].wait()


def leaf_kernel(order, rhs, top, low, basis_t, solved, projected):
    points = rhs.shape[0]
    wide = 128
    numbers = order[...].astype(F32)
    lanes = lax.broadcasted_iota(jnp.int32, (wide, points), 1).astype(F32)
    gather = []
    for i in range(0, points, wide):
        column = jnp.broadcast_to(numbers[:, i:i + wide], (wide, wide)).T
        column = jnp.concatenate([column] * (points // wide), axis=1)
        gather.append(jnp.where(column == lanes, 1.0, 0.0).astype(BF16))
    ordered = pick(jnp.concatenate(gather, axis=0), rhs[...])
    z = mm_parts((top[...], low[...]), split(ordered))
    solved[...] = z
    projected[...] = mm(basis_t[...], z)


def place_kernel(order, solved, carried, solved_out, carried_out):
    points = solved.shape[0]
    rows = lax.broadcasted_iota(jnp.int32, (points, points), 0)
    scatter = jnp.where(order[...] == rows, 1.0, 0.0).astype(BF16)
    solved_out[...] = pick(scatter, solved[...])
    carried_out[...] = pick(scatter, carried[...])


def node_kernel(level, gram, other, precision, *rest):
    coupling = precision[0, level].astype(F32)
    whole = gram[...] + other[...]
    if len(rest) == 5:
        rest[0][...] = scaled_inverse(coupling + whole, *rest[1:])
        return
    transfer, inverse, mover, gram_out, *work = rest
    mixer = transfer[0, level]
    left = mm(mixer, precision[0, level], None, ((0,), (0,)))
    right = sum(mm(part.astype(BF16), mixer, None) for part in parts(whole))
    m = scaled_inverse(coupling + whole, *work)
    n = mm(left, m)
    inverse[...] = m
    mover[...] = n
    gram_out[...] = mm(n, right)


def lift_kernel(first, last, *refs):
    refs = list(refs)
    projected, other, inverse, mover = (ref[...] for ref in refs[:4])
    s = projected + other
    alpha = mm(inverse, s)
    projected_out, total_out, mixing_out = refs[-3:]
    projected_out[...] = mm(mover, s)
    if first:
        total, mixing = alpha, mover.T
    else:
        total, mixing = refs[4][...], refs[5][...]
        total = total + mm(mixing, alpha)
        mixing = mm(mixing, mover, HIGH, ((1,), (1,)))
    if last:
        solved, carried = refs[-5:-3]
        total = solved[...] - mm(carried[...], total)
        mixing = mm(carried[...], mixing)
    total_out[...] = total
    mixing_out[...] = mixing


def root_kernel(pieces, projected, other, inverse, solved, carried, out_far, out, sems):
    alpha = mm(inverse[...], projected[...] + other[...])
    rows = out.shape[0] // pieces
    copies = []
    for i in range(pieces):
        part = pl.ds(i * rows, rows)
        out[part] = solved[part] - mm(carried[part], alpha)
        copies.append(pltpu.make_async_copy(out.at[part], out_far.at[part], sems.at[i]))
        copies[-1].start()
    for copy in copies:
        copy.wait()


def call(kernel, outs, *args, scratch=(), work=0, place=VMEM, result=VMEM, after=()):
    if place is FAR:
        args = [pltpu.with_memory_space_constraint(arg, pltpu.HBM) for arg in args]
    return pl.pallas_call(
        lambda *refs: kernel(*refs[len(after):]),
        out_shape=[jax.ShapeDtypeStruct(getattr(out, "shape", out), getattr(out, "dtype", F32)) for out in outs],
        in_specs=[FAR] * len(after) + [place] * len(args),
        out_specs=[result] * len(outs),
        scratch_shapes=scratch,
        cost_estimate=pl.CostEstimate(flops=work, bytes_accessed=0, transcendentals=0),
        compiler_params=PARAMS,
    )(*after, *args)


def from_partner(block, axis, apart):
    count = lax.axis_size(axis)
    return lax.ppermute(block, axis, [(i, i ^ 1 << apart) for i in range(count)])


def body(rhs, order, inverse, basis, transfer, precision):
    points, columns = rhs.shape
    rank = basis.shape[1]
    square, tall, block = (rank, rank), (points, rank), (rank, columns)
    levels = lax.axis_size("leaf").bit_length() - 1
    pieces = 2
    half = jax.ShapeDtypeStruct(inverse.shape, BF16)
    top, low, basis_t, order, carried, gram = call(
        functools.partial(basis_kernel, pieces), [half, half, (rank, points), order, tall, square],
        inverse, basis, order, place=FAR, work=GIGA,
        scratch=[pltpu.VMEM(inverse.shape, F32), pltpu.VMEM(tall, F32), pltpu.SemaphoreType.DMA((pieces + 2,))]
    )
    other_gram = from_partner(gram, "leaf", 0)
    solved, projected = call(leaf_kernel, [rhs, block], order, rhs, top, low, basis_t, work=2 * GIGA)
    place = lambda *after: call(place_kernel, [rhs, tall], order, solved, carried, work=GIGA, after=after)
    if levels < 3:
        solved, carried = place()
    state, after = (), ()
    for k in range(levels - 1):
        other = from_partner(projected, "leaf", k)
        m, n, gram = call(
            functools.partial(node_kernel, k), [square] * 3, gram, other_gram, precision, transfer,
            scratch=invert_scratch(rank), work=6 * GIGA, after=after
        )
        other_gram = from_partner(gram, "leaf", k + 1)
        last = k == levels - 2
        projected, *state = call(
            functools.partial(lift_kernel, k == 0, last),
            [block, (points, columns), tall] if last else [block, block, square],
            projected, other, m, n, *state, *((solved, carried) if last else ()), work=GIGA
        )
        if k == 0 and not last:
            solved, carried = place(projected)
            after = (carried,)
    solved, carried = state or (solved, carried)
    k = levels - 1
    other = from_partner(projected, "leaf", k)
    (m,) = call(functools.partial(node_kernel, k), [square], gram, other_gram, precision, scratch=invert_scratch(rank), work=6 * GIGA)
    (out,) = call(
        functools.partial(root_kernel, pieces), [rhs], projected, other, m, solved, carried, work=GIGA, result=FAR,
        scratch=[pltpu.VMEM(rhs.shape, F32), pltpu.SemaphoreType.DMA((pieces,))]
    )
    return out


def solution(mesh):
    placed = (
        P("leaf", "rhs"),
        P("leaf", None),
        P("leaf", None),
        P("leaf", None),
        P("leaf", None, None, None),
        P("leaf", None, None, None),
    )
    return jax.shard_map(
        body, mesh=mesh, in_specs=placed, out_specs=P("leaf", "rhs"), check_vma=False
    )
```

```python
import functools

import jax
import jax.numpy as jnp
from jax import lax
from jax.experimental import pallas as pl
from jax.experimental.pallas import tpu as pltpu
from jax.sharding import PartitionSpec as P

F32 = jnp.float32
BF16 = jnp.bfloat16
HIGH = lax.Precision.HIGH
SUB = 8
GIGA = 10 ** 9
VMEM = pl.BlockSpec(memory_space=pltpu.VMEM)
FAR = pl.BlockSpec(memory_space=pltpu.HBM)
PARAMS = pltpu.CompilerParams(vmem_limit_bytes=32 * 1024 * 1024)


def mm(a, b, precision=HIGH, dims=((1,), (0,))):
    return lax.dot_general(a, b, (dims, ((), ())), precision=precision, preferred_element_type=F32)


def split(x):
    top = x.astype(BF16)
    return top, (x - top.astype(F32)).astype(BF16)


def mm_parts(a, b):
    columns = b[0].shape[1]
    both = jnp.dot(a[0], jnp.concatenate(b, axis=1), preferred_element_type=F32)
    return both[:, :columns] + (both[:, columns:] + jnp.dot(a[1], b[0], preferred_element_type=F32))


def pick(mask, x):
    top, low = split(x)
    one = lambda part: lax.dot_general(mask, part, (((1,), (0,)), ((), ())), preferred_element_type=F32)
    return one(top) + one(low)


def reciprocal(x):
    return pltpu.reciprocal(x, approx=True)

def parts(x):
    top = x.astype(BF16).astype(F32)
    rest = x - top
    mid = rest.astype(BF16).astype(F32)
    return top, mid, rest - mid

def spread(x, k):
    return jnp.broadcast_to(x[:, k:k + 1], x.shape)


def four(x, y, cols, at, k, lane, row, hold):
    size = x.shape[1]
    across = size // SUB * SUB
    inside = (lane >= k) & (lane < k + 4)
    own = (row >= at) & (row < at + 4)
    ahead = [(k + 4 + j) % across for j in range(4)]
    coming = [spread(x, a) for a in ahead]
    down = [spread(y, k + j) for j in range(4)]
    hold[8] = x
    for j in range(4):
        hold[j] = cols[j]
        hold[4 + j] = coming[j]
    line = lambda j, i: jnp.broadcast_to(hold[j, at + i:at + i + 1], (SUB, size))
    a0, a1, a2 = line(0, 0), line(1, 0), line(1, 1)
    b00, b01, b10, b11 = line(0, 2), line(1, 2), line(0, 3), line(1, 3)
    c0, c1, c2 = line(2, 2), line(3, 2), line(3, 3)
    det = a0 * a2 - a1 * a1
    g00, g01 = b00 * a2 - b01 * a1, b01 * a0 - b00 * a1
    g10, g11 = b10 * a2 - b11 * a1, b11 * a0 - b10 * a1
    s0 = det * c0 - (g00 * b00 + g01 * b01)
    s1 = det * c1 - (g00 * b10 + g01 * b11)
    s2 = det * c2 - (g10 * b10 + g11 * b11)
    rs = reciprocal(s0 * s2 - s1 * s1)
    ra = reciprocal(det)

    def known(e):
        t2 = det * e[2] - (g00 * e[0] + g01 * e[1])
        t3 = det * e[3] - (g10 * e[0] + g11 * e[1])
        return a2 * e[0] - a1 * e[1], a0 * e[1] - a1 * e[0], s2 * t2 - s1 * t3, s0 * t3 - s1 * t2

    def second(c):
        return c[0], c[1], c[2] - (c[0] * g00 + c[1] * g01) * ra, c[3] - (c[0] * g10 + c[1] * g11) * ra

    def less(base, c, v):
        return (base - (c[0] * v[0] + c[1] * v[1]) * ra) - (c[2] * v[2] + c[3] * v[3]) * rs

    cols = second([jnp.where(own, jnp.where(row == at + j, -1.0, 0.0), cols[j]) for j in range(4)])
    down = second(down)
    there = [known([line(4 + j, i) for i in range(4)]) for j in range(4)]
    if at + 4 < SUB:
        after = [less(jnp.where(own, 0.0, coming[j]), cols, there[j]) for j in range(4)]
    else:
        after = [less(spread(y, ahead[j]), down, there[j]) for j in range(4)]
    here = known([jnp.where(inside, jnp.where(lane == k + j, 1.0, 0.0), line(8, j)) for j in range(4)])
    x = less(jnp.where(inside | own, 0.0, x), cols, here)
    y = less(jnp.where(inside, 0.0, y), down, here)
    return x, y, after


def invert(m, xt, w6, hold):
    size = m.shape[0]
    lane = lax.broadcasted_iota(jnp.int32, (SUB, size), 1)
    row = lax.broadcasted_iota(jnp.int32, (SUB, size), 0)
    wide = lax.broadcasted_iota(jnp.int32, (size, size), 1)
    eye = jnp.where(wide == lax.broadcasted_iota(jnp.int32, (size, size), 0), 1.0, 0.0).astype(BF16)
    count = size // SUB

    def trail(t):
        k = t * SUB
        u = jnp.dot(xt[...], w6[...], preferred_element_type=F32)
        new = jnp.where((wide >= k) & (wide < k + SUB), 0.0, m[...]) - u
        m[...] = new
        return new

    def step(t, carry):
        x, *cols = carry
        k = t * SUB
        after = (t + 1) % count * SUB
        y = trail(t - 1)[after:after + SUB] if t else m[SUB:2 * SUB]
        z = jnp.where(lane < k, -1.0, 1.0) * x
        z = jnp.where((lane >= k) & (lane < k + SUB), jnp.where(lane - k == row, -1.0, 0.0), z)
        h, n, l = parts(z)
        z = jnp.concatenate([h, h, n, n, h, l], axis=0).astype(BF16)
        xt[...] = lax.dot_general(eye, z, (((1,), (1,)), ((), ())), preferred_element_type=F32).astype(BF16)
        for g in range(0, SUB, 4):
            x, y, cols = four(x, y, cols, g, k + g, lane, row, hold.at[g // 4])
        h, n, l = parts(x)
        w6[...] = jnp.concatenate([h, n, h, n, l, h], axis=0).astype(BF16)
        m[pl.ds(k, SUB)] = jnp.zeros((SUB, size), F32)
        return y, *cols

    x = m[0:SUB]
    carry = (x, *(spread(x, j) for j in range(4)))
    for t in range(count):
        carry = step(t, carry)
    trail(count - 1)


def invert_scratch(size):
    return [
        pltpu.VMEM((size, size), F32), pltpu.VMEM((size, 6 * SUB), BF16), pltpu.VMEM((6 * SUB, size), BF16),
        pltpu.VMEM((SUB // 4, 9, SUB, size), F32),
    ]


def scaled_inverse(matrix, *work):
    size = matrix.shape[0]
    rows = lax.broadcasted_iota(jnp.int32, (size, size), 0)
    cols = lax.broadcasted_iota(jnp.int32, (size, size), 1)
    diagonal = jnp.where(rows == cols, matrix, 0.0)
    down = lax.rsqrt(jnp.sum(diagonal, axis=1, keepdims=True))
    across = lax.rsqrt(jnp.sum(diagonal, axis=0, keepdims=True))
    work[0][...] = matrix * down * across
    invert(*work)
    return work[0][...] * down * across


def basis_kernel(pieces, inverse_far, basis_far, order_far, top, low, basis_t, order, carried, gram, inverse, basis, sems):
    rows = inverse.shape[0] // pieces
    copies = [pltpu.make_async_copy(basis_far, basis, sems.at[pieces])]
    for i in range(pieces):
        part = pl.ds(i * rows, rows)
        copies.append(pltpu.make_async_copy(inverse_far.at[part], inverse.at[part], sems.at[i]))
    copies.append(pltpu.make_async_copy(order_far, order, sems.at[pieces + 1]))
    for copy in copies:
        copy.start()
    copies[0].wait()
    basis_parts = split(basis[...])
    across = basis[...].T
    basis_t[...] = across
    across = split(across)
    for i in range(pieces):
        part = slice(i * rows, (i + 1) * rows)
        copies[i + 1].wait()
        block = split(inverse[part])
        top[part], low[part] = block
        carried[part] = mm_parts(block, basis_parts)
    gram[...] = mm_parts(across, split(carried[...]))
    copies[-1].wait()


def leaf_kernel(order, rhs, top, low, basis_t, solved, projected):
    points = rhs.shape[0]
    wide = 128
    numbers = order[...].astype(F32)
    lanes = lax.broadcasted_iota(jnp.int32, (wide, points), 1).astype(F32)
    gather = []
    for i in range(0, points, wide):
        column = jnp.broadcast_to(numbers[:, i:i + wide], (wide, wide)).T
        column = jnp.concatenate([column] * (points // wide), axis=1)
        gather.append(jnp.where(column == lanes, 1.0, 0.0).astype(BF16))
    ordered = pick(jnp.concatenate(gather, axis=0), rhs[...])
    z = mm_parts((top[...], low[...]), split(ordered))
    solved[...] = z
    projected[...] = mm(basis_t[...], z)


def place_kernel(order, solved, carried, solved_out, carried_out):
    points = solved.shape[0]
    rows = lax.broadcasted_iota(jnp.int32, (points, points), 0)
    scatter = jnp.where(order[...] == rows, 1.0, 0.0).astype(BF16)
    solved_out[...] = pick(scatter, solved[...])
    carried_out[...] = pick(scatter, carried[...])


def node_kernel(level, gram, other, precision, *rest):
    coupling = precision[0, level].astype(F32)
    whole = gram[...] + other[...]
    if len(rest) == 5:
        rest[0][...] = scaled_inverse(coupling + whole, *rest[1:])
        return
    transfer, inverse, mover, gram_out, *work = rest
    mixer = transfer[0, level]
    left = mm(mixer, precision[0, level], None, ((0,), (0,)))
    right = sum(mm(part.astype(BF16), mixer, None) for part in parts(whole))
    m = scaled_inverse(coupling + whole, *work)
    n = mm(left, m)
    inverse[...] = m
    mover[...] = n
    gram_out[...] = mm(n, right)


def lift_kernel(first, last, *refs):
    refs = list(refs)
    projected, other, inverse, mover = (ref[...] for ref in refs[:4])
    s = projected + other
    alpha = mm(inverse, s)
    projected_out, total_out, mixing_out = refs[-3:]
    projected_out[...] = mm(mover, s)
    if first:
        total, mixing = alpha, mover.T
    else:
        total, mixing = refs[4][...], refs[5][...]
        total = total + mm(mixing, alpha)
        mixing = mm(mixing, mover, HIGH, ((1,), (1,)))
    if last:
        solved, carried = refs[-5:-3]
        total = solved[...] - mm(carried[...], total)
        mixing = mm(carried[...], mixing)
    total_out[...] = total
    mixing_out[...] = mixing


def root_kernel(pieces, projected, other, inverse, solved, carried, out_far, out, sems):
    alpha = mm(inverse[...], projected[...] + other[...])
    rows = out.shape[0] // pieces
    copies = []
    for i in range(pieces):
        part = pl.ds(i * rows, rows)
        out[part] = solved[part] - mm(carried[part], alpha)
        copies.append(pltpu.make_async_copy(out.at[part], out_far.at[part], sems.at[i]))
        copies[-1].start()
    for copy in copies:
        copy.wait()


def call(kernel, outs, *args, scratch=(), work=0, place=VMEM, result=VMEM, after=()):
    if place is FAR:
        args = [pltpu.with_memory_space_constraint(arg, pltpu.HBM) for arg in args]
    return pl.pallas_call(
        lambda *refs: kernel(*refs[len(after):]),
        out_shape=[jax.ShapeDtypeStruct(getattr(out, "shape", out), getattr(out, "dtype", F32)) for out in outs],
        in_specs=[FAR] * len(after) + [place] * len(args),
        out_specs=[result] * len(outs),
        scratch_shapes=scratch,
        cost_estimate=pl.CostEstimate(flops=work, bytes_accessed=0, transcendentals=0),
        compiler_params=PARAMS,
    )(*after, *args)


def from_partner(block, axis, apart):
    count = lax.axis_size(axis)
    return lax.ppermute(block, axis, [(i, i ^ 1 << apart) for i in range(count)])


def body(rhs, order, inverse, basis, transfer, precision):
    points, columns = rhs.shape
    rank = basis.shape[1]
    square, tall, block = (rank, rank), (points, rank), (rank, columns)
    levels = lax.axis_size("leaf").bit_length() - 1
    pieces = 2
    half = jax.ShapeDtypeStruct(inverse.shape, BF16)
    top, low, basis_t, order, carried, gram = call(
        functools.partial(basis_kernel, pieces), [half, half, (rank, points), order, tall, square],
        inverse, basis, order, place=FAR, work=GIGA,
        scratch=[pltpu.VMEM(inverse.shape, F32), pltpu.VMEM(tall, F32), pltpu.SemaphoreType.DMA((pieces + 2,))]
    )
    other_gram = from_partner(gram, "leaf", 0)
    solved, projected = call(leaf_kernel, [rhs, block], order, rhs, top, low, basis_t, work=2 * GIGA)
    place = lambda *after: call(place_kernel, [rhs, tall], order, solved, carried, work=GIGA, after=after)
    if levels < 3:
        solved, carried = place()
    state, after = (), ()
    for k in range(levels - 1):
        other = from_partner(projected, "leaf", k)
        m, n, gram = call(
            functools.partial(node_kernel, k), [square] * 3, gram, other_gram, precision, transfer,
            scratch=invert_scratch(rank), work=6 * GIGA, after=after
        )
        other_gram = from_partner(gram, "leaf", k + 1)
        last = k == levels - 2
        projected, *state = call(
            functools.partial(lift_kernel, k == 0, last),
            [block, (points, columns), tall] if last else [block, block, square],
            projected, other, m, n, *state, *((solved, carried) if last else ()), work=GIGA
        )
        if k == 0 and not last:
            solved, carried = place(projected)
            after = (carried,)
    solved, carried = state or (solved, carried)
    k = levels - 1
    other = from_partner(projected, "leaf", k)
    (m,) = call(functools.partial(node_kernel, k), [square], gram, other_gram, precision, scratch=invert_scratch(rank), work=6 * GIGA)
    (out,) = call(
        functools.partial(root_kernel, pieces), [rhs], projected, other, m, solved, carried, work=GIGA, result=FAR,
        scratch=[pltpu.VMEM(rhs.shape, F32), pltpu.SemaphoreType.DMA((pieces,))]
    )
    return out


def solution(mesh):
    placed = (
        P("leaf", "rhs"),
        P("leaf", None),
        P("leaf", None),
        P("leaf", None),
        P("leaf", None, None, None),
        P("leaf", None, None, None),
    )
    return jax.shard_map(
        body, mesh=mesh, in_specs=placed, out_specs=P("leaf", "rhs"), check_vma=False
    )
```

```python
import functools

import jax
import jax.numpy as jnp
from jax import lax
from jax.experimental import pallas as pl
from jax.experimental.pallas import tpu as pltpu
from jax.sharding import PartitionSpec as P

F32 = jnp.float32
BF16 = jnp.bfloat16
HIGH = lax.Precision.HIGH
SUB = 8
GIGA = 10 ** 9
VMEM = pl.BlockSpec(memory_space=pltpu.VMEM)
FAR = pl.BlockSpec(memory_space=pltpu.HBM)
PARAMS = pltpu.CompilerParams(vmem_limit_bytes=32 * 1024 * 1024)


def mm(a, b, precision=HIGH, dims=((1,), (0,))):
    return lax.dot_general(a, b, (dims, ((), ())), precision=precision, preferred_element_type=F32)


def split(x):
    top = x.astype(BF16)
    return top, (x - top.astype(F32)).astype(BF16)


def mm_parts(a, b):
    columns = b[0].shape[1]
    both = jnp.dot(a[0], jnp.concatenate(b, axis=1), preferred_element_type=F32)
    return both[:, :columns] + (both[:, columns:] + jnp.dot(a[1], b[0], preferred_element_type=F32))


def pick(mask, x):
    top, low = split(x)
    one = lambda part: lax.dot_general(mask, part, (((1,), (0,)), ((), ())), preferred_element_type=F32)
    return one(top) + one(low)


def reciprocal(x):
    return pltpu.reciprocal(x, approx=True)

def parts(x):
    top = x.astype(BF16).astype(F32)
    rest = x - top
    mid = rest.astype(BF16).astype(F32)
    return top, mid, rest - mid

def spread(x, k):
    return jnp.broadcast_to(x[:, k:k + 1], x.shape)


def four(x, y, cols, at, k, lane, row, hold):
    size = x.shape[1]
    across = size // SUB * SUB
    inside = (lane >= k) & (lane < k + 4)
    own = (row >= at) & (row < at + 4)
    ahead = [(k + 4 + j) % across for j in range(4)]
    coming = [spread(x, a) for a in ahead]
    down = [spread(y, k + j) for j in range(4)]
    for j, tile in enumerate([*cols, *coming, x]):
        hold[j * SUB:(j + 1) * SUB] = tile
    line = lambda j, i: hold[pl.ds(j * SUB + at + i, SUB, stride=0)]
    a0, a1, a2 = line(0, 0), line(1, 0), line(1, 1)
    b00, b01, b10, b11 = line(0, 2), line(1, 2), line(0, 3), line(1, 3)
    c0, c1, c2 = line(2, 2), line(3, 2), line(3, 3)
    det = a0 * a2 - a1 * a1
    g00, g01 = b00 * a2 - b01 * a1, b01 * a0 - b00 * a1
    g10, g11 = b10 * a2 - b11 * a1, b11 * a0 - b10 * a1
    s0 = det * c0 - (g00 * b00 + g01 * b01)
    s1 = det * c1 - (g00 * b10 + g01 * b11)
    s2 = det * c2 - (g10 * b10 + g11 * b11)
    rs = reciprocal(s0 * s2 - s1 * s1)
    ra = reciprocal(det)

    def known(e):
        t2 = det * e[2] - (g00 * e[0] + g01 * e[1])
        t3 = det * e[3] - (g10 * e[0] + g11 * e[1])
        return a2 * e[0] - a1 * e[1], a0 * e[1] - a1 * e[0], s2 * t2 - s1 * t3, s0 * t3 - s1 * t2

    def second(c):
        return c[0], c[1], c[2] - (c[0] * g00 + c[1] * g01) * ra, c[3] - (c[0] * g10 + c[1] * g11) * ra

    def less(base, c, v):
        return (base - (c[0] * v[0] + c[1] * v[1]) * ra) - (c[2] * v[2] + c[3] * v[3]) * rs

    cols = second([jnp.where(own, jnp.where(row == at + j, -1.0, 0.0), cols[j]) for j in range(4)])
    down = second(down)
    there = [known([line(4 + j, i) for i in range(4)]) for j in range(4)]
    if at + 4 < SUB:
        after = [less(jnp.where(own, 0.0, coming[j]), cols, there[j]) for j in range(4)]
    else:
        after = [less(spread(y, ahead[j]), down, there[j]) for j in range(4)]
    here = known([jnp.where(inside, jnp.where(lane == k + j, 1.0, 0.0), line(8, j)) for j in range(4)])
    x = less(jnp.where(inside | own, 0.0, x), cols, here)
    y = less(jnp.where(inside, 0.0, y), down, here)
    return x, y, after


def invert(m, xt, w6, hold):
    size = m.shape[0]
    lane = lax.broadcasted_iota(jnp.int32, (SUB, size), 1)
    row = lax.broadcasted_iota(jnp.int32, (SUB, size), 0)
    wide = lax.broadcasted_iota(jnp.int32, (size, size), 1)
    eye = jnp.where(wide == lax.broadcasted_iota(jnp.int32, (size, size), 0), 1.0, 0.0).astype(BF16)
    count = size // SUB

    def trail(t):
        k = t * SUB
        u = jnp.dot(xt[...], w6[...], preferred_element_type=F32)
        new = jnp.where((wide >= k) & (wide < k + SUB), 0.0, m[...]) - u
        m[...] = new
        return new

    def step(t, carry):
        x, *cols = carry
        k = t * SUB
        after = (t + 1) % count * SUB
        y = trail(t - 1)[after:after + SUB] if t else m[SUB:2 * SUB]
        z = jnp.where(lane < k, -1.0, 1.0) * x
        z = jnp.where((lane >= k) & (lane < k + SUB), jnp.where(lane - k == row, -1.0, 0.0), z)
        h, n, l = parts(z)
        z = jnp.concatenate([h, h, n, n, h, l], axis=0).astype(BF16)
        xt[...] = lax.dot_general(eye, z, (((1,), (1,)), ((), ())), preferred_element_type=F32).astype(BF16)
        for g in range(0, SUB, 4):
            x, y, cols = four(x, y, cols, g, k + g, lane, row, hold.at[g // 4])
        h, n, l = parts(x)
        w6[...] = jnp.concatenate([h, n, h, n, l, h], axis=0).astype(BF16)
        m[pl.ds(k, SUB)] = jnp.zeros((SUB, size), F32)
        return y, *cols

    x = m[0:SUB]
    carry = (x, *(spread(x, j) for j in range(4)))
    for t in range(count):
        carry = step(t, carry)
    trail(count - 1)


def invert_scratch(size):
    return [
        pltpu.VMEM((size, size), F32), pltpu.VMEM((size, 6 * SUB), BF16), pltpu.VMEM((6 * SUB, size), BF16),
        pltpu.VMEM((SUB // 4, 10 * SUB, size), F32),
    ]


def scaled_inverse(matrix, *work):
    size = matrix.shape[0]
    rows = lax.broadcasted_iota(jnp.int32, (size, size), 0)
    cols = lax.broadcasted_iota(jnp.int32, (size, size), 1)
    diagonal = jnp.where(rows == cols, matrix, 0.0)
    down = lax.rsqrt(jnp.sum(diagonal, axis=1, keepdims=True))
    across = lax.rsqrt(jnp.sum(diagonal, axis=0, keepdims=True))
    work[0][...] = matrix * down * across
    invert(*work)
    return work[0][...] * down * across


def basis_kernel(pieces, inverse_far, basis_far, order_far, top, low, basis_t, order, carried, gram, inverse, basis, sems):
    rows = inverse.shape[0] // pieces
    copies = [pltpu.make_async_copy(basis_far, basis, sems.at[pieces])]
    for i in range(pieces):
        part = pl.ds(i * rows, rows)
        copies.append(pltpu.make_async_copy(inverse_far.at[part], inverse.at[part], sems.at[i]))
    copies.append(pltpu.make_async_copy(order_far, order, sems.at[pieces + 1]))
    for copy in copies:
        copy.start()
    copies[0].wait()
    basis_parts = split(basis[...])
    across = basis[...].T
    basis_t[...] = across
    across = split(across)
    for i in range(pieces):
        part = slice(i * rows, (i + 1) * rows)
        copies[i + 1].wait()
        block = split(inverse[part])
        top[part], low[part] = block
        carried[part] = mm_parts(block, basis_parts)
    gram[...] = mm_parts(across, split(carried[...]))
    copies[-1].wait()


def leaf_kernel(order, rhs, top, low, basis_t, solved, projected):
    points = rhs.shape[0]
    wide = 128
    numbers = order[...].astype(F32)
    lanes = lax.broadcasted_iota(jnp.int32, (wide, points), 1).astype(F32)
    gather = []
    for i in range(0, points, wide):
        column = jnp.broadcast_to(numbers[:, i:i + wide], (wide, wide)).T
        column = jnp.concatenate([column] * (points // wide), axis=1)
        gather.append(jnp.where(column == lanes, 1.0, 0.0).astype(BF16))
    ordered = pick(jnp.concatenate(gather, axis=0), rhs[...])
    z = mm_parts((top[...], low[...]), split(ordered))
    solved[...] = z
    projected[...] = mm(basis_t[...], z)


def place_kernel(order, solved, carried, solved_out, carried_out):
    points = solved.shape[0]
    rows = lax.broadcasted_iota(jnp.int32, (points, points), 0)
    scatter = jnp.where(order[...] == rows, 1.0, 0.0).astype(BF16)
    solved_out[...] = pick(scatter, solved[...])
    carried_out[...] = pick(scatter, carried[...])


def node_kernel(level, gram, other, precision, *rest):
    coupling = precision[0, level].astype(F32)
    whole = gram[...] + other[...]
    if len(rest) == 5:
        rest[0][...] = scaled_inverse(coupling + whole, *rest[1:])
        return
    transfer, inverse, mover, gram_out, *work = rest
    mixer = transfer[0, level]
    left = mm(mixer, precision[0, level], None, ((0,), (0,)))
    right = sum(mm(part.astype(BF16), mixer, None) for part in parts(whole))
    m = scaled_inverse(coupling + whole, *work)
    n = mm(left, m)
    inverse[...] = m
    mover[...] = n
    gram_out[...] = mm(n, right)


def lift_kernel(first, last, *refs):
    refs = list(refs)
    projected, other, inverse, mover = (ref[...] for ref in refs[:4])
    s = projected + other
    alpha = mm(inverse, s)
    projected_out, total_out, mixing_out = refs[-3:]
    projected_out[...] = mm(mover, s)
    if first:
        total, mixing = alpha, mover.T
    else:
        total, mixing = refs[4][...], refs[5][...]
        total = total + mm(mixing, alpha)
        mixing = mm(mixing, mover, HIGH, ((1,), (1,)))
    if last:
        solved, carried = refs[-5:-3]
        total = solved[...] - mm(carried[...], total)
        mixing = mm(carried[...], mixing)
    total_out[...] = total
    mixing_out[...] = mixing


def root_kernel(pieces, projected, other, inverse, solved, carried, out_far, out, sems):
    alpha = mm(inverse[...], projected[...] + other[...])
    rows = out.shape[0] // pieces
    copies = []
    for i in range(pieces):
        part = pl.ds(i * rows, rows)
        out[part] = solved[part] - mm(carried[part], alpha)
        copies.append(pltpu.make_async_copy(out.at[part], out_far.at[part], sems.at[i]))
        copies[-1].start()
    for copy in copies:
        copy.wait()


def call(kernel, outs, *args, scratch=(), work=0, place=VMEM, result=VMEM, after=()):
    if place is FAR:
        args = [pltpu.with_memory_space_constraint(arg, pltpu.HBM) for arg in args]
    return pl.pallas_call(
        lambda *refs: kernel(*refs[len(after):]),
        out_shape=[jax.ShapeDtypeStruct(getattr(out, "shape", out), getattr(out, "dtype", F32)) for out in outs],
        in_specs=[FAR] * len(after) + [place] * len(args),
        out_specs=[result] * len(outs),
        scratch_shapes=scratch,
        cost_estimate=pl.CostEstimate(flops=work, bytes_accessed=0, transcendentals=0),
        compiler_params=PARAMS,
    )(*after, *args)


def from_partner(block, axis, apart):
    count = lax.axis_size(axis)
    return lax.ppermute(block, axis, [(i, i ^ 1 << apart) for i in range(count)])


def body(rhs, order, inverse, basis, transfer, precision):
    points, columns = rhs.shape
    rank = basis.shape[1]
    square, tall, block = (rank, rank), (points, rank), (rank, columns)
    levels = lax.axis_size("leaf").bit_length() - 1
    pieces = 2
    half = jax.ShapeDtypeStruct(inverse.shape, BF16)
    top, low, basis_t, order, carried, gram = call(
        functools.partial(basis_kernel, pieces), [half, half, (rank, points), order, tall, square],
        inverse, basis, order, place=FAR, work=GIGA,
        scratch=[pltpu.VMEM(inverse.shape, F32), pltpu.VMEM(tall, F32), pltpu.SemaphoreType.DMA((pieces + 2,))]
    )
    other_gram = from_partner(gram, "leaf", 0)
    solved, projected = call(leaf_kernel, [rhs, block], order, rhs, top, low, basis_t, work=2 * GIGA)
    place = lambda *after: call(place_kernel, [rhs, tall], order, solved, carried, work=GIGA, after=after)
    if levels < 3:
        solved, carried = place()
    state, after = (), ()
    for k in range(levels - 1):
        other = from_partner(projected, "leaf", k)
        m, n, gram = call(
            functools.partial(node_kernel, k), [square] * 3, gram, other_gram, precision, transfer,
            scratch=invert_scratch(rank), work=6 * GIGA, after=after
        )
        other_gram = from_partner(gram, "leaf", k + 1)
        last = k == levels - 2
        projected, *state = call(
            functools.partial(lift_kernel, k == 0, last),
            [block, (points, columns), tall] if last else [block, block, square],
            projected, other, m, n, *state, *((solved, carried) if last else ()), work=GIGA
        )
        if k == 0 and not last:
            solved, carried = place(projected)
            after = (carried,)
    solved, carried = state or (solved, carried)
    k = levels - 1
    other = from_partner(projected, "leaf", k)
    (m,) = call(functools.partial(node_kernel, k), [square], gram, other_gram, precision, scratch=invert_scratch(rank), work=6 * GIGA)
    (out,) = call(
        functools.partial(root_kernel, 2 * pieces), [rhs], projected, other, m, solved, carried, work=GIGA, result=FAR,
        scratch=[pltpu.VMEM(rhs.shape, F32), pltpu.SemaphoreType.DMA((2 * pieces,))]
    )
    return out


def solution(mesh):
    placed = (
        P("leaf", "rhs"),
        P("leaf", None),
        P("leaf", None),
        P("leaf", None),
        P("leaf", None, None, None),
        P("leaf", None, None, None),
    )
    return jax.shard_map(
        body, mesh=mesh, in_specs=placed, out_specs=P("leaf", "rhs"), check_vma=False
    )
```

```python
import functools

import jax
import jax.numpy as jnp
from jax import lax
from jax.experimental import pallas as pl
from jax.experimental.pallas import tpu as pltpu
from jax.sharding import PartitionSpec as P

F32 = jnp.float32
BF16 = jnp.bfloat16
HIGH = lax.Precision.HIGH
SUB = 8
GIGA = 10 ** 9
VMEM = pl.BlockSpec(memory_space=pltpu.VMEM)
FAR = pl.BlockSpec(memory_space=pltpu.HBM)
PARAMS = pltpu.CompilerParams(vmem_limit_bytes=32 * 1024 * 1024)


def mm(a, b, precision=HIGH, dims=((1,), (0,))):
    return lax.dot_general(a, b, (dims, ((), ())), precision=precision, preferred_element_type=F32)


def split(x):
    top = x.astype(BF16)
    return top, (x - top.astype(F32)).astype(BF16)


def mm_parts(a, b):
    columns = b[0].shape[1]
    both = jnp.dot(a[0], jnp.concatenate(b, axis=1), preferred_element_type=F32)
    return both[:, :columns] + (both[:, columns:] + jnp.dot(a[1], b[0], preferred_element_type=F32))


def pick(mask, x):
    top, low = split(x)
    one = lambda part: lax.dot_general(mask, part, (((1,), (0,)), ((), ())), preferred_element_type=F32)
    return one(top) + one(low)


def reciprocal(x):
    return pltpu.reciprocal(x, approx=True)

def parts(x):
    top = x.astype(BF16).astype(F32)
    rest = x - top
    mid = rest.astype(BF16).astype(F32)
    return top, mid, rest - mid

def spread(x, k):
    return jnp.broadcast_to(x[:, k:k + 1], x.shape)


def four(x, y, pivot, at, k, lane, row, hold):
    size = x.shape[1]
    inside = (lane >= k) & (lane < k + 4)
    own = (row >= at) & (row < at + 4)
    ahead = [(k + 4 + j) % size for j in range(4)]
    cols = [spread(x, k + j) for j in range(4)]
    down = [spread(y, k + j) for j in range(4)]
    coming = [spread(x, a) for a in ahead]
    tiles = [x, *coming]
    if at + 4 < SUB:
        first, start = 1, at + 4
    else:
        first, start = 5, 0
        tiles += [spread(y, a) for a in ahead]
    for j, tile in enumerate(tiles):
        hold[j * SUB:(j + 1) * SUB] = tile
    line = lambda j, i: hold[pl.ds(j * SUB + i, SUB, stride=0)]
    a0, a1, b00, b10, a2, b01, b11, c0, c1, c2 = pivot
    det = a0 * a2 - a1 * a1
    g00, g01 = b00 * a2 - b01 * a1, b01 * a0 - b00 * a1
    g10, g11 = b10 * a2 - b11 * a1, b11 * a0 - b10 * a1
    s0 = det * c0 - (g00 * b00 + g01 * b01)
    s1 = det * c1 - (g00 * b10 + g01 * b11)
    s2 = det * c2 - (g10 * b10 + g11 * b11)
    rs = reciprocal(s0 * s2 - s1 * s1)
    ra = reciprocal(det)

    def known(e):
        t2 = det * e[2] - (g00 * e[0] + g01 * e[1])
        t3 = det * e[3] - (g10 * e[0] + g11 * e[1])
        return a2 * e[0] - a1 * e[1], a0 * e[1] - a1 * e[0], s2 * t2 - s1 * t3, s0 * t3 - s1 * t2, t2, t3

    def second(c):
        return c[0], c[1], c[2] - (c[0] * g00 + c[1] * g01) * ra, c[3] - (c[0] * g10 + c[1] * g11) * ra

    def less(base, c, v):
        return (base - (c[0] * v[0] + c[1] * v[1]) * ra) - (c[2] * v[2] + c[3] * v[3]) * rs

    after = []
    sides = [[line(1 + j, at + i) for i in range(4)] for j in range(4)]
    there = [known(e) for e in sides]
    for i in range(4):
        for j in range(i, 4):
            e, v, t = sides[i], there[j], there[i][4:]
            plain = line(first + j, start + i) - (e[0] * v[0] + e[1] * v[1]) * ra
            after.append(plain - ((t[0] * v[2] + t[1] * v[3]) * ra) * rs)
    here = known([jnp.where(inside, jnp.where(lane == k + j, 1.0, 0.0), line(0, at + j)) for j in range(4)])
    cols = [jnp.where(own, jnp.where(row == at + j, -1.0, 0.0), cols[j]) for j in range(4)]
    x = less(jnp.where(inside | own, 0.0, x), second(cols), here)
    y = less(jnp.where(inside, 0.0, y), second(down), here)
    return x, y, after


def invert(m, xt, w6, hold):
    size = m.shape[0]
    lane = lax.broadcasted_iota(jnp.int32, (SUB, size), 1)
    row = lax.broadcasted_iota(jnp.int32, (SUB, size), 0)
    wide = lax.broadcasted_iota(jnp.int32, (size, size), 1)
    eye = jnp.where(wide == lax.broadcasted_iota(jnp.int32, (size, size), 0), 1.0, 0.0).astype(BF16)
    count = size // SUB

    def trail(t):
        k = t * SUB
        u = jnp.dot(xt[...], w6[...], preferred_element_type=F32)
        new = jnp.where((wide >= k) & (wide < k + SUB), 0.0, m[...]) - u
        m[...] = new
        return new

    def step(t, carry):
        x, pivot = carry
        k = t * SUB
        after = (t + 1) % count * SUB
        y = trail(t - 1)[after:after + SUB] if t else m[SUB:2 * SUB]
        z = jnp.where(lane < k, -1.0, 1.0) * x
        z = jnp.where((lane >= k) & (lane < k + SUB), jnp.where(lane - k == row, -1.0, 0.0), z)
        h, n, l = parts(z)
        z = jnp.concatenate([h, h, n, n, h, l], axis=0).astype(BF16)
        xt[...] = lax.dot_general(eye, z, (((1,), (1,)), ((), ())), preferred_element_type=F32).astype(BF16)
        for g in range(0, SUB, 4):
            x, y, pivot = four(x, y, pivot, g, k + g, lane, row, hold.at[g // 4])
        h, n, l = parts(x)
        w6[...] = jnp.concatenate([h, n, h, n, l, h], axis=0).astype(BF16)
        m[pl.ds(k, SUB)] = jnp.zeros((SUB, size), F32)
        return y, pivot

    x = m[0:SUB]
    carry = x, [jnp.broadcast_to(x[i:i + 1, j:j + 1], (SUB, size)) for i in range(4) for j in range(i, 4)]
    for t in range(count):
        carry = step(t, carry)
    trail(count - 1)


def invert_scratch(size):
    return [
        pltpu.VMEM((size, size), F32), pltpu.VMEM((size, 6 * SUB), BF16), pltpu.VMEM((6 * SUB, size), BF16),
        pltpu.VMEM((SUB // 4, 10 * SUB, size), F32),
    ]


def scaled_inverse(matrix, *work):
    size = matrix.shape[0]
    rows = lax.broadcasted_iota(jnp.int32, (size, size), 0)
    cols = lax.broadcasted_iota(jnp.int32, (size, size), 1)
    diagonal = jnp.where(rows == cols, matrix, 0.0)
    down = lax.rsqrt(jnp.sum(diagonal, axis=1, keepdims=True))
    across = lax.rsqrt(jnp.sum(diagonal, axis=0, keepdims=True))
    work[0][...] = matrix * down * across
    invert(*work)
    return work[0][...] * down * across


def basis_kernel(pieces, inverse_far, basis_far, order_far, top, low, basis_t, order, carried, gram, inverse, basis, sems):
    rows = inverse.shape[0] // pieces
    copies = [pltpu.make_async_copy(basis_far, basis, sems.at[pieces])]
    for i in range(pieces):
        part = pl.ds(i * rows, rows)
        copies.append(pltpu.make_async_copy(inverse_far.at[part], inverse.at[part], sems.at[i]))
    copies.append(pltpu.make_async_copy(order_far, order, sems.at[pieces + 1]))
    for copy in copies:
        copy.start()
    copies[0].wait()
    basis_parts = split(basis[...])
    across = basis[...].T
    basis_t[...] = across
    across = split(across)
    for i in range(pieces):
        part = slice(i * rows, (i + 1) * rows)
        copies[i + 1].wait()
        block = split(inverse[part])
        top[part], low[part] = block
        carried[part] = mm_parts(block, basis_parts)
    gram[...] = mm_parts(across, split(carried[...]))
    copies[-1].wait()


def leaf_kernel(order, rhs, top, low, basis_t, solved, projected):
    points = rhs.shape[0]
    wide = 128
    numbers = order[...].astype(F32)
    lanes = lax.broadcasted_iota(jnp.int32, (wide, points), 1).astype(F32)
    gather = []
    for i in range(0, points, wide):
        column = jnp.broadcast_to(numbers[:, i:i + wide], (wide, wide)).T
        column = jnp.concatenate([column] * (points // wide), axis=1)
        gather.append(jnp.where(column == lanes, 1.0, 0.0).astype(BF16))
    ordered = pick(jnp.concatenate(gather, axis=0), rhs[...])
    z = mm_parts((top[...], low[...]), split(ordered))
    solved[...] = z
    projected[...] = mm(basis_t[...], z)


def place_kernel(order, solved, carried, solved_out, carried_out):
    points = solved.shape[0]
    rows = lax.broadcasted_iota(jnp.int32, (points, points), 0)
    scatter = jnp.where(order[...] == rows, 1.0, 0.0).astype(BF16)
    solved_out[...] = pick(scatter, solved[...])
    carried_out[...] = pick(scatter, carried[...])


def node_kernel(level, gram, other, precision, *rest):
    coupling = precision[0, level].astype(F32)
    whole = gram[...] + other[...]
    if len(rest) == 5:
        rest[0][...] = scaled_inverse(coupling + whole, *rest[1:])
        return
    transfer, inverse, mover, gram_out, *work = rest
    mixer = transfer[0, level]
    left = mm(mixer, precision[0, level], None, ((0,), (0,)))
    right = sum(mm(part.astype(BF16), mixer, None) for part in parts(whole))
    m = scaled_inverse(coupling + whole, *work)
    n = mm(left, m)
    inverse[...] = m
    mover[...] = n
    gram_out[...] = mm(n, right)


def lift_kernel(first, last, *refs):
    refs = list(refs)
    projected, other, inverse, mover = (ref[...] for ref in refs[:4])
    s = projected + other
    alpha = mm(inverse, s)
    projected_out, total_out, mixing_out = refs[-3:]
    projected_out[...] = mm(mover, s)
    if first:
        total, mixing = alpha, mover.T
    else:
        total, mixing = refs[4][...], refs[5][...]
        total = total + mm(mixing, alpha)
        mixing = mm(mixing, mover, HIGH, ((1,), (1,)))
    if last:
        solved, carried = refs[-5:-3]
        total = solved[...] - mm(carried[...], total)
        mixing = mm(carried[...], mixing)
    total_out[...] = total
    mixing_out[...] = mixing


def root_kernel(pieces, projected, other, inverse, solved, carried, out_far, out, sems):
    alpha = mm(inverse[...], projected[...] + other[...])
    rows = out.shape[0] // pieces
    copies = []
    for i in range(pieces):
        part = pl.ds(i * rows, rows)
        out[part] = solved[part] - mm(carried[part], alpha)
        copies.append(pltpu.make_async_copy(out.at[part], out_far.at[part], sems.at[i]))
        copies[-1].start()
    for copy in copies:
        copy.wait()


def call(kernel, outs, *args, scratch=(), work=0, place=VMEM, result=VMEM, after=()):
    if place is FAR:
        args = [pltpu.with_memory_space_constraint(arg, pltpu.HBM) for arg in args]
    return pl.pallas_call(
        lambda *refs: kernel(*refs[len(after):]),
        out_shape=[jax.ShapeDtypeStruct(getattr(out, "shape", out), getattr(out, "dtype", F32)) for out in outs],
        in_specs=[FAR] * len(after) + [place] * len(args),
        out_specs=[result] * len(outs),
        scratch_shapes=scratch,
        cost_estimate=pl.CostEstimate(flops=work, bytes_accessed=0, transcendentals=0),
        compiler_params=PARAMS,
    )(*after, *args)


def from_partner(block, axis, apart):
    count = lax.axis_size(axis)
    return lax.ppermute(block, axis, [(i, i ^ 1 << apart) for i in range(count)])


def body(rhs, order, inverse, basis, transfer, precision):
    points, columns = rhs.shape
    rank = basis.shape[1]
    square, tall, block = (rank, rank), (points, rank), (rank, columns)
    levels = lax.axis_size("leaf").bit_length() - 1
    pieces = 2
    half = jax.ShapeDtypeStruct(inverse.shape, BF16)
    top, low, basis_t, order, carried, gram = call(
        functools.partial(basis_kernel, pieces), [half, half, (rank, points), order, tall, square],
        inverse, basis, order, place=FAR, work=GIGA,
        scratch=[pltpu.VMEM(inverse.shape, F32), pltpu.VMEM(tall, F32), pltpu.SemaphoreType.DMA((pieces + 2,))]
    )
    other_gram = from_partner(gram, "leaf", 0)
    solved, projected = call(leaf_kernel, [rhs, block], order, rhs, top, low, basis_t, work=2 * GIGA)
    place = lambda *after: call(place_kernel, [rhs, tall], order, solved, carried, work=GIGA, after=after)
    if levels < 3:
        solved, carried = place()
    state, after = (), ()
    for k in range(levels - 1):
        other = from_partner(projected, "leaf", k)
        m, n, gram = call(
            functools.partial(node_kernel, k), [square] * 3, gram, other_gram, precision, transfer,
            scratch=invert_scratch(rank), work=6 * GIGA, after=after
        )
        other_gram = from_partner(gram, "leaf", k + 1)
        last = k == levels - 2
        projected, *state = call(
            functools.partial(lift_kernel, k == 0, last),
            [block, (points, columns), tall] if last else [block, block, square],
            projected, other, m, n, *state, *((solved, carried) if last else ()), work=GIGA
        )
        if k == 0 and not last:
            solved, carried = place(projected)
            after = (carried,)
    solved, carried = state or (solved, carried)
    k = levels - 1
    other = from_partner(projected, "leaf", k)
    (m,) = call(functools.partial(node_kernel, k), [square], gram, other_gram, precision, scratch=invert_scratch(rank), work=6 * GIGA)
    (out,) = call(
        functools.partial(root_kernel, 2 * pieces), [rhs], projected, other, m, solved, carried, work=GIGA, result=FAR,
        scratch=[pltpu.VMEM(rhs.shape, F32), pltpu.SemaphoreType.DMA((2 * pieces,))]
    )
    return out


def solution(mesh):
    placed = (
        P("leaf", "rhs"),
        P("leaf", None),
        P("leaf", None),
        P("leaf", None),
        P("leaf", None, None, None),
        P("leaf", None, None, None),
    )
    return jax.shard_map(
        body, mesh=mesh, in_specs=placed, out_specs=P("leaf", "rhs"), check_vma=False
    )
```

```python
import functools

import jax
import jax.numpy as jnp
from jax import lax
from jax.experimental import pallas as pl
from jax.experimental.pallas import tpu as pltpu
from jax.sharding import PartitionSpec as P

F32 = jnp.float32
BF16 = jnp.bfloat16
HIGH = lax.Precision.HIGH
SUB = 8
GIGA = 10 ** 9
VMEM = pl.BlockSpec(memory_space=pltpu.VMEM)
FAR = pl.BlockSpec(memory_space=pltpu.HBM)
PARAMS = pltpu.CompilerParams(vmem_limit_bytes=32 * 1024 * 1024)


def mm(a, b, precision=HIGH, dims=((1,), (0,))):
    return lax.dot_general(a, b, (dims, ((), ())), precision=precision, preferred_element_type=F32)


def split(x):
    top = x.astype(BF16)
    return top, (x - top.astype(F32)).astype(BF16)


def mm_parts(a, b):
    columns = b[0].shape[1]
    both = jnp.dot(a[0], jnp.concatenate(b, axis=1), preferred_element_type=F32)
    return both[:, :columns] + (both[:, columns:] + jnp.dot(a[1], b[0], preferred_element_type=F32))


def pick(mask, x):
    top, low = split(x)
    one = lambda part: lax.dot_general(mask, part, (((1,), (0,)), ((), ())), preferred_element_type=F32)
    return one(top) + one(low)


def reciprocal(x):
    return pltpu.reciprocal(x, approx=True)

def parts(x):
    top = x.astype(BF16).astype(F32)
    rest = x - top
    mid = rest.astype(BF16).astype(F32)
    return top, mid, rest - mid

def spread(x, k):
    return jnp.broadcast_to(x[:, k:k + 1], x.shape)


def four(x, y, cols, at, k, lane, row, hold):
    size = x.shape[1]
    across = size // SUB * SUB
    inside = (lane >= k) & (lane < k + 4)
    own = (row >= at) & (row < at + 4)
    ahead = [(k + 4 + j) % across for j in range(4)]
    coming = [spread(x, a) for a in ahead]
    down = [spread(y, k + j) for j in range(4)]
    for j, tile in enumerate([*cols, *coming, x]):
        hold[j * SUB:(j + 1) * SUB] = tile
    line = lambda j, i: hold[pl.ds(j * SUB + at + i, SUB, stride=0)]
    a0, a1, a2 = line(0, 0), line(1, 0), line(1, 1)
    b00, b01, b10, b11 = line(0, 2), line(1, 2), line(0, 3), line(1, 3)
    c0, c1, c2 = line(2, 2), line(3, 2), line(3, 3)
    det = a0 * a2 - a1 * a1
    g00, g01 = b00 * a2 - b01 * a1, b01 * a0 - b00 * a1
    g10, g11 = b10 * a2 - b11 * a1, b11 * a0 - b10 * a1
    s0 = det * c0 - (g00 * b00 + g01 * b01)
    s1 = det * c1 - (g00 * b10 + g01 * b11)
    s2 = det * c2 - (g10 * b10 + g11 * b11)
    rs = reciprocal(s0 * s2 - s1 * s1)
    ra = reciprocal(det)

    def known(e):
        t2 = det * e[2] - (g00 * e[0] + g01 * e[1])
        t3 = det * e[3] - (g10 * e[0] + g11 * e[1])
        return a2 * e[0] - a1 * e[1], a0 * e[1] - a1 * e[0], s2 * t2 - s1 * t3, s0 * t3 - s1 * t2

    def second(c):
        return c[0], c[1], c[2] - (c[0] * g00 + c[1] * g01) * ra, c[3] - (c[0] * g10 + c[1] * g11) * ra

    def less(base, c, v):
        return (base - (c[0] * v[0] + c[1] * v[1]) * ra) - (c[2] * v[2] + c[3] * v[3]) * rs

    cols = second([jnp.where(own, jnp.where(row == at + j, -1.0, 0.0), cols[j]) for j in range(4)])
    down = second(down)
    there = [known([line(4 + j, i) for i in range(4)]) for j in range(4)]
    if at + 4 < SUB:
        after = [less(jnp.where(own, 0.0, coming[j]), cols, there[j]) for j in range(4)]
    else:
        after = [less(spread(y, ahead[j]), down, there[j]) for j in range(4)]
    here = known([jnp.where(inside, jnp.where(lane == k + j, 1.0, 0.0), line(8, j)) for j in range(4)])
    x = less(jnp.where(inside | own, 0.0, x), cols, here)
    y = less(jnp.where(inside, 0.0, y), down, here)
    return x, y, after


def invert(m, xt, w6, hold):
    size = m.shape[0]
    lane = lax.broadcasted_iota(jnp.int32, (SUB, size), 1)
    row = lax.broadcasted_iota(jnp.int32, (SUB, size), 0)
    wide = lax.broadcasted_iota(jnp.int32, (size, size), 1)
    eye = jnp.where(wide == lax.broadcasted_iota(jnp.int32, (size, size), 0), 1.0, 0.0).astype(BF16)
    count = size // SUB

    def trail(t):
        k = t * SUB
        u = jnp.dot(xt[...], w6[...], preferred_element_type=F32)
        new = jnp.where((wide >= k) & (wide < k + SUB), 0.0, m[...]) - u
        m[...] = new
        return new

    def step(t, carry):
        x, *cols = carry
        k = t * SUB
        after = (t + 1) % count * SUB
        y = trail(t - 1)[after:after + SUB] if t else m[SUB:2 * SUB]
        z = jnp.where(lane < k, -1.0, 1.0) * x
        z = jnp.where((lane >= k) & (lane < k + SUB), jnp.where(lane - k == row, -1.0, 0.0), z)
        h, n, l = parts(z)
        z = jnp.concatenate([h, h, n, n, h, l], axis=0).astype(BF16)
        xt[...] = lax.dot_general(eye, z, (((1,), (1,)), ((), ())), preferred_element_type=F32).astype(BF16)
        for g in range(0, SUB, 4):
            x, y, cols = four(x, y, cols, g, k + g, lane, row, hold.at[g // 4])
        h, n, l = parts(x)
        w6[...] = jnp.concatenate([h, n, h, n, l, h], axis=0).astype(BF16)
        m[pl.ds(k, SUB)] = jnp.zeros((SUB, size), F32)
        return y, *cols

    x = m[0:SUB]
    carry = (x, *(spread(x, j) for j in range(4)))
    for t in range(count):
        carry = step(t, carry)
    trail(count - 1)


def invert_scratch(size):
    return [
        pltpu.VMEM((size, size), F32), pltpu.VMEM((size, 6 * SUB), BF16), pltpu.VMEM((6 * SUB, size), BF16),
        pltpu.VMEM((SUB // 4, 10 * SUB, size), F32),
    ]


def scaled_inverse(matrix, *work):
    size = matrix.shape[0]
    rows = lax.broadcasted_iota(jnp.int32, (size, size), 0)
    cols = lax.broadcasted_iota(jnp.int32, (size, size), 1)
    diagonal = jnp.where(rows == cols, matrix, 0.0)
    down = lax.rsqrt(jnp.sum(diagonal, axis=1, keepdims=True))
    across = lax.rsqrt(jnp.sum(diagonal, axis=0, keepdims=True))
    work[0][...] = matrix * down * across
    invert(*work)
    return work[0][...] * down * across


def fold(gram):
    size = gram.shape[0]
    half = size // 2
    rows = lax.broadcasted_iota(jnp.int32, (half, size), 0)
    cols = lax.broadcasted_iota(jnp.int32, (half, size), 1)
    low = gram[half:]
    body = jnp.where(cols < rows, pltpu.roll(low, half, 1), gram[:half])
    diagonal = jnp.sum(jnp.where(cols == rows + half, low, 0.0), axis=0, keepdims=True)
    return jnp.concatenate([body, jnp.where(rows[:SUB] == 0, diagonal, 0.0)], axis=0)


def unfold(folded):
    size = folded.shape[1]
    half = size // 2
    rows = lax.broadcasted_iota(jnp.int32, (size, size), 0)
    cols = lax.broadcasted_iota(jnp.int32, (size, size), 1)
    body = folded[:half]
    below = cols[:half] < rows[:half]
    low = pltpu.roll(jnp.where(below, body, 0.0), half, 1)
    low = jnp.where(cols[:half] == rows[:half] + half, folded[half:half + 1], low)
    upper = jnp.concatenate([jnp.where(below, 0.0, body), low], axis=0)
    return upper + jnp.where(rows == cols, 0.0, upper.T)


def basis_kernel(pieces, inverse_far, basis_far, order_far, top, low, basis_t, order, carried, gram, inverse, basis, sems):
    rows = inverse.shape[0] // pieces
    copies = [pltpu.make_async_copy(basis_far, basis, sems.at[pieces])]
    for i in range(pieces):
        part = pl.ds(i * rows, rows)
        copies.append(pltpu.make_async_copy(inverse_far.at[part], inverse.at[part], sems.at[i]))
    copies.append(pltpu.make_async_copy(order_far, order, sems.at[pieces + 1]))
    for copy in copies:
        copy.start()
    copies[0].wait()
    basis_parts = split(basis[...])
    across = basis[...].T
    basis_t[...] = across
    across = split(across)
    for i in range(pieces):
        part = slice(i * rows, (i + 1) * rows)
        copies[i + 1].wait()
        block = split(inverse[part])
        top[part], low[part] = block
        carried[part] = mm_parts(block, basis_parts)
    gram[...] = fold(mm_parts(across, split(carried[...])))
    copies[-1].wait()


def leaf_kernel(order, rhs, top, low, basis_t, solved, projected):
    points = rhs.shape[0]
    wide = 128
    numbers = order[...].astype(F32)
    lanes = lax.broadcasted_iota(jnp.int32, (wide, points), 1).astype(F32)
    gather = []
    for i in range(0, points, wide):
        column = jnp.broadcast_to(numbers[:, i:i + wide], (wide, wide)).T
        column = jnp.concatenate([column] * (points // wide), axis=1)
        gather.append(jnp.where(column == lanes, 1.0, 0.0).astype(BF16))
    ordered = pick(jnp.concatenate(gather, axis=0), rhs[...])
    z = mm_parts((top[...], low[...]), split(ordered))
    solved[...] = z
    projected[...] = mm(basis_t[...], z)


def node_kernel(level, gram, other, precision, *rest):
    coupling = precision[0, level].astype(F32)
    whole = unfold(gram[...] + other[...])
    if len(rest) == 5:
        rest[0][...] = scaled_inverse(coupling + whole, *rest[1:])
        return
    transfer, inverse, mover, gram_out, *work = rest
    mixer = transfer[0, level]
    left = mm(mixer, precision[0, level], None, ((0,), (0,)))
    right = sum(mm(part.astype(BF16), mixer, None) for part in parts(whole))
    m = scaled_inverse(coupling + whole, *work)
    n = mm(left, m)
    inverse[...] = m
    mover[...] = n
    gram_out[...] = fold(mm(n, right))


def lift_kernel(first, last, *refs):
    refs = list(refs)
    projected, other, inverse, mover = (refs.pop(0)[...] for _ in range(4))
    s = projected + other
    alpha = mm(inverse, s)
    outs = refs[-5:] if first and not last else refs[-3:]
    outs[0][...] = mm(mover, s)
    if first:
        order, solved, carried = (refs.pop(0)[...] for _ in range(3))
        points = solved.shape[0]
        rows = lax.broadcasted_iota(jnp.int32, (points, points), 0)
        scatter = jnp.where(order == rows, 1.0, 0.0).astype(BF16)
        solved, carried = pick(scatter, solved), pick(scatter, carried)
        total, mixing = alpha, mover.T
    else:
        total, mixing, solved, carried = (refs.pop(0)[...] for _ in range(4))
        total = total + mm(mixing, alpha)
        mixing = mm(mixing, mover, HIGH, ((1,), (1,)))
    if last:
        total = solved - mm(carried, total)
        mixing = mm(carried, mixing)
    outs[1][...] = total
    outs[2][...] = mixing
    if first and not last:
        outs[3][...] = solved
        outs[4][...] = carried


def root_kernel(pieces, projected, other, inverse, solved, carried, out_far, out, sems):
    alpha = mm(inverse[...], projected[...] + other[...])
    rows = out.shape[0] // pieces
    copies = []
    for i in range(pieces):
        part = pl.ds(i * rows, rows)
        out[part] = solved[part] - mm(carried[part], alpha)
        copies.append(pltpu.make_async_copy(out.at[part], out_far.at[part], sems.at[i]))
        copies[-1].start()
    for copy in copies:
        copy.wait()


def call(kernel, outs, *args, scratch=(), work=0, place=VMEM, result=VMEM):
    if place is FAR:
        args = [pltpu.with_memory_space_constraint(arg, pltpu.HBM) for arg in args]
    return pl.pallas_call(
        kernel,
        out_shape=[jax.ShapeDtypeStruct(getattr(out, "shape", out), getattr(out, "dtype", F32)) for out in outs],
        in_specs=[place] * len(args),
        out_specs=[result] * len(outs),
        scratch_shapes=scratch,
        cost_estimate=pl.CostEstimate(flops=work, bytes_accessed=0, transcendentals=0),
        compiler_params=PARAMS,
    )(*args)


def from_partner(block, axis, apart):
    count = lax.axis_size(axis)
    return lax.ppermute(block, axis, [(i, i ^ 1 << apart) for i in range(count)])


def body(rhs, order, inverse, basis, transfer, precision):
    points, columns = rhs.shape
    rank = basis.shape[1]
    square, tall, block = (rank, rank), (points, rank), (rank, columns)
    folded = (rank // 2 + SUB, rank)
    levels = lax.axis_size("leaf").bit_length() - 1
    pieces = 2
    half = jax.ShapeDtypeStruct(inverse.shape, BF16)
    top, low, basis_t, order, carried, gram = call(
        functools.partial(basis_kernel, pieces), [half, half, (rank, points), order, tall, folded],
        inverse, basis, order, place=FAR, work=GIGA,
        scratch=[pltpu.VMEM(inverse.shape, F32), pltpu.VMEM(tall, F32), pltpu.SemaphoreType.DMA((pieces + 2,))]
    )
    other_gram = from_partner(gram, "leaf", 0)
    solved, projected = call(leaf_kernel, [rhs, block], order, rhs, top, low, basis_t, work=2 * GIGA)
    if levels == 1:
        raise NotImplementedError("one level")
    state = [order, solved, carried]
    for k in range(levels - 1):
        other = from_partner(projected, "leaf", k)
        m, n, gram = call(
            functools.partial(node_kernel, k), [square, square, folded], gram, other_gram, precision, transfer,
            scratch=invert_scratch(rank), work=6 * GIGA
        )
        other_gram = from_partner(gram, "leaf", k + 1)
        first, last = k == 0, k == levels - 2
        outs = [rhs, tall] if last else [block, square, rhs, tall] if first else [block, square]
        projected, *new = call(
            functools.partial(lift_kernel, first, last), [block] + outs, projected, other, m, n, *state, work=GIGA
        )
        state = new + state[len(new):]
    solved, carried = state[:2]
    k = levels - 1
    other = from_partner(projected, "leaf", k)
    (m,) = call(functools.partial(node_kernel, k), [square], gram, other_gram, precision, scratch=invert_scratch(rank), work=6 * GIGA)
    (out,) = call(
        functools.partial(root_kernel, 2 * pieces), [rhs], projected, other, m, solved, carried, work=GIGA, result=FAR,
        scratch=[pltpu.VMEM(rhs.shape, F32), pltpu.SemaphoreType.DMA((2 * pieces,))]
    )
    return out


def solution(mesh):
    placed = (
        P("leaf", "rhs"),
        P("leaf", None),
        P("leaf", None),
        P("leaf", None),
        P("leaf", None, None, None),
        P("leaf", None, None, None),
    )
    return jax.shard_map(
        body, mesh=mesh, in_specs=placed, out_specs=P("leaf", "rhs"), check_vma=False
    )
```

```python
import functools

import jax
import jax.numpy as jnp
from jax import lax
from jax.experimental import pallas as pl
from jax.experimental.pallas import tpu as pltpu
from jax.sharding import PartitionSpec as P

F32 = jnp.float32
BF16 = jnp.bfloat16
HIGH = lax.Precision.HIGH
SUB = 8
GIGA = 10 ** 9
VMEM = pl.BlockSpec(memory_space=pltpu.VMEM)
FAR = pl.BlockSpec(memory_space=pltpu.HBM)
PARAMS = pltpu.CompilerParams(vmem_limit_bytes=32 * 1024 * 1024)


def mm(a, b, precision=HIGH, dims=((1,), (0,))):
    return lax.dot_general(a, b, (dims, ((), ())), precision=precision, preferred_element_type=F32)


def split(x):
    top = x.astype(BF16)
    return top, (x - top.astype(F32)).astype(BF16)


def mm_parts(a, b):
    columns = b[0].shape[1]
    both = jnp.dot(a[0], jnp.concatenate(b, axis=1), preferred_element_type=F32)
    return both[:, :columns] + (both[:, columns:] + jnp.dot(a[1], b[0], preferred_element_type=F32))


def pick(mask, x):
    top, low = split(x)
    one = lambda part: lax.dot_general(mask, part, (((1,), (0,)), ((), ())), preferred_element_type=F32)
    return one(top) + one(low)


def reciprocal(x):
    return pltpu.reciprocal(x, approx=True)

def parts(x):
    top = x.astype(BF16).astype(F32)
    rest = x - top
    mid = rest.astype(BF16).astype(F32)
    return top, mid, rest - mid

def spread(x, k):
    return jnp.broadcast_to(x[:, k:k + 1], x.shape)


def four(x, y, at, k, lane, row, hold):
    size = x.shape[1]
    inside = (lane >= k) & (lane < k + 4)
    own = (row >= at) & (row < at + 4)
    cols = [spread(x, k + j) for j in range(4)]
    down = [spread(y, k + j) for j in range(4)]
    for j, tile in enumerate([*cols, x]):
        hold[j * SUB:(j + 1) * SUB] = tile
    line = lambda j, i: hold[pl.ds(j * SUB + at + i, SUB, stride=0)]
    a0, a1, a2 = line(0, 0), line(1, 0), line(1, 1)
    b00, b01, b10, b11 = line(0, 2), line(1, 2), line(0, 3), line(1, 3)
    c0, c1, c2 = line(2, 2), line(3, 2), line(3, 3)
    det = a0 * a2 - a1 * a1
    g00, g01 = b00 * a2 - b01 * a1, b01 * a0 - b00 * a1
    g10, g11 = b10 * a2 - b11 * a1, b11 * a0 - b10 * a1
    s0 = det * c0 - (g00 * b00 + g01 * b01)
    s1 = det * c1 - (g00 * b10 + g01 * b11)
    s2 = det * c2 - (g10 * b10 + g11 * b11)
    rs = reciprocal(s0 * s2 - s1 * s1)
    ra = reciprocal(det)
    e = [jnp.where(inside, jnp.where(lane == k + j, 1.0, 0.0), line(4, j)) for j in range(4)]
    t2 = det * e[2] - (g00 * e[0] + g01 * e[1])
    t3 = det * e[3] - (g10 * e[0] + g11 * e[1])
    v0, v1 = a2 * e[0] - a1 * e[1], a0 * e[1] - a1 * e[0]
    v2, v3 = s2 * t2 - s1 * t3, s0 * t3 - s1 * t2

    def less(base, c):
        c2, c3 = c[2] - (c[0] * g00 + c[1] * g01) * ra, c[3] - (c[0] * g10 + c[1] * g11) * ra
        return (base - (c[0] * v0 + c[1] * v1) * ra) - (c2 * v2 + c3 * v3) * rs

    cols = [jnp.where(own, jnp.where(row == at + j, -1.0, 0.0), cols[j]) for j in range(4)]
    return less(jnp.where(inside | own, 0.0, x), cols), less(jnp.where(inside, 0.0, y), down)


def invert(m, xt, w6, hold):
    size = m.shape[0]
    lane = lax.broadcasted_iota(jnp.int32, (SUB, size), 1)
    row = lax.broadcasted_iota(jnp.int32, (SUB, size), 0)
    wide = lax.broadcasted_iota(jnp.int32, (size, size), 1)
    eye = jnp.where(wide == lax.broadcasted_iota(jnp.int32, (size, size), 0), 1.0, 0.0).astype(BF16)
    count = size // SUB

    def trail():
        new = m[...] - jnp.dot(xt[...], w6[...], preferred_element_type=F32)
        m[...] = new
        return new

    x, y = m[0:SUB], m[SUB:2 * SUB]
    for t in range(count):
        k = t * SUB
        if t:
            after = (t + 1) % count * SUB
            y = trail()[after:after + SUB]
        unit = jnp.where(lane - row == k, 1.0, 0.0)
        z = jnp.where((lane >= k) & (lane < k + SUB), -unit, jnp.where(lane < k, -x, x))
        h, n, l = parts(z)
        z = jnp.concatenate([h, h, n, n, h, l], axis=0).astype(BF16)
        xt[...] = lax.dot_general(eye, z, (((1,), (1,)), ((), ())), preferred_element_type=F32).astype(BF16)
        for g in range(0, SUB, 4):
            x, y = four(x, y, g, k + g, lane, row, hold.at[g // 4])
        h, n, l = parts(x + unit)
        w6[...] = jnp.concatenate([h, n, h, n, l, h], axis=0).astype(BF16)
        m[k:k + SUB] = -unit
        x = y
    trail()


def invert_scratch(size):
    return [
        pltpu.VMEM((size, size), F32), pltpu.VMEM((size, 6 * SUB), BF16), pltpu.VMEM((6 * SUB, size), BF16),
        pltpu.VMEM((SUB // 4, 6 * SUB, size), F32),
    ]


def scaled_inverse(matrix, *work):
    size = matrix.shape[0]
    rows = lax.broadcasted_iota(jnp.int32, (size, size), 0)
    cols = lax.broadcasted_iota(jnp.int32, (size, size), 1)
    diagonal = jnp.where(rows == cols, matrix, 0.0)
    down = lax.rsqrt(jnp.sum(diagonal, axis=1, keepdims=True))
    across = lax.rsqrt(jnp.sum(diagonal, axis=0, keepdims=True))
    work[0][...] = matrix * down * across
    invert(*work)
    return work[0][...] * down * across


def fold(gram):
    size = gram.shape[0]
    half = size // 2
    rows = lax.broadcasted_iota(jnp.int32, (half, size), 0)
    cols = lax.broadcasted_iota(jnp.int32, (half, size), 1)
    low = gram[half:]
    body = jnp.where(cols < rows, pltpu.roll(low, half, 1), gram[:half])
    diagonal = jnp.sum(jnp.where(cols == rows + half, low, 0.0), axis=0, keepdims=True)
    return jnp.concatenate([body, jnp.where(rows[:SUB] == 0, diagonal, 0.0)], axis=0)


def unfold(folded):
    size = folded.shape[1]
    half = size // 2
    rows = lax.broadcasted_iota(jnp.int32, (size, size), 0)
    cols = lax.broadcasted_iota(jnp.int32, (size, size), 1)
    body = folded[:half]
    below = cols[:half] < rows[:half]
    low = pltpu.roll(jnp.where(below, body, 0.0), half, 1)
    low = jnp.where(cols[:half] == rows[:half] + half, folded[half:half + 1], low)
    upper = jnp.concatenate([jnp.where(below, 0.0, body), low], axis=0)
    return upper + jnp.where(rows == cols, 0.0, upper.T)


def basis_kernel(pieces, inverse_far, basis_far, order_far, top, low, basis_t, order, carried, gram, inverse, basis, sems):
    rows = inverse.shape[0] // pieces
    copies = [pltpu.make_async_copy(basis_far, basis, sems.at[pieces])]
    for i in range(pieces):
        part = pl.ds(i * rows, rows)
        copies.append(pltpu.make_async_copy(inverse_far.at[part], inverse.at[part], sems.at[i]))
    copies.append(pltpu.make_async_copy(order_far, order, sems.at[pieces + 1]))
    for copy in copies:
        copy.start()
    copies[0].wait()
    basis_parts = split(basis[...])
    across = basis[...].T
    basis_t[...] = across
    across = split(across)
    for i in range(pieces):
        part = slice(i * rows, (i + 1) * rows)
        copies[i + 1].wait()
        block = split(inverse[part])
        top[part], low[part] = block
        carried[part] = mm_parts(block, basis_parts)
    gram[...] = fold(mm_parts(across, split(carried[...])))
    copies[-1].wait()


def leaf_kernel(order, rhs, top, low, basis_t, solved, projected):
    points = rhs.shape[0]
    wide = 128
    numbers = order[...].astype(F32)
    lanes = lax.broadcasted_iota(jnp.int32, (wide, points), 1).astype(F32)
    gather = []
    for i in range(0, points, wide):
        column = jnp.broadcast_to(numbers[:, i:i + wide], (wide, wide)).T
        column = jnp.concatenate([column] * (points // wide), axis=1)
        gather.append(jnp.where(column == lanes, 1.0, 0.0).astype(BF16))
    ordered = pick(jnp.concatenate(gather, axis=0), rhs[...])
    z = mm_parts((top[...], low[...]), split(ordered))
    solved[...] = z
    projected[...] = mm(basis_t[...], z)


def node_kernel(level, gram, other, precision, *rest):
    coupling = precision[0, level].astype(F32)
    whole = unfold(gram[...] + other[...])
    if len(rest) == 5:
        rest[0][...] = scaled_inverse(coupling + whole, *rest[1:])
        return
    transfer, inverse, mover, gram_out, *work = rest
    mixer = transfer[0, level]
    left = mm(mixer, precision[0, level], None, ((0,), (0,)))
    right = sum(mm(part.astype(BF16), mixer, None) for part in parts(whole))
    m = scaled_inverse(coupling + whole, *work)
    n = mm(left, m)
    inverse[...] = m
    mover[...] = n
    gram_out[...] = fold(mm(n, right))


def lift_kernel(first, last, *refs):
    refs = list(refs)
    projected, other, inverse, mover = (refs.pop(0)[...] for _ in range(4))
    s = projected + other
    alpha = mm(inverse, s)
    outs = refs[-5:] if first and not last else refs[-3:]
    outs[0][...] = mm(mover, s)
    if first:
        order, solved, carried = (refs.pop(0)[...] for _ in range(3))
        points = solved.shape[0]
        rows = lax.broadcasted_iota(jnp.int32, (points, points), 0)
        scatter = jnp.where(order == rows, 1.0, 0.0).astype(BF16)
        solved, carried = pick(scatter, solved), pick(scatter, carried)
        total, mixing = alpha, mover.T
    else:
        total, mixing, solved, carried = (refs.pop(0)[...] for _ in range(4))
        total = total + mm(mixing, alpha)
        mixing = mm(mixing, mover, HIGH, ((1,), (1,)))
    if last:
        total = solved - mm(carried, total)
        mixing = mm(carried, mixing)
    outs[1][...] = total
    outs[2][...] = mixing
    if first and not last:
        outs[3][...] = solved
        outs[4][...] = carried


def root_kernel(pieces, projected, other, inverse, solved, carried, out_far, out, sems):
    alpha = mm(inverse[...], projected[...] + other[...])
    rows = out.shape[0] // pieces
    copies = []
    for i in range(pieces):
        part = pl.ds(i * rows, rows)
        out[part] = solved[part] - mm(carried[part], alpha)
        copies.append(pltpu.make_async_copy(out.at[part], out_far.at[part], sems.at[i]))
        copies[-1].start()
    for copy in copies:
        copy.wait()


def call(kernel, outs, *args, scratch=(), work=0, place=VMEM, result=VMEM):
    if place is FAR:
        args = [pltpu.with_memory_space_constraint(arg, pltpu.HBM) for arg in args]
    return pl.pallas_call(
        kernel,
        out_shape=[jax.ShapeDtypeStruct(getattr(out, "shape", out), getattr(out, "dtype", F32)) for out in outs],
        in_specs=[place] * len(args),
        out_specs=[result] * len(outs),
        scratch_shapes=scratch,
        cost_estimate=pl.CostEstimate(flops=work, bytes_accessed=0, transcendentals=0),
        compiler_params=PARAMS,
    )(*args)


def from_partner(block, axis, apart):
    count = lax.axis_size(axis)
    return lax.ppermute(block, axis, [(i, i ^ 1 << apart) for i in range(count)])


def body(rhs, order, inverse, basis, transfer, precision):
    points, columns = rhs.shape
    rank = basis.shape[1]
    square, tall, block = (rank, rank), (points, rank), (rank, columns)
    folded = (rank // 2 + SUB, rank)
    levels = lax.axis_size("leaf").bit_length() - 1
    pieces = 2
    half = jax.ShapeDtypeStruct(inverse.shape, BF16)
    top, low, basis_t, order, carried, gram = call(
        functools.partial(basis_kernel, pieces), [half, half, (rank, points), order, tall, folded],
        inverse, basis, order, place=FAR, work=GIGA,
        scratch=[pltpu.VMEM(inverse.shape, F32), pltpu.VMEM(tall, F32), pltpu.SemaphoreType.DMA((pieces + 2,))]
    )
    other_gram = from_partner(gram, "leaf", 0)
    solved, projected = call(leaf_kernel, [rhs, block], order, rhs, top, low, basis_t, work=2 * GIGA)
    if levels == 1:
        raise NotImplementedError("one level")
    state = [order, solved, carried]
    for k in range(levels - 1):
        other = from_partner(projected, "leaf", k)
        m, n, gram = call(
            functools.partial(node_kernel, k), [square, square, folded], gram, other_gram, precision, transfer,
            scratch=invert_scratch(rank), work=6 * GIGA
        )
        other_gram = from_partner(gram, "leaf", k + 1)
        first, last = k == 0, k == levels - 2
        outs = [rhs, tall] if last else [block, square, rhs, tall] if first else [block, square]
        projected, *new = call(
            functools.partial(lift_kernel, first, last), [block] + outs, projected, other, m, n, *state, work=GIGA
        )
        state = new + state[len(new):]
    solved, carried = state[:2]
    k = levels - 1
    other = from_partner(projected, "leaf", k)
    (m,) = call(functools.partial(node_kernel, k), [square], gram, other_gram, precision, scratch=invert_scratch(rank), work=6 * GIGA)
    (out,) = call(
        functools.partial(root_kernel, 2 * pieces), [rhs], projected, other, m, solved, carried, work=GIGA, result=FAR,
        scratch=[pltpu.VMEM(rhs.shape, F32), pltpu.SemaphoreType.DMA((2 * pieces,))]
    )
    return out


def solution(mesh):
    placed = (
        P("leaf", "rhs"),
        P("leaf", None),
        P("leaf", None),
        P("leaf", None),
        P("leaf", None, None, None),
        P("leaf", None, None, None),
    )
    return jax.shard_map(
        body, mesh=mesh, in_specs=placed, out_specs=P("leaf", "rhs"), check_vma=False
    )
```

```python
import functools

import jax
import jax.numpy as jnp
from jax import lax
from jax.experimental import pallas as pl
from jax.experimental.pallas import tpu as pltpu
from jax.sharding import PartitionSpec as P

F32 = jnp.float32
BF16 = jnp.bfloat16
HIGH = lax.Precision.HIGH
SUB = 8
GIGA = 10 ** 9
VMEM = pl.BlockSpec(memory_space=pltpu.VMEM)
FAR = pl.BlockSpec(memory_space=pltpu.HBM)
PARAMS = pltpu.CompilerParams(vmem_limit_bytes=32 * 1024 * 1024)


def mm(a, b, precision=HIGH, dims=((1,), (0,))):
    return lax.dot_general(a, b, (dims, ((), ())), precision=precision, preferred_element_type=F32)


def split(x):
    top = x.astype(BF16)
    return top, (x - top.astype(F32)).astype(BF16)


def mm_parts(a, b):
    columns = b[0].shape[1]
    both = jnp.dot(a[0], jnp.concatenate(b, axis=1), preferred_element_type=F32)
    return both[:, :columns] + (both[:, columns:] + jnp.dot(a[1], b[0], preferred_element_type=F32))


def pick(mask, x):
    top, low = split(x)
    one = lambda part: lax.dot_general(mask, part, (((1,), (0,)), ((), ())), preferred_element_type=F32)
    return one(top) + one(low)


def reciprocal(x):
    return pltpu.reciprocal(x, approx=True)

def parts(x):
    top = x.astype(BF16).astype(F32)
    rest = x - top
    mid = rest.astype(BF16).astype(F32)
    return top, mid, rest - mid

def spread(x, k):
    return jnp.broadcast_to(x[:, k:k + 1], x.shape)


def four(x, y, cols, at, k, lane, row, hold):
    size = x.shape[1]
    inside = (lane >= k) & (lane < k + 4)
    own = (row >= at) & (row < at + 4)
    ahead = [(k + 4 + j) % size for j in range(4)]
    coming = [spread(x, a) for a in ahead]
    down = [spread(y, k + j) for j in range(4)]
    for j, tile in enumerate([*cols, *coming, x]):
        hold[j * SUB:(j + 1) * SUB] = tile
    line = lambda j, i: hold[pl.ds(j * SUB + at + i, SUB, stride=0)]
    a0, a1, a2 = line(0, 0), line(1, 0), line(1, 1)
    b00, b01, b10, b11 = line(0, 2), line(1, 2), line(0, 3), line(1, 3)
    c0, c1, c2 = line(2, 2), line(3, 2), line(3, 3)
    det = a0 * a2 - a1 * a1
    g00, g01 = b00 * a2 - b01 * a1, b01 * a0 - b00 * a1
    g10, g11 = b10 * a2 - b11 * a1, b11 * a0 - b10 * a1
    s0 = det * c0 - (g00 * b00 + g01 * b01)
    s1 = det * c1 - (g00 * b10 + g01 * b11)
    s2 = det * c2 - (g10 * b10 + g11 * b11)
    rs = reciprocal(s0 * s2 - s1 * s1)
    ra = reciprocal(det)

    def left(c):
        f0, f1 = (a2 * c[0] - a1 * c[1]) * ra, (a0 * c[1] - a1 * c[0]) * ra
        p2, p3 = c[2] - (f0 * b00 + f1 * b01), c[3] - (f0 * b10 + f1 * b11)
        return f0, f1, s2 * p2 - s1 * p3, s0 * p3 - s1 * p2

    def right(e):
        return e[0], e[1], det * e[2] - (g00 * e[0] + g01 * e[1]), det * e[3] - (g10 * e[0] + g11 * e[1])

    def less(base, c, e):
        return (base - (c[0] * e[0] + c[1] * e[1])) - (c[2] * e[2] + c[3] * e[3]) * rs

    cols = left([jnp.where(own, jnp.where(row == at + j, -1.0, 0.0), cols[j]) for j in range(4)])
    down = left(down)
    there = [right([line(4 + j, i) for i in range(4)]) for j in range(4)]
    if at + 4 < SUB:
        after = [less(jnp.where(own, 0.0, coming[j]), cols, there[j]) for j in range(4)]
    else:
        after = [less(spread(y, ahead[j]), down, there[j]) for j in range(4)]
    here = right([jnp.where(inside, jnp.where(lane == k + j, 1.0, 0.0), line(8, j)) for j in range(4)])
    return less(jnp.where(inside | own, 0.0, x), cols, here), less(jnp.where(inside, 0.0, y), down, here), after


def invert(m, xt, w6, hold):
    size = m.shape[0]
    lane = lax.broadcasted_iota(jnp.int32, (SUB, size), 1)
    row = lax.broadcasted_iota(jnp.int32, (SUB, size), 0)
    wide = lax.broadcasted_iota(jnp.int32, (size, size), 1)
    eye = jnp.where(wide == lax.broadcasted_iota(jnp.int32, (size, size), 0), 1.0, 0.0).astype(BF16)
    count = size // SUB

    def trail():
        new = m[...] - jnp.dot(xt[...], w6[...], preferred_element_type=F32)
        m[...] = new
        return new

    x, y = m[0:SUB], m[SUB:2 * SUB]
    cols = [spread(x, j) for j in range(4)]
    for t in range(count):
        k = t * SUB
        if t:
            after = (t + 1) % count * SUB
            y = trail()[after:after + SUB]
        unit = jnp.where(lane - row == k, 1.0, 0.0)
        panel = (lane >= k) & (lane < k + SUB)
        z = jnp.where(panel, -unit, jnp.where(lane < k, -x, x))
        h, n, l = parts(z)
        z = jnp.concatenate([h, h, n, n, h, l], axis=0).astype(BF16)
        xt[...] = lax.dot_general(eye, z, (((1,), (1,)), ((), ())), preferred_element_type=F32).astype(BF16)
        for g in range(0, SUB, 4):
            x, y, cols = four(x, y, cols, g, k + g, lane, row, hold.at[g // 4])
        h, n, l = parts(x + unit)
        w6[...] = jnp.concatenate([h, n, h, n, l, h], axis=0).astype(BF16)
        m[k:k + SUB] = -unit
        x = y
    trail()


def invert_scratch(size):
    return [
        pltpu.VMEM((size, size), F32), pltpu.VMEM((size, 6 * SUB), BF16), pltpu.VMEM((6 * SUB, size), BF16),
        pltpu.VMEM((SUB // 4, 10 * SUB, size), F32),
    ]


def scaled_inverse(matrix, *work):
    size = matrix.shape[0]
    rows = lax.broadcasted_iota(jnp.int32, (size, size), 0)
    cols = lax.broadcasted_iota(jnp.int32, (size, size), 1)
    diagonal = jnp.where(rows == cols, matrix, 0.0)
    down = lax.rsqrt(jnp.sum(diagonal, axis=1, keepdims=True))
    across = lax.rsqrt(jnp.sum(diagonal, axis=0, keepdims=True))
    work[0][...] = matrix * down * across
    invert(*work)
    return work[0][...] * down * across


def fold(gram):
    size = gram.shape[0]
    half = size // 2
    rows = lax.broadcasted_iota(jnp.int32, (half, size), 0)
    cols = lax.broadcasted_iota(jnp.int32, (half, size), 1)
    low = gram[half:]
    body = jnp.where(cols < rows, pltpu.roll(low, half, 1), gram[:half])
    diagonal = jnp.sum(jnp.where(cols == rows + half, low, 0.0), axis=0, keepdims=True)
    return jnp.concatenate([body, jnp.where(rows[:SUB] == 0, diagonal, 0.0)], axis=0)


def unfold(folded):
    size = folded.shape[1]
    half = size // 2
    rows = lax.broadcasted_iota(jnp.int32, (size, size), 0)
    cols = lax.broadcasted_iota(jnp.int32, (size, size), 1)
    body = folded[:half]
    below = cols[:half] < rows[:half]
    low = pltpu.roll(jnp.where(below, body, 0.0), half, 1)
    low = jnp.where(cols[:half] == rows[:half] + half, folded[half:half + 1], low)
    upper = jnp.concatenate([jnp.where(below, 0.0, body), low], axis=0)
    return upper + jnp.where(rows == cols, 0.0, upper.T)


def basis_kernel(pieces, inverse_far, basis_far, order_far, top, low, basis_t, order, carried, gram, inverse, basis, sems):
    rows = inverse.shape[0] // pieces
    copies = [pltpu.make_async_copy(basis_far, basis, sems.at[pieces])]
    for i in range(pieces):
        part = pl.ds(i * rows, rows)
        copies.append(pltpu.make_async_copy(inverse_far.at[part], inverse.at[part], sems.at[i]))
    copies.append(pltpu.make_async_copy(order_far, order, sems.at[pieces + 1]))
    for copy in copies:
        copy.start()
    copies[0].wait()
    basis_parts = split(basis[...])
    across = basis[...].T
    basis_t[...] = across
    across = split(across)
    for i in range(pieces):
        part = slice(i * rows, (i + 1) * rows)
        copies[i + 1].wait()
        block = split(inverse[part])
        top[part], low[part] = block
        carried[part] = mm_parts(block, basis_parts)
    gram[...] = fold(mm_parts(across, split(carried[...])))
    copies[-1].wait()


def leaf_kernel(order, rhs, top, low, basis_t, solved, projected):
    points = rhs.shape[0]
    wide = 128
    numbers = order[...].astype(F32)
    lanes = lax.broadcasted_iota(jnp.int32, (wide, points), 1).astype(F32)
    gather = []
    for i in range(0, points, wide):
        column = jnp.broadcast_to(numbers[:, i:i + wide], (wide, wide)).T
        column = jnp.concatenate([column] * (points // wide), axis=1)
        gather.append(jnp.where(column == lanes, 1.0, 0.0).astype(BF16))
    ordered = pick(jnp.concatenate(gather, axis=0), rhs[...])
    z = mm_parts((top[...], low[...]), split(ordered))
    solved[...] = z
    projected[...] = mm(basis_t[...], z)


def node_kernel(level, gram, other, precision, *rest):
    coupling = precision[0, level].astype(F32)
    whole = unfold(gram[...] + other[...])
    if len(rest) == 5:
        rest[0][...] = scaled_inverse(coupling + whole, *rest[1:])
        return
    transfer, inverse, mover, gram_out, *work = rest
    mixer = transfer[0, level]
    left = mm(mixer, precision[0, level], None, ((0,), (0,)))
    right = sum(mm(part.astype(BF16), mixer, None) for part in parts(whole))
    m = scaled_inverse(coupling + whole, *work)
    n = mm(left, m)
    inverse[...] = m
    mover[...] = n
    gram_out[...] = fold(mm(n, right))


def lift_kernel(first, last, *refs):
    refs = list(refs)
    projected, other, inverse, mover = (refs.pop(0)[...] for _ in range(4))
    s = projected + other
    alpha = mm(inverse, s)
    outs = refs[-5:] if first and not last else refs[-3:]
    outs[0][...] = mm(mover, s)
    if first:
        order, solved, carried = (refs.pop(0)[...] for _ in range(3))
        points = solved.shape[0]
        rows = lax.broadcasted_iota(jnp.int32, (points, points), 0)
        scatter = jnp.where(order == rows, 1.0, 0.0).astype(BF16)
        solved, carried = pick(scatter, solved), pick(scatter, carried)
        total, mixing = alpha, mover.T
    else:
        total, mixing, solved, carried = (refs.pop(0)[...] for _ in range(4))
        total = total + mm(mixing, alpha)
        mixing = mm(mixing, mover, HIGH, ((1,), (1,)))
    if last:
        total = solved - mm(carried, total)
        mixing = mm(carried, mixing)
    outs[1][...] = total
    outs[2][...] = mixing
    if first and not last:
        outs[3][...] = solved
        outs[4][...] = carried


def root_kernel(pieces, projected, other, inverse, solved, carried, out_far, out, sems):
    alpha = mm(inverse[...], projected[...] + other[...])
    rows = out.shape[0] // pieces
    copies = []
    for i in range(pieces):
        part = pl.ds(i * rows, rows)
        out[part] = solved[part] - mm(carried[part], alpha)
        copies.append(pltpu.make_async_copy(out.at[part], out_far.at[part], sems.at[i]))
        copies[-1].start()
    for copy in copies:
        copy.wait()


def call(kernel, outs, *args, scratch=(), work=0, place=VMEM, result=VMEM):
    if place is FAR:
        args = [pltpu.with_memory_space_constraint(arg, pltpu.HBM) for arg in args]
    return pl.pallas_call(
        kernel,
        out_shape=[jax.ShapeDtypeStruct(getattr(out, "shape", out), getattr(out, "dtype", F32)) for out in outs],
        in_specs=[place] * len(args),
        out_specs=[result] * len(outs),
        scratch_shapes=scratch,
        cost_estimate=pl.CostEstimate(flops=work, bytes_accessed=0, transcendentals=0),
        compiler_params=PARAMS,
    )(*args)


def from_partner(block, axis, apart):
    count = lax.axis_size(axis)
    return lax.ppermute(block, axis, [(i, i ^ 1 << apart) for i in range(count)])


def body(rhs, order, inverse, basis, transfer, precision):
    points, columns = rhs.shape
    rank = basis.shape[1]
    square, tall, block = (rank, rank), (points, rank), (rank, columns)
    folded = (rank // 2 + SUB, rank)
    levels = lax.axis_size("leaf").bit_length() - 1
    pieces = 2
    half = jax.ShapeDtypeStruct(inverse.shape, BF16)
    top, low, basis_t, order, carried, gram = call(
        functools.partial(basis_kernel, pieces), [half, half, (rank, points), order, tall, folded],
        inverse, basis, order, place=FAR, work=GIGA,
        scratch=[pltpu.VMEM(inverse.shape, F32), pltpu.VMEM(tall, F32), pltpu.SemaphoreType.DMA((pieces + 2,))]
    )
    other_gram = from_partner(gram, "leaf", 0)
    solved, projected = call(leaf_kernel, [rhs, block], order, rhs, top, low, basis_t, work=2 * GIGA)
    if levels == 1:
        raise NotImplementedError("one level")
    state = [order, solved, carried]
    for k in range(levels - 1):
        other = from_partner(projected, "leaf", k)
        m, n, gram = call(
            functools.partial(node_kernel, k), [square, square, folded], gram, other_gram, precision, transfer,
            scratch=invert_scratch(rank), work=6 * GIGA
        )
        other_gram = from_partner(gram, "leaf", k + 1)
        first, last = k == 0, k == levels - 2
        outs = [rhs, tall] if last else [block, square, rhs, tall] if first else [block, square]
        projected, *new = call(
            functools.partial(lift_kernel, first, last), [block] + outs, projected, other, m, n, *state, work=GIGA
        )
        state = new + state[len(new):]
    solved, carried = state[:2]
    k = levels - 1
    other = from_partner(projected, "leaf", k)
    (m,) = call(functools.partial(node_kernel, k), [square], gram, other_gram, precision, scratch=invert_scratch(rank), work=6 * GIGA)
    (out,) = call(
        functools.partial(root_kernel, 2 * pieces), [rhs], projected, other, m, solved, carried, work=GIGA, result=FAR,
        scratch=[pltpu.VMEM(rhs.shape, F32), pltpu.SemaphoreType.DMA((2 * pieces,))]
    )
    return out


def solution(mesh):
    placed = (
        P("leaf", "rhs"),
        P("leaf", None),
        P("leaf", None),
        P("leaf", None),
        P("leaf", None, None, None),
        P("leaf", None, None, None),
    )
    return jax.shard_map(
        body, mesh=mesh, in_specs=placed, out_specs=P("leaf", "rhs"), check_vma=False
    )
```

```python
import functools

import jax
import jax.numpy as jnp
from jax import lax
from jax.experimental import pallas as pl
from jax.experimental.pallas import tpu as pltpu
from jax.sharding import PartitionSpec as P

F32 = jnp.float32
BF16 = jnp.bfloat16
HIGH = lax.Precision.HIGH
SUB = 8
GIGA = 10 ** 9
VMEM = pl.BlockSpec(memory_space=pltpu.VMEM)
FAR = pl.BlockSpec(memory_space=pltpu.HBM)
PARAMS = pltpu.CompilerParams(vmem_limit_bytes=32 * 1024 * 1024)


def mm(a, b, precision=HIGH, dims=((1,), (0,))):
    return lax.dot_general(a, b, (dims, ((), ())), precision=precision, preferred_element_type=F32)


def split(x):
    top = x.astype(BF16)
    return top, (x - top.astype(F32)).astype(BF16)


def mm_parts(a, b):
    columns = b[0].shape[1]
    both = jnp.dot(a[0], jnp.concatenate(b, axis=1), preferred_element_type=F32)
    return both[:, :columns] + (both[:, columns:] + jnp.dot(a[1], b[0], preferred_element_type=F32))


def pick(mask, x):
    top, low = split(x)
    one = lambda part: lax.dot_general(mask, part, (((1,), (0,)), ((), ())), preferred_element_type=F32)
    return one(top) + one(low)


def reciprocal(x):
    return pltpu.reciprocal(x, approx=True)

def parts(x):
    top = x.astype(BF16).astype(F32)
    rest = x - top
    mid = rest.astype(BF16).astype(F32)
    return top, mid, rest - mid

def spread(x, k):
    return jnp.broadcast_to(x[:, k:k + 1], x.shape)


def four(x, y, cols, at, k, lane, row, hold):
    size = x.shape[1]
    across = size // SUB * SUB
    inside = (lane >= k) & (lane < k + 4)
    own = (row >= at) & (row < at + 4)
    ahead = [(k + 4 + j) % across for j in range(4)]
    coming = [spread(x, a) for a in ahead]
    down = [spread(y, k + j) for j in range(4)]
    for j, tile in enumerate([*cols, *coming, x]):
        hold[j * SUB:(j + 1) * SUB] = tile
    line = lambda j, i: hold[pl.ds(j * SUB + at + i, SUB, stride=0)]
    a0, a1, a2 = line(0, 0), line(1, 0), line(1, 1)
    b00, b01, b10, b11 = line(0, 2), line(1, 2), line(0, 3), line(1, 3)
    c0, c1, c2 = line(2, 2), line(3, 2), line(3, 3)
    det = a0 * a2 - a1 * a1
    g00, g01 = b00 * a2 - b01 * a1, b01 * a0 - b00 * a1
    g10, g11 = b10 * a2 - b11 * a1, b11 * a0 - b10 * a1
    s0 = det * c0 - (g00 * b00 + g01 * b01)
    s1 = det * c1 - (g00 * b10 + g01 * b11)
    s2 = det * c2 - (g10 * b10 + g11 * b11)
    rs = reciprocal(s0 * s2 - s1 * s1)
    ra = reciprocal(det)

    def known(e):
        t2 = det * e[2] - (g00 * e[0] + g01 * e[1])
        t3 = det * e[3] - (g10 * e[0] + g11 * e[1])
        return a2 * e[0] - a1 * e[1], a0 * e[1] - a1 * e[0], s2 * t2 - s1 * t3, s0 * t3 - s1 * t2

    def second(c):
        return c[0], c[1], c[2] - (c[0] * g00 + c[1] * g01) * ra, c[3] - (c[0] * g10 + c[1] * g11) * ra

    def less(base, c, v):
        return (base - (c[0] * v[0] + c[1] * v[1]) * ra) - (c[2] * v[2] + c[3] * v[3]) * rs

    cols = second([jnp.where(own, jnp.where(row == at + j, -1.0, 0.0), cols[j]) for j in range(4)])
    down = second(down)
    there = [known([line(4 + j, i) for i in range(4)]) for j in range(4)]
    if at + 4 < SUB:
        after = [less(jnp.where(own, 0.0, coming[j]), cols, there[j]) for j in range(4)]
    else:
        after = [less(spread(y, ahead[j]), down, there[j]) for j in range(4)]
    here = known([jnp.where(inside, jnp.where(lane == k + j, 1.0, 0.0), line(8, j)) for j in range(4)])
    x = less(jnp.where(inside | own, 0.0, x), cols, here)
    y = less(jnp.where(inside, 0.0, y), down, here)
    return x, y, after


def invert(m, xt, w6, hold):
    size = m.shape[0]
    lane = lax.broadcasted_iota(jnp.int32, (SUB, size), 1)
    row = lax.broadcasted_iota(jnp.int32, (SUB, size), 0)
    wide = lax.broadcasted_iota(jnp.int32, (size, size), 1)
    eye = jnp.where(wide == lax.broadcasted_iota(jnp.int32, (size, size), 0), 1.0, 0.0).astype(BF16)
    count = size // SUB

    def trail():
        new = m[...] - jnp.dot(xt[...], w6[...], preferred_element_type=F32)
        m[...] = new
        return new

    x, y = m[0:SUB], m[SUB:2 * SUB]
    cols = [spread(x, j) for j in range(4)]
    for t in range(count):
        k = t * SUB
        if t:
            after = (t + 1) % count * SUB
            y = trail()[after:after + SUB]
        unit = jnp.where(lane - row == k, 1.0, 0.0)
        z = jnp.where((lane >= k) & (lane < k + SUB), -unit, jnp.where(lane < k, -x, x))
        h, n, l = parts(z)
        z = jnp.concatenate([h, h, n, n, h, l], axis=0).astype(BF16)
        xt[...] = lax.dot_general(eye, z, (((1,), (1,)), ((), ())), preferred_element_type=F32).astype(BF16)
        for g in range(0, SUB, 4):
            x, y, cols = four(x, y, cols, g, k + g, lane, row, hold.at[g // 4])
        h, n, l = parts(x + unit)
        w6[...] = jnp.concatenate([h, n, h, n, l, h], axis=0).astype(BF16)
        m[k:k + SUB] = -unit
        x = y
    trail()


def invert_scratch(size):
    return [
        pltpu.VMEM((size, size), F32), pltpu.VMEM((size, 6 * SUB), BF16), pltpu.VMEM((6 * SUB, size), BF16),
        pltpu.VMEM((SUB // 4, 10 * SUB, size), F32),
    ]


def scaled_inverse(matrix, *work):
    size = matrix.shape[0]
    row = lax.broadcasted_iota(jnp.int32, (SUB, size), 0)
    lane = lax.broadcasted_iota(jnp.int32, (SUB, size), 1)
    tiles = [(k, matrix[k:k + SUB]) for k in range(0, size, SUB)]
    down = [lax.rsqrt(jnp.take_along_axis(tile, row + k, axis=1, mode="promise_in_bounds")) for k, tile in tiles]
    diagonal = sum(jnp.where(lane - row == k, scale, 0.0) for (k, _), scale in zip(tiles, down))
    across = jnp.sum(diagonal, axis=0, keepdims=True)
    down = jnp.concatenate(down, axis=0)
    work[0][...] = matrix * down * across
    invert(*work)
    return work[0][...] * down * across


def fold(gram):
    size = gram.shape[0]
    half = size // 2
    rows = lax.broadcasted_iota(jnp.int32, (half, size), 0)
    cols = lax.broadcasted_iota(jnp.int32, (half, size), 1)
    low = gram[half:]
    body = jnp.where(cols < rows, pltpu.roll(low, half, 1), gram[:half])
    diagonal = jnp.sum(jnp.where(cols == rows + half, low, 0.0), axis=0, keepdims=True)
    return jnp.concatenate([body, jnp.where(rows[:SUB] == 0, diagonal, 0.0)], axis=0)


def unfold(folded):
    size = folded.shape[1]
    half = size // 2
    rows = lax.broadcasted_iota(jnp.int32, (size, size), 0)
    cols = lax.broadcasted_iota(jnp.int32, (size, size), 1)
    body = folded[:half]
    below = cols[:half] < rows[:half]
    low = pltpu.roll(jnp.where(below, body, 0.0), half, 1)
    low = jnp.where(cols[:half] == rows[:half] + half, folded[half:half + 1], low)
    upper = jnp.concatenate([jnp.where(below, 0.0, body), low], axis=0)
    return upper + jnp.where(rows == cols, 0.0, upper.T)


def basis_kernel(pieces, inverse_far, basis_far, order_far, top, low, basis_t, order, carried, gram, inverse, basis, sems):
    rows = inverse.shape[0] // pieces
    copies = [pltpu.make_async_copy(basis_far, basis, sems.at[pieces])]
    for i in range(pieces):
        part = pl.ds(i * rows, rows)
        copies.append(pltpu.make_async_copy(inverse_far.at[part], inverse.at[part], sems.at[i]))
    copies.append(pltpu.make_async_copy(order_far, order, sems.at[pieces + 1]))
    for copy in copies:
        copy.start()
    copies[0].wait()
    basis_parts = split(basis[...])
    across = basis[...].T
    basis_t[...] = across
    across = split(across)
    for i in range(pieces):
        part = slice(i * rows, (i + 1) * rows)
        copies[i + 1].wait()
        block = split(inverse[part])
        top[part], low[part] = block
        carried[part] = mm_parts(block, basis_parts)
    gram[...] = fold(mm_parts(across, split(carried[...])))
    copies[-1].wait()


def leaf_kernel(order, rhs, top, low, basis_t, solved, projected):
    points = rhs.shape[0]
    wide = 128
    numbers = order[...].astype(F32)
    lanes = lax.broadcasted_iota(jnp.int32, (wide, points), 1).astype(F32)
    gather = []
    for i in range(0, points, wide):
        column = jnp.broadcast_to(numbers[:, i:i + wide], (wide, wide)).T
        column = jnp.concatenate([column] * (points // wide), axis=1)
        gather.append(jnp.where(column == lanes, 1.0, 0.0).astype(BF16))
    ordered = pick(jnp.concatenate(gather, axis=0), rhs[...])
    z = mm_parts((top[...], low[...]), split(ordered))
    solved[...] = z
    projected[...] = mm(basis_t[...], z)


def node_kernel(level, gram, other, precision, *rest):
    coupling = precision[0, level].astype(F32)
    whole = unfold(gram[...] + other[...])
    if len(rest) == 5:
        rest[0][...] = scaled_inverse(coupling + whole, *rest[1:])
        return
    transfer, inverse, mover, gram_out, *work = rest
    mixer = transfer[0, level]
    left = split(mm(mixer, precision[0, level], None, ((0,), (0,))))
    right = split(sum(mm(part.astype(BF16), mixer, None) for part in parts(whole)))
    m = scaled_inverse(coupling + whole, *work)
    n = mm_parts(left, split(m))
    inverse[...] = m
    mover[...] = n
    gram_out[...] = fold(mm_parts(split(n), right))


def lift_kernel(first, last, *refs):
    refs = list(refs)
    projected, other, inverse, mover = (refs.pop(0)[...] for _ in range(4))
    s = projected + other
    alpha = mm(inverse, s)
    outs = refs[-5:] if first and not last else refs[-3:]
    outs[0][...] = mm(mover, s)
    if first:
        order, solved, carried = (refs.pop(0)[...] for _ in range(3))
        points = solved.shape[0]
        rows = lax.broadcasted_iota(jnp.int32, (points, points), 0)
        scatter = jnp.where(order == rows, 1.0, 0.0).astype(BF16)
        solved, carried = pick(scatter, solved), pick(scatter, carried)
        total, mixing = alpha, mover.T
    else:
        total, mixing, solved, carried = (refs.pop(0)[...] for _ in range(4))
        total = total + mm(mixing, alpha)
        mixing = mm(mixing, mover, HIGH, ((1,), (1,)))
    if last:
        total = solved - mm(carried, total)
        mixing = mm(carried, mixing)
    outs[1][...] = total
    outs[2][...] = mixing
    if first and not last:
        outs[3][...] = solved
        outs[4][...] = carried


def root_kernel(pieces, projected, other, inverse, solved, carried, out_far, out, sems):
    alpha = split(mm_parts(split(inverse[...]), split(projected[...] + other[...])))
    rows = out.shape[0] // pieces
    copies = []
    for i in range(pieces):
        part = pl.ds(i * rows, rows)
        out[part] = solved[part] - mm_parts(split(carried[part]), alpha)
        copies.append(pltpu.make_async_copy(out.at[part], out_far.at[part], sems.at[i]))
        copies[-1].start()
    for copy in copies:
        copy.wait()


def call(kernel, outs, *args, scratch=(), work=0, place=VMEM, result=VMEM):
    if place is FAR:
        args = [pltpu.with_memory_space_constraint(arg, pltpu.HBM) for arg in args]
    return pl.pallas_call(
        kernel,
        out_shape=[jax.ShapeDtypeStruct(getattr(out, "shape", out), getattr(out, "dtype", F32)) for out in outs],
        in_specs=[place] * len(args),
        out_specs=[result] * len(outs),
        scratch_shapes=scratch,
        cost_estimate=pl.CostEstimate(flops=work, bytes_accessed=0, transcendentals=0),
        compiler_params=PARAMS,
    )(*args)


def from_partner(block, axis, apart):
    count = lax.axis_size(axis)
    return lax.ppermute(block, axis, [(i, i ^ 1 << apart) for i in range(count)])


def body(rhs, order, inverse, basis, transfer, precision):
    points, columns = rhs.shape
    rank = basis.shape[1]
    square, tall, block = (rank, rank), (points, rank), (rank, columns)
    folded = (rank // 2 + SUB, rank)
    levels = lax.axis_size("leaf").bit_length() - 1
    pieces = 2
    half = jax.ShapeDtypeStruct(inverse.shape, BF16)
    top, low, basis_t, order, carried, gram = call(
        functools.partial(basis_kernel, pieces), [half, half, (rank, points), order, tall, folded],
        inverse, basis, order, place=FAR, work=GIGA,
        scratch=[pltpu.VMEM(inverse.shape, F32), pltpu.VMEM(tall, F32), pltpu.SemaphoreType.DMA((pieces + 2,))]
    )
    other_gram = from_partner(gram, "leaf", 0)
    solved, projected = call(leaf_kernel, [rhs, block], order, rhs, top, low, basis_t, work=2 * GIGA)
    if levels == 1:
        raise NotImplementedError("one level")
    state = [order, solved, carried]
    for k in range(levels - 1):
        other = from_partner(projected, "leaf", k)
        m, n, gram = call(
            functools.partial(node_kernel, k), [square, square, folded], gram, other_gram, precision, transfer,
            scratch=invert_scratch(rank), work=6 * GIGA
        )
        other_gram = from_partner(gram, "leaf", k + 1)
        first, last = k == 0, k == levels - 2
        outs = [rhs, tall] if last else [block, square, rhs, tall] if first else [block, square]
        projected, *new = call(
            functools.partial(lift_kernel, first, last), [block] + outs, projected, other, m, n, *state, work=GIGA
        )
        state = new + state[len(new):]
    solved, carried = state[:2]
    k = levels - 1
    other = from_partner(projected, "leaf", k)
    (m,) = call(functools.partial(node_kernel, k), [square], gram, other_gram, precision, scratch=invert_scratch(rank), work=6 * GIGA)
    (out,) = call(
        functools.partial(root_kernel, 2 * pieces), [rhs], projected, other, m, solved, carried, work=GIGA, result=FAR,
        scratch=[pltpu.VMEM(rhs.shape, F32), pltpu.SemaphoreType.DMA((2 * pieces,))]
    )
    return out


def solution(mesh):
    placed = (
        P("leaf", "rhs"),
        P("leaf", None),
        P("leaf", None),
        P("leaf", None),
        P("leaf", None, None, None),
        P("leaf", None, None, None),
    )
    return jax.shard_map(
        body, mesh=mesh, in_specs=placed, out_specs=P("leaf", "rhs"), check_vma=False
    )
```

```python
import functools

import jax
import jax.numpy as jnp
from jax import lax
from jax.experimental import pallas as pl
from jax.experimental.pallas import tpu as pltpu
from jax.sharding import PartitionSpec as P

F32 = jnp.float32
BF16 = jnp.bfloat16
HIGH = lax.Precision.HIGH
SUB = 8
GIGA = 10 ** 9
VMEM = pl.BlockSpec(memory_space=pltpu.VMEM)
FAR = pl.BlockSpec(memory_space=pltpu.HBM)
PARAMS = pltpu.CompilerParams(vmem_limit_bytes=32 * 1024 * 1024)


def mm(a, b, precision=HIGH, dims=((1,), (0,))):
    return lax.dot_general(a, b, (dims, ((), ())), precision=precision, preferred_element_type=F32)


def split(x):
    top = x.astype(BF16)
    return top, (x - top.astype(F32)).astype(BF16)


def mm_parts(a, b):
    columns = b[0].shape[1]
    both = jnp.dot(a[0], jnp.concatenate(b, axis=1), preferred_element_type=F32)
    return both[:, :columns] + (both[:, columns:] + jnp.dot(a[1], b[0], preferred_element_type=F32))


def pick(mask, x):
    top, low = split(x)
    one = lambda part: lax.dot_general(mask, part, (((1,), (0,)), ((), ())), preferred_element_type=F32)
    return one(top) + one(low)


def reciprocal(x):
    return pltpu.reciprocal(x, approx=True)

def parts(x):
    top = x.astype(BF16).astype(F32)
    rest = x - top
    mid = rest.astype(BF16).astype(F32)
    return top, mid, rest - mid

def spread(x, k):
    return jnp.broadcast_to(x[:, k:k + 1], x.shape)


def four(x, y, cols, at, k, lane, row, hold, other, later):
    size = x.shape[1]
    across = size // SUB * SUB
    inside = (lane >= k) & (lane < k + 4)
    own = (row >= at) & (row < at + 4)
    ahead = [(k + 4 + j) % across for j in range(4)]
    for j in range(4):
        hold[0, j * SUB:(j + 1) * SUB] = cols[j]
    line = lambda j, i: hold[0, pl.ds(j * SUB + at + i, SUB, stride=0)]
    a0, a1, a2 = line(0, 0), line(1, 0), line(1, 1)
    b00, b01, b10, b11 = line(0, 2), line(1, 2), line(0, 3), line(1, 3)
    c0, c1, c2 = line(2, 2), line(3, 2), line(3, 3)
    later[0, 0:SUB] = x
    coming = [spread(x, a) for a in ahead]
    for j in range(4):
        other[0, j * SUB:(j + 1) * SUB] = coming[j]
    down = [spread(y, k + j) for j in range(4)]
    side = lambda j, i: other[0, pl.ds(j * SUB + at + i, SUB, stride=0)]
    old = lambda i: later[0, pl.ds(at + i, SUB, stride=0)]
    det = a0 * a2 - a1 * a1
    g00, g01 = b00 * a2 - b01 * a1, b01 * a0 - b00 * a1
    g10, g11 = b10 * a2 - b11 * a1, b11 * a0 - b10 * a1
    s0 = det * c0 - (g00 * b00 + g01 * b01)
    s1 = det * c1 - (g00 * b10 + g01 * b11)
    s2 = det * c2 - (g10 * b10 + g11 * b11)
    rs = reciprocal(s0 * s2 - s1 * s1)
    ra = reciprocal(det)

    def known(e):
        t2 = det * e[2] - (g00 * e[0] + g01 * e[1])
        t3 = det * e[3] - (g10 * e[0] + g11 * e[1])
        return a2 * e[0] - a1 * e[1], a0 * e[1] - a1 * e[0], s2 * t2 - s1 * t3, s0 * t3 - s1 * t2

    def second(c):
        return c[0], c[1], c[2] - (c[0] * g00 + c[1] * g01) * ra, c[3] - (c[0] * g10 + c[1] * g11) * ra

    def less(base, c, v):
        return (base - (c[0] * v[0] + c[1] * v[1]) * ra) - (c[2] * v[2] + c[3] * v[3]) * rs

    cols = second([jnp.where(own, jnp.where(row == at + j, -1.0, 0.0), cols[j]) for j in range(4)])
    down = second(down)
    there = [known([side(j, i) for i in range(4)]) for j in range(4)]
    if at + 4 < SUB:
        after = [less(jnp.where(own, 0.0, coming[j]), cols, there[j]) for j in range(4)]
    else:
        after = [less(spread(y, ahead[j]), down, there[j]) for j in range(4)]
    here = known([jnp.where(inside, jnp.where(lane == k + j, 1.0, 0.0), old(j)) for j in range(4)])
    x = less(jnp.where(inside | own, 0.0, x), cols, here)
    y = less(jnp.where(inside, 0.0, y), down, here)
    return x, y, after


def invert(m, xt, w6, *rooms):
    size = m.shape[0]
    lane = lax.broadcasted_iota(jnp.int32, (SUB, size), 1)
    row = lax.broadcasted_iota(jnp.int32, (SUB, size), 0)
    wide = lax.broadcasted_iota(jnp.int32, (size, size), 1)
    eye = jnp.where(wide == lax.broadcasted_iota(jnp.int32, (size, size), 0), 1.0, 0.0).astype(BF16)
    count = size // SUB

    def trail(t):
        k = t * SUB
        u = jnp.dot(xt[...], w6[...], preferred_element_type=F32)
        new = jnp.where((wide >= k) & (wide < k + SUB), 0.0, m[...]) - u
        m[...] = new
        return new

    def step(t, carry):
        x, *cols = carry
        k = t * SUB
        after = (t + 1) % count * SUB
        y = trail(t - 1)[after:after + SUB] if t else m[SUB:2 * SUB]
        z = jnp.where(lane < k, -1.0, 1.0) * x
        z = jnp.where((lane >= k) & (lane < k + SUB), jnp.where(lane - k == row, -1.0, 0.0), z)
        h, n, l = parts(z)
        z = jnp.concatenate([h, h, n, n, h, l], axis=0).astype(BF16)
        xt[...] = lax.dot_general(eye, z, (((1,), (1,)), ((), ())), preferred_element_type=F32).astype(BF16)
        for g in range(0, SUB, 4):
            x, y, cols = four(x, y, cols, g, k + g, lane, row, *(room.at[pl.ds(g // 4, 1)] for room in rooms))
        h, n, l = parts(x)
        w6[...] = jnp.concatenate([h, n, h, n, l, h], axis=0).astype(BF16)
        m[pl.ds(k, SUB)] = jnp.zeros((SUB, size), F32)
        return y, *cols

    x = m[0:SUB]
    carry = (x, *(spread(x, j) for j in range(4)))
    for t in range(count):
        carry = step(t, carry)
    trail(count - 1)


def invert_scratch(size):
    return [
        pltpu.VMEM((size, size), F32), pltpu.VMEM((size, 6 * SUB), BF16), pltpu.VMEM((6 * SUB, size), BF16),
        *(pltpu.VMEM((SUB // 4, tiles * SUB, size), F32) for tiles in (5, 5, 2)),
    ]


def scaled_inverse(matrix, *work):
    size = matrix.shape[0]
    rows = lax.broadcasted_iota(jnp.int32, (size, size), 0)
    cols = lax.broadcasted_iota(jnp.int32, (size, size), 1)
    diagonal = jnp.where(rows == cols, matrix, 0.0)
    down = lax.rsqrt(jnp.sum(diagonal, axis=1, keepdims=True))
    across = lax.rsqrt(jnp.sum(diagonal, axis=0, keepdims=True))
    work[0][...] = matrix * down * across
    invert(*work)
    return work[0][...] * down * across


def fold(gram):
    size = gram.shape[0]
    half = size // 2
    rows = lax.broadcasted_iota(jnp.int32, (half, size), 0)
    cols = lax.broadcasted_iota(jnp.int32, (half, size), 1)
    low = gram[half:]
    body = jnp.where(cols < rows, pltpu.roll(low, half, 1), gram[:half])
    diagonal = jnp.sum(jnp.where(cols == rows + half, low, 0.0), axis=0, keepdims=True)
    return jnp.concatenate([body, jnp.where(rows[:SUB] == 0, diagonal, 0.0)], axis=0)


def unfold(folded):
    size = folded.shape[1]
    half = size // 2
    rows = lax.broadcasted_iota(jnp.int32, (size, size), 0)
    cols = lax.broadcasted_iota(jnp.int32, (size, size), 1)
    body = folded[:half]
    below = cols[:half] < rows[:half]
    low = pltpu.roll(jnp.where(below, body, 0.0), half, 1)
    low = jnp.where(cols[:half] == rows[:half] + half, folded[half:half + 1], low)
    upper = jnp.concatenate([jnp.where(below, 0.0, body), low], axis=0)
    return upper + jnp.where(rows == cols, 0.0, upper.T)


def basis_kernel(pieces, inverse_far, basis_far, order_far, top, low, basis_t, order, carried, gram, inverse, basis, sems):
    rows = inverse.shape[0] // pieces
    copies = [pltpu.make_async_copy(basis_far, basis, sems.at[pieces])]
    for i in range(pieces):
        part = pl.ds(i * rows, rows)
        copies.append(pltpu.make_async_copy(inverse_far.at[part], inverse.at[part], sems.at[i]))
    copies.append(pltpu.make_async_copy(order_far, order, sems.at[pieces + 1]))
    for copy in copies:
        copy.start()
    copies[0].wait()
    basis_parts = split(basis[...])
    across = basis[...].T
    basis_t[...] = across
    across = split(across)
    for i in range(pieces):
        part = slice(i * rows, (i + 1) * rows)
        copies[i + 1].wait()
        block = split(inverse[part])
        top[part], low[part] = block
        carried[part] = mm_parts(block, basis_parts)
    gram[...] = fold(mm_parts(across, split(carried[...])))
    copies[-1].wait()


def leaf_kernel(order, rhs, top, low, basis_t, solved, projected):
    points = rhs.shape[0]
    wide = 128
    numbers = order[...].astype(F32)
    lanes = lax.broadcasted_iota(jnp.int32, (wide, points), 1).astype(F32)
    gather = []
    for i in range(0, points, wide):
        column = jnp.broadcast_to(numbers[:, i:i + wide], (wide, wide)).T
        column = jnp.concatenate([column] * (points // wide), axis=1)
        gather.append(jnp.where(column == lanes, 1.0, 0.0).astype(BF16))
    ordered = pick(jnp.concatenate(gather, axis=0), rhs[...])
    z = mm_parts((top[...], low[...]), split(ordered))
    solved[...] = z
    projected[...] = mm(basis_t[...], z)


def node_kernel(level, gram, other, precision, *rest):
    coupling = precision[0, level].astype(F32)
    whole = unfold(gram[...] + other[...])
    if len(rest) == 7:
        rest[0][...] = scaled_inverse(coupling + whole, *rest[1:])
        return
    transfer, inverse, mover, gram_out, *work = rest
    mixer = transfer[0, level]
    left = split(mm(mixer, precision[0, level], None, ((0,), (0,))))
    right = split(sum(mm(part.astype(BF16), mixer, None) for part in parts(whole)))
    m = scaled_inverse(coupling + whole, *work)
    n = mm_parts(left, split(m))
    inverse[...] = m
    mover[...] = n
    gram_out[...] = fold(mm_parts(split(n), right))


def lift_kernel(first, last, *refs):
    refs = list(refs)
    projected, other, inverse, mover = (refs.pop(0)[...] for _ in range(4))
    s = projected + other
    alpha = mm(inverse, s)
    outs = refs[-5:] if first and not last else refs[-3:]
    outs[0][...] = mm(mover, s)
    if first:
        order, solved, carried = (refs.pop(0)[...] for _ in range(3))
        points = solved.shape[0]
        rows = lax.broadcasted_iota(jnp.int32, (points, points), 0)
        scatter = jnp.where(order == rows, 1.0, 0.0).astype(BF16)
        solved, carried = pick(scatter, solved), pick(scatter, carried)
        total, mixing = alpha, mover.T
    else:
        total, mixing, solved, carried = (refs.pop(0)[...] for _ in range(4))
        total = total + mm(mixing, alpha)
        mixing = mm(mixing, mover, HIGH, ((1,), (1,)))
    if last:
        total = solved - mm(carried, total)
        mixing = mm(carried, mixing)
    outs[1][...] = total
    outs[2][...] = mixing
    if first and not last:
        outs[3][...] = solved
        outs[4][...] = carried


def root_kernel(pieces, projected, other, inverse, solved, carried, out_far, out, sems):
    alpha = split(mm_parts(split(inverse[...]), split(projected[...] + other[...])))
    rows = out.shape[0] // pieces
    copies = []
    for i in range(pieces):
        part = pl.ds(i * rows, rows)
        out[part] = solved[part] - mm_parts(split(carried[part]), alpha)
        copies.append(pltpu.make_async_copy(out.at[part], out_far.at[part], sems.at[i]))
        copies[-1].start()
    for copy in copies:
        copy.wait()


def call(kernel, outs, *args, scratch=(), work=0, place=VMEM, result=VMEM):
    if place is FAR:
        args = [pltpu.with_memory_space_constraint(arg, pltpu.HBM) for arg in args]
    return pl.pallas_call(
        kernel,
        out_shape=[jax.ShapeDtypeStruct(getattr(out, "shape", out), getattr(out, "dtype", F32)) for out in outs],
        in_specs=[place] * len(args),
        out_specs=[result] * len(outs),
        scratch_shapes=scratch,
        cost_estimate=pl.CostEstimate(flops=work, bytes_accessed=0, transcendentals=0),
        compiler_params=PARAMS,
    )(*args)


def from_partner(block, axis, apart):
    count = lax.axis_size(axis)
    return lax.ppermute(block, axis, [(i, i ^ 1 << apart) for i in range(count)])


def body(rhs, order, inverse, basis, transfer, precision):
    points, columns = rhs.shape
    rank = basis.shape[1]
    square, tall, block = (rank, rank), (points, rank), (rank, columns)
    folded = (rank // 2 + SUB, rank)
    levels = lax.axis_size("leaf").bit_length() - 1
    pieces = 2
    half = jax.ShapeDtypeStruct(inverse.shape, BF16)
    top, low, basis_t, order, carried, gram = call(
        functools.partial(basis_kernel, pieces), [half, half, (rank, points), order, tall, folded],
        inverse, basis, order, place=FAR, work=GIGA,
        scratch=[pltpu.VMEM(inverse.shape, F32), pltpu.VMEM(tall, F32), pltpu.SemaphoreType.DMA((pieces + 2,))]
    )
    other_gram = from_partner(gram, "leaf", 0)
    solved, projected = call(leaf_kernel, [rhs, block], order, rhs, top, low, basis_t, work=2 * GIGA)
    if levels == 1:
        raise NotImplementedError("one level")
    state = [order, solved, carried]
    for k in range(levels - 1):
        other = from_partner(projected, "leaf", k)
        m, n, gram = call(
            functools.partial(node_kernel, k), [square, square, folded], gram, other_gram, precision, transfer,
            scratch=invert_scratch(rank), work=6 * GIGA
        )
        other_gram = from_partner(gram, "leaf", k + 1)
        first, last = k == 0, k == levels - 2
        outs = [rhs, tall] if last else [block, square, rhs, tall] if first else [block, square]
        projected, *new = call(
            functools.partial(lift_kernel, first, last), [block] + outs, projected, other, m, n, *state, work=GIGA
        )
        state = new + state[len(new):]
    solved, carried = state[:2]
    k = levels - 1
    other = from_partner(projected, "leaf", k)
    (m,) = call(functools.partial(node_kernel, k), [square], gram, other_gram, precision, scratch=invert_scratch(rank), work=6 * GIGA)
    (out,) = call(
        functools.partial(root_kernel, 2 * pieces), [rhs], projected, other, m, solved, carried, work=GIGA, result=FAR,
        scratch=[pltpu.VMEM(rhs.shape, F32), pltpu.SemaphoreType.DMA((2 * pieces,))]
    )
    return out


def solution(mesh):
    placed = (
        P("leaf", "rhs"),
        P("leaf", None),
        P("leaf", None),
        P("leaf", None),
        P("leaf", None, None, None),
        P("leaf", None, None, None),
    )
    return jax.shard_map(
        body, mesh=mesh, in_specs=placed, out_specs=P("leaf", "rhs"), check_vma=False
    )
```

```python
import functools

import jax
import jax.numpy as jnp
from jax import lax
from jax.experimental import pallas as pl
from jax.experimental.pallas import tpu as pltpu
from jax.sharding import PartitionSpec as P

F32 = jnp.float32
BF16 = jnp.bfloat16
HIGH = lax.Precision.HIGH
SUB = 8
GIGA = 10 ** 9
VMEM = pl.BlockSpec(memory_space=pltpu.VMEM)
FAR = pl.BlockSpec(memory_space=pltpu.HBM)
PARAMS = pltpu.CompilerParams(vmem_limit_bytes=32 * 1024 * 1024)


def mm(a, b, precision=HIGH, dims=((1,), (0,))):
    return lax.dot_general(a, b, (dims, ((), ())), precision=precision, preferred_element_type=F32)


def split(x):
    top = x.astype(BF16)
    return top, (x - top.astype(F32)).astype(BF16)


def mm_parts(a, b):
    columns = b[0].shape[1]
    both = jnp.dot(a[0], jnp.concatenate(b, axis=1), preferred_element_type=F32)
    return both[:, :columns] + (both[:, columns:] + jnp.dot(a[1], b[0], preferred_element_type=F32))


def pick(mask, x):
    top, low = split(x)
    one = lambda part: lax.dot_general(mask, part, (((1,), (0,)), ((), ())), preferred_element_type=F32)
    return one(top) + one(low)


def reciprocal(x):
    return pltpu.reciprocal(x, approx=True)

def parts(x):
    top = x.astype(BF16).astype(F32)
    rest = x - top
    mid = rest.astype(BF16).astype(F32)
    return top, mid, rest - mid

def spread(x, k):
    return jnp.broadcast_to(x[:, k:k + 1], x.shape)


def four(x, y, cols, at, k, lane, row, hold, other, later):
    size = x.shape[1]
    across = size // SUB * SUB
    inside = (lane >= k) & (lane < k + 4)
    own = (row >= at) & (row < at + 4)
    ahead = [(k + 4 + j) % across for j in range(4)]
    for j in range(4):
        hold[0, j * SUB:(j + 1) * SUB] = cols[j]
    line = lambda j, i: hold[0, pl.ds(j * SUB + at + i, SUB, stride=0)]
    a0, a1, a2 = line(0, 0), line(1, 0), line(1, 1)
    b00, b01, b10, b11 = line(0, 2), line(1, 2), line(0, 3), line(1, 3)
    c0, c1, c2 = line(2, 2), line(3, 2), line(3, 3)
    later[0, 0:SUB] = x
    coming = [spread(x, a) for a in ahead]
    for j in range(4):
        other[0, j * SUB:(j + 1) * SUB] = coming[j]
    down = [spread(y, k + j) for j in range(4)]
    side = lambda j, i: other[0, pl.ds(j * SUB + at + i, SUB, stride=0)]
    old = lambda i: later[0, pl.ds(at + i, SUB, stride=0)]
    det = a0 * a2 - a1 * a1
    g00, g01 = b00 * a2 - b01 * a1, b01 * a0 - b00 * a1
    g10, g11 = b10 * a2 - b11 * a1, b11 * a0 - b10 * a1
    s0 = det * c0 - (g00 * b00 + g01 * b01)
    s1 = det * c1 - (g00 * b10 + g01 * b11)
    s2 = det * c2 - (g10 * b10 + g11 * b11)
    rs = reciprocal(s0 * s2 - s1 * s1)
    ra = reciprocal(det)

    def known(e):
        t2 = det * e[2] - (g00 * e[0] + g01 * e[1])
        t3 = det * e[3] - (g10 * e[0] + g11 * e[1])
        return a2 * e[0] - a1 * e[1], a0 * e[1] - a1 * e[0], s2 * t2 - s1 * t3, s0 * t3 - s1 * t2

    def second(c):
        return c[0], c[1], c[2] - (c[0] * g00 + c[1] * g01) * ra, c[3] - (c[0] * g10 + c[1] * g11) * ra

    def less(base, c, v):
        return (base - (c[0] * v[0] + c[1] * v[1]) * ra) - (c[2] * v[2] + c[3] * v[3]) * rs

    cols = second([jnp.where(own, jnp.where(row == at + j, -1.0, 0.0), cols[j]) for j in range(4)])
    down = second(down)
    there = [known([side(j, i) for i in range(4)]) for j in range(4)]
    if at + 4 < SUB:
        after = [less(jnp.where(own, 0.0, coming[j]), cols, there[j]) for j in range(4)]
    else:
        after = [less(spread(y, ahead[j]), down, there[j]) for j in range(4)]
    here = known([jnp.where(inside, jnp.where(lane == k + j, 1.0, 0.0), old(j)) for j in range(4)])
    x = less(jnp.where(inside | own, 0.0, x), cols, here)
    y = less(jnp.where(inside, 0.0, y), down, here)
    return x, y, after


def invert(m, xt, w6, *rooms):
    size = m.shape[0]
    lane = lax.broadcasted_iota(jnp.int32, (SUB, size), 1)
    row = lax.broadcasted_iota(jnp.int32, (SUB, size), 0)
    wide = lax.broadcasted_iota(jnp.int32, (size, size), 1)
    eye = jnp.where(wide == lax.broadcasted_iota(jnp.int32, (size, size), 0), 1.0, 0.0).astype(BF16)
    count = size // SUB

    def trail(t):
        k = t * SUB
        u = jnp.dot(xt[...], w6[...], preferred_element_type=F32)
        new = jnp.where((wide >= k) & (wide < k + SUB), 0.0, m[...]) - u
        m[...] = new
        return new

    def step(t, carry):
        x, *cols = carry
        k = t * SUB
        after = (t + 1) % count * SUB
        y = trail(t - 1)[after:after + SUB] if t else m[SUB:2 * SUB]
        z = jnp.where(lane < k, -1.0, 1.0) * x
        z = jnp.where((lane >= k) & (lane < k + SUB), jnp.where(lane - k == row, -1.0, 0.0), z)
        h, n, l = parts(z)
        z = jnp.concatenate([h, h, n, n, h, l], axis=0).astype(BF16)
        xt[...] = lax.dot_general(eye, z, (((1,), (1,)), ((), ())), preferred_element_type=F32).astype(BF16)
        for g in range(0, SUB, 4):
            x, y, cols = four(x, y, cols, g, k + g, lane, row, *(room.at[pl.ds(g // 4, 1)] for room in rooms))
        h, n, l = parts(x)
        w6[...] = jnp.concatenate([h, n, h, n, l, h], axis=0).astype(BF16)
        m[pl.ds(k, SUB)] = jnp.zeros((SUB, size), F32)
        return y, *cols

    x = m[0:SUB]
    carry = (x, *(spread(x, j) for j in range(4)))
    for t in range(count):
        carry = step(t, carry)
    trail(count - 1)


def invert_scratch(size):
    return [
        pltpu.VMEM((size, size), F32), pltpu.VMEM((size, 6 * SUB), BF16), pltpu.VMEM((6 * SUB, size), BF16),
        *(pltpu.VMEM((SUB // 4, tiles * SUB, size), F32) for tiles in (5, 5, 2)),
    ]


def scaled_inverse(matrix, *work):
    size = matrix.shape[0]
    rows = lax.broadcasted_iota(jnp.int32, (size, size), 0)
    cols = lax.broadcasted_iota(jnp.int32, (size, size), 1)
    diagonal = jnp.where(rows == cols, matrix, 0.0)
    down = lax.rsqrt(jnp.sum(diagonal, axis=1, keepdims=True))
    across = lax.rsqrt(jnp.sum(diagonal, axis=0, keepdims=True))
    work[0][...] = matrix * down * across
    invert(*work)
    return work[0][...] * down * across


def fold(gram):
    size = gram.shape[0]
    half = size // 2
    rows = lax.broadcasted_iota(jnp.int32, (half, size), 0)
    cols = lax.broadcasted_iota(jnp.int32, (half, size), 1)
    low = gram[half:]
    body = jnp.where(cols < rows, pltpu.roll(low, half, 1), gram[:half])
    diagonal = jnp.sum(jnp.where(cols == rows + half, low, 0.0), axis=0, keepdims=True)
    return jnp.concatenate([body, jnp.where(rows[:SUB] == 0, diagonal, 0.0)], axis=0)


def unfold(folded):
    size = folded.shape[1]
    half = size // 2
    rows = lax.broadcasted_iota(jnp.int32, (size, size), 0)
    cols = lax.broadcasted_iota(jnp.int32, (size, size), 1)
    body = folded[:half]
    below = cols[:half] < rows[:half]
    low = pltpu.roll(jnp.where(below, body, 0.0), half, 1)
    low = jnp.where(cols[:half] == rows[:half] + half, folded[half:half + 1], low)
    upper = jnp.concatenate([jnp.where(below, 0.0, body), low], axis=0)
    return upper + jnp.where(rows == cols, 0.0, upper.T)


def basis_kernel(pieces, inverse_far, basis_far, order_far, top, low, basis_t, order, carried, gram, inverse, basis, sems):
    rows = inverse.shape[0] // pieces
    copies = [pltpu.make_async_copy(basis_far, basis, sems.at[pieces])]
    for i in range(pieces):
        part = pl.ds(i * rows, rows)
        copies.append(pltpu.make_async_copy(inverse_far.at[part], inverse.at[part], sems.at[i]))
    copies.append(pltpu.make_async_copy(order_far, order, sems.at[pieces + 1]))
    for copy in copies:
        copy.start()
    copies[0].wait()
    basis_parts = split(basis[...])
    across = basis[...].T
    basis_t[...] = across
    across = split(across)
    for i in range(pieces):
        part = slice(i * rows, (i + 1) * rows)
        copies[i + 1].wait()
        block = split(inverse[part])
        top[part], low[part] = block
        carried[part] = mm_parts(block, basis_parts)
    gram[...] = fold(mm_parts(across, split(carried[...])))
    copies[-1].wait()


def leaf_kernel(order, rhs, top, low, basis_t, solved, projected):
    points = rhs.shape[0]
    wide = 128
    numbers = order[...].astype(F32)
    lanes = lax.broadcasted_iota(jnp.int32, (wide, points), 1).astype(F32)
    gather = []
    for i in range(0, points, wide):
        column = jnp.broadcast_to(numbers[:, i:i + wide], (wide, wide)).T
        column = jnp.concatenate([column] * (points // wide), axis=1)
        gather.append(jnp.where(column == lanes, 1.0, 0.0).astype(BF16))
    ordered = pick(jnp.concatenate(gather, axis=0), rhs[...])
    z = mm_parts((top[...], low[...]), split(ordered))
    solved[...] = z
    projected[...] = mm(basis_t[...], z)


def node_kernel(level, gram, other, precision, *rest):
    coupling = precision[0, level].astype(F32)
    whole = unfold(gram[...] + other[...])
    if len(rest) == 7:
        rest[0][...] = scaled_inverse(coupling + whole, *rest[1:])
        return
    transfer, inverse, mover, gram_out, *work = rest
    mixer = transfer[0, level]
    left = split(mm(mixer, precision[0, level], None, ((0,), (0,))))
    right = split(sum(mm(part.astype(BF16), mixer, None) for part in parts(whole)))
    m = scaled_inverse(coupling + whole, *work)
    n = mm_parts(left, split(m))
    inverse[...] = m
    mover[...] = n
    gram_out[...] = fold(mm_parts(split(n), right))


def lift_kernel(first, last, *refs):
    refs = list(refs)
    projected, other, inverse, mover = (refs.pop(0)[...] for _ in range(4))
    s = projected + other
    alpha = mm(inverse, s)
    outs = refs[-5:] if first and not last else refs[-3:]
    outs[0][...] = mm(mover, s)
    if first:
        order, solved, carried = (refs.pop(0)[...] for _ in range(3))
        points = solved.shape[0]
        rows = lax.broadcasted_iota(jnp.int32, (points, points), 0)
        scatter = jnp.where(order == rows, 1.0, 0.0).astype(BF16)
        solved, carried = pick(scatter, solved), pick(scatter, carried)
        total, mixing = alpha, mover.T
    else:
        total, mixing, solved, carried = (refs.pop(0)[...] for _ in range(4))
        total = total + mm(mixing, alpha)
        mixing = mm(mixing, mover, HIGH, ((1,), (1,)))
    if last:
        total = solved - mm(carried, total)
        mixing = mm(carried, mixing)
    outs[1][...] = total
    outs[2][...] = mixing
    if first and not last:
        outs[3][...] = solved
        outs[4][...] = carried


def root_kernel(pieces, projected, other, inverse, solved, carried, out_far, out, sems):
    alpha = split(mm_parts(split(inverse[...]), split(projected[...] + other[...])))
    rows = out.shape[0] // pieces
    copies = []
    for i in range(pieces):
        part = pl.ds(i * rows, rows)
        out[part] = solved[part] - mm_parts(split(carried[part]), alpha)
        copies.append(pltpu.make_async_copy(out.at[part], out_far.at[part], sems.at[i]))
        copies[-1].start()
    for copy in copies:
        copy.wait()


def call(kernel, outs, *args, scratch=(), work=0, place=VMEM, result=VMEM):
    if place is FAR:
        args = [pltpu.with_memory_space_constraint(arg, pltpu.HBM) for arg in args]
    return pl.pallas_call(
        kernel,
        out_shape=[jax.ShapeDtypeStruct(getattr(out, "shape", out), getattr(out, "dtype", F32)) for out in outs],
        in_specs=[place] * len(args),
        out_specs=[result] * len(outs),
        scratch_shapes=scratch,
        cost_estimate=pl.CostEstimate(flops=work, bytes_accessed=0, transcendentals=0),
        compiler_params=PARAMS,
    )(*args)


def from_partner(block, axis, apart):
    count = lax.axis_size(axis)
    return lax.ppermute(block, axis, [(i, i ^ 1 << apart) for i in range(count)])


def body(rhs, order, inverse, basis, transfer, precision):
    points, columns = rhs.shape
    rank = basis.shape[1]
    square, tall, block = (rank, rank), (points, rank), (rank, columns)
    folded = (rank // 2 + SUB, rank)
    levels = lax.axis_size("leaf").bit_length() - 1
    pieces = 4
    half = jax.ShapeDtypeStruct(inverse.shape, BF16)
    top, low, basis_t, order, carried, gram = call(
        functools.partial(basis_kernel, pieces), [half, half, (rank, points), order, tall, folded],
        inverse, basis, order, place=FAR, work=GIGA,
        scratch=[pltpu.VMEM(inverse.shape, F32), pltpu.VMEM(tall, F32), pltpu.SemaphoreType.DMA((pieces + 2,))]
    )
    other_gram = from_partner(gram, "leaf", 0)
    solved, projected = call(leaf_kernel, [rhs, block], order, rhs, top, low, basis_t, work=2 * GIGA)
    if levels == 1:
        raise NotImplementedError("one level")
    state = [order, solved, carried]
    for k in range(levels - 1):
        other = from_partner(projected, "leaf", k)
        m, n, gram = call(
            functools.partial(node_kernel, k), [square, square, folded], gram, other_gram, precision, transfer,
            scratch=invert_scratch(rank), work=6 * GIGA
        )
        other_gram = from_partner(gram, "leaf", k + 1)
        first, last = k == 0, k == levels - 2
        outs = [rhs, tall] if last else [block, square, rhs, tall] if first else [block, square]
        projected, *new = call(
            functools.partial(lift_kernel, first, last), [block] + outs, projected, other, m, n, *state, work=GIGA
        )
        state = new + state[len(new):]
    solved, carried = state[:2]
    k = levels - 1
    other = from_partner(projected, "leaf", k)
    (m,) = call(functools.partial(node_kernel, k), [square], gram, other_gram, precision, scratch=invert_scratch(rank), work=6 * GIGA)
    (out,) = call(
        functools.partial(root_kernel, pieces), [rhs], projected, other, m, solved, carried, work=GIGA, result=FAR,
        scratch=[pltpu.VMEM(rhs.shape, F32), pltpu.SemaphoreType.DMA((pieces,))]
    )
    return out


def solution(mesh):
    placed = (
        P("leaf", "rhs"),
        P("leaf", None),
        P("leaf", None),
        P("leaf", None),
        P("leaf", None, None, None),
        P("leaf", None, None, None),
    )
    return jax.shard_map(
        body, mesh=mesh, in_specs=placed, out_specs=P("leaf", "rhs"), check_vma=False
    )
```

```python
import functools

import jax
import jax.numpy as jnp
from jax import lax
from jax.experimental import pallas as pl
from jax.experimental.pallas import tpu as pltpu
from jax.sharding import PartitionSpec as P

F32 = jnp.float32
BF16 = jnp.bfloat16
HIGH = lax.Precision.HIGH
SUB = 8
GIGA = 10 ** 9
VMEM = pl.BlockSpec(memory_space=pltpu.VMEM)
FAR = pl.BlockSpec(memory_space=pltpu.HBM)
PARAMS = pltpu.CompilerParams(vmem_limit_bytes=32 * 1024 * 1024)


def mm(a, b, precision=HIGH, dims=((1,), (0,))):
    return lax.dot_general(a, b, (dims, ((), ())), precision=precision, preferred_element_type=F32)


def split(x):
    top = x.astype(BF16)
    return top, (x - top.astype(F32)).astype(BF16)


def mm_parts(a, b):
    columns = b[0].shape[1]
    both = jnp.dot(a[0], jnp.concatenate(b, axis=1), preferred_element_type=F32)
    return both[:, :columns] + (both[:, columns:] + jnp.dot(a[1], b[0], preferred_element_type=F32))


def pick(mask, x):
    top, low = split(x)
    one = lambda part: lax.dot_general(mask, part, (((1,), (0,)), ((), ())), preferred_element_type=F32)
    return one(top) + one(low)


def reciprocal(x):
    return pltpu.reciprocal(x, approx=True)

def parts(x):
    top = x.astype(BF16).astype(F32)
    rest = x - top
    mid = rest.astype(BF16).astype(F32)
    return top, mid, rest - mid

def spread(x, k):
    return jnp.broadcast_to(x[:, k:k + 1], x.shape)


def four(x, y, cols, at, k, lane, row, hold, other, later):
    size = x.shape[1]
    across = size // SUB * SUB
    inside = (lane >= k) & (lane < k + 4)
    own = (row >= at) & (row < at + 4)
    ahead = [(k + 4 + j) % across for j in range(4)]
    for j in range(4):
        hold[0, j * SUB:(j + 1) * SUB] = cols[j]
    line = lambda j, i: hold[0, pl.ds(j * SUB + at + i, SUB, stride=0)]
    a0, a1, a2 = line(0, 0), line(1, 0), line(1, 1)
    b00, b01, b10, b11 = line(0, 2), line(1, 2), line(0, 3), line(1, 3)
    c0, c1, c2 = line(2, 2), line(3, 2), line(3, 3)
    later[0, 0:SUB] = x
    coming = [spread(x, a) for a in ahead]
    for j in range(4):
        other[0, j * SUB:(j + 1) * SUB] = coming[j]
    down = [spread(y, k + j) for j in range(4)]
    side = lambda j, i: other[0, pl.ds(j * SUB + at + i, SUB, stride=0)]
    old = lambda i: later[0, pl.ds(at + i, SUB, stride=0)]
    det = a0 * a2 - a1 * a1
    g00, g01 = b00 * a2 - b01 * a1, b01 * a0 - b00 * a1
    g10, g11 = b10 * a2 - b11 * a1, b11 * a0 - b10 * a1
    s0 = det * c0 - (g00 * b00 + g01 * b01)
    s1 = det * c1 - (g00 * b10 + g01 * b11)
    s2 = det * c2 - (g10 * b10 + g11 * b11)
    rs = reciprocal(s0 * s2 - s1 * s1)
    ra = reciprocal(det)

    def known(e):
        t2 = det * e[2] - (g00 * e[0] + g01 * e[1])
        t3 = det * e[3] - (g10 * e[0] + g11 * e[1])
        return a2 * e[0] - a1 * e[1], a0 * e[1] - a1 * e[0], s2 * t2 - s1 * t3, s0 * t3 - s1 * t2

    def second(c):
        return c[0], c[1], c[2] - (c[0] * g00 + c[1] * g01) * ra, c[3] - (c[0] * g10 + c[1] * g11) * ra

    def less(base, c, v):
        return (base - (c[0] * v[0] + c[1] * v[1]) * ra) - (c[2] * v[2] + c[3] * v[3]) * rs

    cols = second([jnp.where(own, jnp.where(row == at + j, -1.0, 0.0), cols[j]) for j in range(4)])
    down = second(down)
    there = [known([side(j, i) for i in range(4)]) for j in range(4)]
    if at + 4 < SUB:
        after = [less(jnp.where(own, 0.0, coming[j]), cols, there[j]) for j in range(4)]
    else:
        after = [less(spread(y, ahead[j]), down, there[j]) for j in range(4)]
    here = known([jnp.where(inside, jnp.where(lane == k + j, 1.0, 0.0), old(j)) for j in range(4)])
    x = less(jnp.where(inside | own, 0.0, x), cols, here)
    y = less(jnp.where(inside, 0.0, y), down, here)
    return x, y, after


def invert(m, xt, w6, *rooms):
    size = m.shape[0]
    lane = lax.broadcasted_iota(jnp.int32, (SUB, size), 1)
    row = lax.broadcasted_iota(jnp.int32, (SUB, size), 0)
    wide = lax.broadcasted_iota(jnp.int32, (size, size), 1)
    eye = jnp.where(wide == lax.broadcasted_iota(jnp.int32, (size, size), 0), 1.0, 0.0).astype(BF16)
    count = size // SUB

    def trail(t):
        k = t * SUB
        u = jnp.dot(xt[...], w6[...], preferred_element_type=F32)
        new = jnp.where((wide >= k) & (wide < k + SUB), 0.0, m[...]) - u
        m[...] = new
        return new

    def step(t, carry):
        x, *cols = carry
        k = t * SUB
        after = (t + 1) % count * SUB
        y = trail(t - 1)[after:after + SUB] if t else m[SUB:2 * SUB]
        z = jnp.where(lane < k, -1.0, 1.0) * x
        z = jnp.where((lane >= k) & (lane < k + SUB), jnp.where(lane - k == row, -1.0, 0.0), z)
        h, n, l = parts(z)
        z = jnp.concatenate([h, h, n, n, h, l], axis=0).astype(BF16)
        xt[...] = lax.dot_general(eye, z, (((1,), (1,)), ((), ())), preferred_element_type=F32).astype(BF16)
        for g in range(0, SUB, 4):
            x, y, cols = four(x, y, cols, g, k + g, lane, row, *(room.at[pl.ds(g // 4, 1)] for room in rooms))
        h, n, l = parts(x)
        w6[...] = jnp.concatenate([h, n, h, n, l, h], axis=0).astype(BF16)
        m[pl.ds(k, SUB)] = jnp.zeros((SUB, size), F32)
        return y, *cols

    x = m[0:SUB]
    carry = (x, *(spread(x, j) for j in range(4)))
    for t in range(count):
        carry = step(t, carry)
    trail(count - 1)


def invert_scratch(size):
    return [
        pltpu.VMEM((size, size), F32), pltpu.VMEM((size, 6 * SUB), BF16), pltpu.VMEM((6 * SUB, size), BF16),
        *(pltpu.VMEM((SUB // 4, tiles * SUB, size), F32) for tiles in (5, 5, 2)),
    ]


def scaled_inverse(matrix, *work):
    size = matrix.shape[0]
    rows = lax.broadcasted_iota(jnp.int32, (size, size), 0)
    cols = lax.broadcasted_iota(jnp.int32, (size, size), 1)
    diagonal = jnp.where(rows == cols, matrix, 0.0)
    down = lax.rsqrt(jnp.sum(diagonal, axis=1, keepdims=True))
    across = lax.rsqrt(jnp.sum(diagonal, axis=0, keepdims=True))
    work[0][...] = matrix * down * across
    invert(*work)
    return work[0][...] * down * across


def fold(gram):
    size = gram.shape[0]
    half = size // 2
    rows = lax.broadcasted_iota(jnp.int32, (half, size), 0)
    cols = lax.broadcasted_iota(jnp.int32, (half, size), 1)
    low = gram[half:]
    body = jnp.where(cols < rows, pltpu.roll(low, half, 1), gram[:half])
    diagonal = jnp.sum(jnp.where(cols == rows + half, low, 0.0), axis=0, keepdims=True)
    return jnp.concatenate([body, jnp.where(rows[:SUB] == 0, diagonal, 0.0)], axis=0)


def unfold(folded):
    size = folded.shape[1]
    half = size // 2
    rows = lax.broadcasted_iota(jnp.int32, (size, size), 0)
    cols = lax.broadcasted_iota(jnp.int32, (size, size), 1)
    body = folded[:half]
    below = cols[:half] < rows[:half]
    low = pltpu.roll(jnp.where(below, body, 0.0), half, 1)
    low = jnp.where(cols[:half] == rows[:half] + half, folded[half:half + 1], low)
    upper = jnp.concatenate([jnp.where(below, 0.0, body), low], axis=0)
    return upper + jnp.where(rows == cols, 0.0, upper.T)


def basis_kernel(inverse_far, basis_far, order_far, top, low, basis_t, order, carried, gram, inverse, basis, sems):
    pairs = (basis_far, basis), (inverse_far, inverse), (order_far, order)
    copies = [pltpu.make_async_copy(far, near, sems.at[i]) for i, (far, near) in enumerate(pairs)]
    for copy in copies:
        copy.start()
    copies[0].wait()
    basis_parts = split(basis[...])
    across = basis[...].T
    basis_t[...] = across
    across = split(across)
    copies[1].wait()
    block = split(inverse[...])
    top[...], low[...] = block
    q = mm_parts(block, basis_parts)
    carried[...] = q
    gram[...] = fold(mm_parts(across, split(q)))
    copies[2].wait()


def leaf_kernel(order, rhs, top, low, basis_t, solved, projected):
    points = rhs.shape[0]
    wide = 128
    numbers = order[...].astype(F32)
    lanes = lax.broadcasted_iota(jnp.int32, (wide, points), 1).astype(F32)
    gather = []
    for i in range(0, points, wide):
        column = jnp.broadcast_to(numbers[:, i:i + wide], (wide, wide)).T
        column = jnp.concatenate([column] * (points // wide), axis=1)
        gather.append(jnp.where(column == lanes, 1.0, 0.0).astype(BF16))
    ordered = pick(jnp.concatenate(gather, axis=0), rhs[...])
    z = mm_parts((top[...], low[...]), split(ordered))
    solved[...] = z
    projected[...] = mm(basis_t[...], z)


def node_kernel(level, gram, other, precision, *rest):
    coupling = precision[0, level].astype(F32)
    whole = unfold(gram[...] + other[...])
    if len(rest) == 7:
        rest[0][...] = scaled_inverse(coupling + whole, *rest[1:])
        return
    transfer, inverse, mover, gram_out, *work = rest
    mixer = transfer[0, level]
    left = split(mm(mixer, precision[0, level], None, ((0,), (0,))))
    right = split(sum(mm(part.astype(BF16), mixer, None) for part in parts(whole)))
    m = scaled_inverse(coupling + whole, *work)
    n = mm_parts(left, split(m))
    inverse[...] = m
    mover[...] = n
    gram_out[...] = fold(mm_parts(split(n), right))


def lift_kernel(first, last, *refs):
    refs = list(refs)
    projected, other, inverse, mover = (refs.pop(0)[...] for _ in range(4))
    s = projected + other
    alpha = mm(inverse, s)
    outs = refs[-5:] if first and not last else refs[-3:]
    outs[0][...] = mm(mover, s)
    if first:
        order, solved, carried = (refs.pop(0)[...] for _ in range(3))
        points = solved.shape[0]
        rows = lax.broadcasted_iota(jnp.int32, (points, points), 0)
        scatter = jnp.where(order == rows, 1.0, 0.0).astype(BF16)
        solved, carried = pick(scatter, solved), pick(scatter, carried)
        total, mixing = alpha, mover.T
    else:
        total, mixing, solved, carried = (refs.pop(0)[...] for _ in range(4))
        total = total + mm(mixing, alpha)
        mixing = mm(mixing, mover, HIGH, ((1,), (1,)))
    if last:
        total = solved - mm(carried, total)
        mixing = mm(carried, mixing)
    outs[1][...] = total
    outs[2][...] = mixing
    if first and not last:
        outs[3][...] = solved
        outs[4][...] = carried


def root_kernel(pieces, projected, other, inverse, solved, carried, out_far, out, sems):
    alpha = split(mm_parts(split(inverse[...]), split(projected[...] + other[...])))
    rows = out.shape[0] // pieces
    copies = []
    for i in range(pieces):
        part = pl.ds(i * rows, rows)
        out[part] = solved[part] - mm_parts(split(carried[part]), alpha)
        copies.append(pltpu.make_async_copy(out.at[part], out_far.at[part], sems.at[i]))
        copies[-1].start()
    for copy in copies:
        copy.wait()


def call(kernel, outs, *args, scratch=(), work=0, place=VMEM, result=VMEM):
    if place is FAR:
        args = [pltpu.with_memory_space_constraint(arg, pltpu.HBM) for arg in args]
    return pl.pallas_call(
        kernel,
        out_shape=[jax.ShapeDtypeStruct(getattr(out, "shape", out), getattr(out, "dtype", F32)) for out in outs],
        in_specs=[place] * len(args),
        out_specs=[result] * len(outs),
        scratch_shapes=scratch,
        cost_estimate=pl.CostEstimate(flops=work, bytes_accessed=0, transcendentals=0),
        compiler_params=PARAMS,
    )(*args)


def from_partner(block, axis, apart):
    count = lax.axis_size(axis)
    return lax.ppermute(block, axis, [(i, i ^ 1 << apart) for i in range(count)])


def body(rhs, order, inverse, basis, transfer, precision):
    points, columns = rhs.shape
    rank = basis.shape[1]
    square, tall, block = (rank, rank), (points, rank), (rank, columns)
    folded = (rank // 2 + SUB, rank)
    levels = lax.axis_size("leaf").bit_length() - 1
    pieces = 8
    half = jax.ShapeDtypeStruct(inverse.shape, BF16)
    top, low, basis_t, order, carried, gram = call(
        basis_kernel, [half, half, (rank, points), order, tall, folded],
        inverse, basis, order, place=FAR, work=GIGA,
        scratch=[pltpu.VMEM(inverse.shape, F32), pltpu.VMEM(tall, F32), pltpu.SemaphoreType.DMA((3,))]
    )
    other_gram = from_partner(gram, "leaf", 0)
    solved, projected = call(leaf_kernel, [rhs, block], order, rhs, top, low, basis_t, work=2 * GIGA)
    if levels == 1:
        raise NotImplementedError("one level")
    state = [order, solved, carried]
    for k in range(levels - 1):
        other = from_partner(projected, "leaf", k)
        m, n, gram = call(
            functools.partial(node_kernel, k), [square, square, folded], gram, other_gram, precision, transfer,
            scratch=invert_scratch(rank), work=6 * GIGA
        )
        other_gram = from_partner(gram, "leaf", k + 1)
        first, last = k == 0, k == levels - 2
        outs = [rhs, tall] if last else [block, square, rhs, tall] if first else [block, square]
        projected, *new = call(
            functools.partial(lift_kernel, first, last), [block] + outs, projected, other, m, n, *state, work=GIGA
        )
        state = new + state[len(new):]
    solved, carried = state[:2]
    k = levels - 1
    other = from_partner(projected, "leaf", k)
    (m,) = call(functools.partial(node_kernel, k), [square], gram, other_gram, precision, scratch=invert_scratch(rank), work=6 * GIGA)
    (out,) = call(
        functools.partial(root_kernel, pieces), [rhs], projected, other, m, solved, carried, work=GIGA, result=FAR,
        scratch=[pltpu.VMEM(rhs.shape, F32), pltpu.SemaphoreType.DMA((pieces,))]
    )
    return out


def solution(mesh):
    placed = (
        P("leaf", "rhs"),
        P("leaf", None),
        P("leaf", None),
        P("leaf", None),
        P("leaf", None, None, None),
        P("leaf", None, None, None),
    )
    return jax.shard_map(
        body, mesh=mesh, in_specs=placed, out_specs=P("leaf", "rhs"), check_vma=False
    )
```
